32 devices in a mesh: img: 32 (over z, y, x, core).
Axes of the slice: x: 2, y: 2, z: 4, core: 2. Of those that a mesh axis runs over, the one named last changes fastest.
Arguments:
- token_embeddings: bfloat16 [128, 576, 384], P('img')
- upstream_sensitivity: bfloat16 [128, 576, 384], P('img')
- tile_lattice_edges: int32 [128], P('img'), may hold values from 14 to 24, as said below
- opening_standardizer_factor: float32 [384], replicated, may hold values from 0.5 to 1.5
- opening_standardizer_offset: float32 [384], replicated, may hold values from -4 to 4
- projection_triple_matrix: bfloat16 [384, 1152], replicated, may hold values from -0.3125 to 0.3125
- projection_triple_offset: float32 [1152], replicated, may hold values from -4 to 4
- sharpness_factor: float32 [8], replicated, may hold values from 4 to 16
- mixing_exit_matrix: bfloat16 [384, 384], replicated, may hold values from -0.875 to 0.875
- mixing_exit_offset: float32 [384], replicated, may hold values from -4 to 4
- mixing_branch_factor: float32 [384], replicated, may hold values from 0.5 to 1.5
- middle_standardizer_factor: float32 [384], replicated, may hold values from 0.5 to 1.5
- middle_standardizer_offset: float32 [384], replicated, may hold values from -4 to 4
- early_perchannel_stencil: float32 [3, 3, 384], replicated, may hold values from -2 to 2
- early_perchannel_offset: float32 [384], replicated, may hold values from -4 to 4
- cohort_normalizer_factor: float32 [384], replicated, may hold values from 0.5 to 1.5
- cohort_normalizer_offset: float32 [384], replicated, may hold values from -4 to 4
- later_perchannel_stencil: float32 [3, 3, 384], replicated, may hold values from -2 to 2
- later_perchannel_offset: float32 [384], replicated, may hold values from -4 to 4
- neighbour_branch_factor: float32 [384], replicated, may hold values from 0.5 to 1.5
- closing_standardizer_factor: float32 [384], replicated, may hold values from 0.5 to 1.5
- closing_standardizer_offset: float32 [384], replicated, may hold values from -4 to 4
- perceptron_entry_matrix: bfloat16 [384, 1536], replicated, may hold values from -0.3125 to 0.3125
- perceptron_entry_offset: float32 [1536], replicated, may hold values from -4 to 4
- perceptron_exit_matrix: bfloat16 [1536, 384], replicated, may hold values from -0.15625 to 0.15625
- perceptron_exit_offset: float32 [384], replicated, may hold values from -4 to 4
- perceptron_branch_factor: float32 [384], replicated, may hold values from 0.5 to 1.5
Outputs:
- layer_out: bfloat16 [128, 576, 384], P('img')
- grad_input: bfloat16 [128, 576, 384], P('img')
- grad_norm1_gain: float32 [384], replicated
- grad_norm1_shift: float32 [384], replicated
- grad_qkv_weight: float32 [384, 1152], replicated
- grad_qkv_bias: float32 [1152], replicated
- sharpness_sensitivity: float32 [8], replicated
- grad_proj_weight: float32 [384, 384], replicated
- grad_proj_bias: float32 [384], replicated
- grad_scale_attn: float32 [384], replicated
- grad_norm2_gain: float32 [384], replicated
- grad_norm2_shift: float32 [384], replicated
- grad_conv1_kernel: float32 [3, 3, 384], replicated
- grad_conv1_bias: float32 [384], replicated
- grad_batch_gain: float32 [384], replicated
- grad_batch_shift: float32 [384], replicated
- grad_conv2_kernel: float32 [3, 3, 384], replicated
- grad_conv2_bias: float32 [384], replicated
- grad_scale_local: float32 [384], replicated
- grad_norm3_gain: float32 [384], replicated
- grad_norm3_shift: float32 [384], replicated
- grad_fc1_weight: float32 [384, 1536], replicated
- grad_fc1_bias: float32 [1536], replicated
- grad_fc2_weight: float32 [1536, 384], replicated
- grad_fc2_bias: float32 [384], replicated
- grad_scale_mlp: float32 [384], replicated
The draws below stay inside these ranges and needn't reach their ends.
Inputs may be any that keep to these rules, and one draw needn't show every extreme that they name: `tile_lattice_edges`: each image's grid side is 24, 18 or (168) // 12; every draw has an image of each of the two extreme sides.
All inputs are finite; a program needn't handle non-finite values.
Results may differ from the reference program's by a relative error of at most 0.012.
Values sent between devices are 32-bit elements; how exact they have to be, the bound alone decides.
A program may use at most 192 MiB of HBM per device.

```python
import math
import jax
import jax.numpy as jnp
from jax import lax

D = 384
CHANNEL_GROUPS = 8
FF = 1536
HD = 48
GRID = 24
IMG_DEV = 4
TOKS = 576
IMGS = 128
N_IMG = 32


def image_field(key, noise, offset_scale):
    shift_key = jax.random.fold_in(key, 2)
    rise = 1.0 + 2.0 * jnp.arange(IMGS, dtype=jnp.float32) / max(IMGS - 1, 1)
    offsets = jax.random.normal(shift_key, (IMGS, 1, D), dtype=jnp.float32) * offset_scale * rise[:, None, None]
    return noise + offsets


def draw_token_embeddings(key, part):
    key = jax.random.fold_in(key, 11)
    noise_key = jax.random.fold_in(key, 1)
    noise = jnp.clip(jax.random.normal(noise_key, (IMGS, TOKS, D), dtype=jnp.float32), -5.0, 5.0)
    return image_field(key, noise, 0.3).astype(jnp.bfloat16)


def draw_upstream_sensitivity(key, part):
    key = jax.random.fold_in(key, 13)
    noise_key = jax.random.fold_in(key, 1)
    noise = jnp.clip(jax.random.normal(noise_key, (IMGS, TOKS, D), dtype=jnp.float32), -5.0, 5.0)
    return image_field(key, noise, 0.3).astype(jnp.bfloat16)


def draw_tile_lattice_edges(key, part):
    key = jax.random.fold_in(key, 17)
    pick_key, large_key, small_key = jax.random.split(key, 3)
    picks = jax.random.randint(pick_key, (IMGS,), 0, 1236)
    middle = 3 * GRID // 4
    least = 7 * GRID // 12
    sides = jnp.where(picks < 512, GRID, jnp.where(picks < 896, middle, least))
    large_slot = jax.random.randint(large_key, (), 0, IMGS)
    small_slot = (large_slot + 1 + jax.random.randint(small_key, (), 0, IMGS - 1)) % IMGS
    sides = sides.at[large_slot].set(GRID).at[small_slot].set(least)
    return sides.astype(jnp.int32)


def gaussian(own_key, extent, scale, bound, kind=jnp.bfloat16):
    result = scale * jax.random.normal(own_key, extent, jnp.float32)
    return jnp.clip(result, min=-bound, max=bound).astype(kind)


def setup_inputs(seed: int = 0) -> dict:
    key_of = jax.random.split(jax.random.key(seed), 28)
    return {
        "token_embeddings": draw_token_embeddings(jax.random.fold_in(key_of[27], 71), 0),
        "upstream_sensitivity": draw_upstream_sensitivity(jax.random.fold_in(key_of[27], 71), 0),
        "tile_lattice_edges": draw_tile_lattice_edges(jax.random.fold_in(key_of[27], 71), 0),
        "opening_standardizer_factor": jnp.clip(jax.random.uniform(key_of[3], (D,), jnp.float32, 0.5, 1.5), 0.5, 1.5),
        "opening_standardizer_offset": gaussian(key_of[4], (D,), 0.3, 4.0, jnp.float32),
        "projection_triple_matrix": gaussian(key_of[5], (D, 3 * D), D ** -0.5, 0.3125),
        "projection_triple_offset": gaussian(key_of[6], (3 * D,), 0.3, 4.0, jnp.float32),
        "sharpness_factor": jnp.clip(jnp.exp(jax.random.uniform(key_of[7], (CHANNEL_GROUPS,), jnp.float32, math.log(4.0), math.log(16.0))), 4.0, 16.0),
        "mixing_exit_matrix": gaussian(key_of[8], (D, D), (D // 8) ** -0.5, 0.875),
        "mixing_exit_offset": gaussian(key_of[9], (D,), 0.3, 4.0, jnp.float32),
        "mixing_branch_factor": jnp.clip(jax.random.uniform(key_of[10], (D,), jnp.float32, 0.5, 1.5), 0.5, 1.5),
        "middle_standardizer_factor": jnp.clip(jax.random.uniform(key_of[11], (D,), jnp.float32, 0.5, 1.5), 0.5, 1.5),
        "middle_standardizer_offset": gaussian(key_of[12], (D,), 0.3, 4.0, jnp.float32),
        "early_perchannel_stencil": gaussian(key_of[13], (3, 3, D), 9 ** -0.5, 2.0, jnp.float32),
        "early_perchannel_offset": gaussian(key_of[14], (D,), 0.3, 4.0, jnp.float32),
        "cohort_normalizer_factor": jnp.clip(jax.random.uniform(key_of[15], (D,), jnp.float32, 0.5, 1.5), 0.5, 1.5),
        "cohort_normalizer_offset": gaussian(key_of[16], (D,), 0.3, 4.0, jnp.float32),
        "later_perchannel_stencil": gaussian(key_of[17], (3, 3, D), 9 ** -0.5, 2.0, jnp.float32),
        "later_perchannel_offset": gaussian(key_of[18], (D,), 0.3, 4.0, jnp.float32),
        "neighbour_branch_factor": jnp.clip(jax.random.uniform(key_of[19], (D,), jnp.float32, 0.5, 1.5), 0.5, 1.5),
        "closing_standardizer_factor": jnp.clip(jax.random.uniform(key_of[20], (D,), jnp.float32, 0.5, 1.5), 0.5, 1.5),
        "closing_standardizer_offset": gaussian(key_of[21], (D,), 0.3, 4.0, jnp.float32),
        "perceptron_entry_matrix": gaussian(key_of[22], (D, FF), D ** -0.5, 0.3125),
        "perceptron_entry_offset": gaussian(key_of[23], (FF,), 0.3, 4.0, jnp.float32),
        "perceptron_exit_matrix": gaussian(key_of[24], (FF, D), FF ** -0.5, 0.15625),
        "perceptron_exit_offset": gaussian(key_of[25], (D,), 0.3, 4.0, jnp.float32),
        "perceptron_branch_factor": jnp.clip(jax.random.uniform(key_of[26], (D,), jnp.float32, 0.5, 1.5), 0.5, 1.5),
    }


HIGH = lax.Precision.HIGHEST

@jax.custom_vjp
def low(v):
    return lax.optimization_barrier(v.astype(jnp.bfloat16)).astype(jnp.float32)

@jax.custom_vjp
def low_back(v):
    return v

def low_keep(v):
    return (low(v), None)

def low_pass(kept, grad):
    return (grad,)

def back_keep(v):
    return (v, None)

def back_low(kept, grad):
    return (low(grad),)
low.defvjp(low_keep, low_pass)
low_back.defvjp(back_keep, back_low)

def valid_tokens(tile_lattice_edges):
    places = jnp.arange(GRID * GRID, dtype=jnp.int32)
    row_index = places // GRID
    col_index = places % GRID
    limits = tile_lattice_edges[:, None]
    inside = (row_index[None, :] < limits) & (col_index[None, :] < limits)
    return inside.astype(jnp.float32)[:, :, None]

def layer_norm(value, gain, shift):
    centre = value - lax.optimization_barrier(jnp.mean(value, axis=-1, keepdims=True))
    spread = lax.optimization_barrier(jnp.mean(centre * centre, axis=-1, keepdims=True))
    return centre * lax.rsqrt(spread + 1e-06) * gain + shift

def depthwise(value, kernel):
    images = value.shape[0]
    plane = value.reshape(images, GRID, GRID, D)
    padded = jnp.pad(plane, ((0, 0), (1, 1), (1, 1), (0, 0)))
    total = jnp.zeros_like(plane)
    for row_step in range(3):
        for col_step in range(3):
            total = total + kernel[row_step, col_step] * padded[:, row_step:row_step + GRID, col_step:col_step + GRID, :]
    return total.reshape(images, GRID * GRID, D)

def unit_columns(value):
    return value * lax.rsqrt(lax.optimization_barrier(jnp.sum(value * value, axis=1, keepdims=True)) + 1e-06)

def reference(token_embeddings, upstream_sensitivity, tile_lattice_edges, opening_standardizer_factor, opening_standardizer_offset, projection_triple_matrix, projection_triple_offset, sharpness_factor, mixing_exit_matrix, mixing_exit_offset, mixing_branch_factor, middle_standardizer_factor, middle_standardizer_offset, early_perchannel_stencil, early_perchannel_offset, cohort_normalizer_factor, cohort_normalizer_offset, later_perchannel_stencil, later_perchannel_offset, neighbour_branch_factor, closing_standardizer_factor, closing_standardizer_offset, perceptron_entry_matrix, perceptron_entry_offset, perceptron_exit_matrix, perceptron_exit_offset, perceptron_branch_factor):
    inside = valid_tokens(tile_lattice_edges)
    total_count = jnp.sum(inside)
    block_rows = IMG_DEV * TOKS
    split_shape = (IMG_DEV, TOKS, CHANNEL_GROUPS, HD)
    block_shape = (N_IMG, IMG_DEV, TOKS, D)
    inside_blocks = inside.reshape(N_IMG, IMG_DEV, TOKS, 1)

    def apply_block(tokens_single_precise, opening_standardizer_factor, opening_standardizer_offset, projection_triple_matrix, projection_triple_offset, sharpness_factor, mixing_exit_matrix, mixing_exit_offset, mixing_branch_factor, middle_standardizer_factor, middle_standardizer_offset, early_perchannel_stencil, early_perchannel_offset, cohort_normalizer_factor, cohort_normalizer_offset, later_perchannel_stencil, later_perchannel_offset, neighbour_branch_factor, closing_standardizer_factor, closing_standardizer_offset, perceptron_entry_matrix, perceptron_entry_offset, perceptron_exit_matrix, perceptron_exit_offset, perceptron_branch_factor):

        def front(pair):
            tokens_here, inside_here = pair
            normed1 = low(inside_here * layer_norm(tokens_here, opening_standardizer_factor, opening_standardizer_offset))
            qkv_rows = inside_here * (low_back(jnp.dot(normed1.reshape(block_rows, D), projection_triple_matrix, precision=HIGH)).reshape(IMG_DEV, TOKS, 3 * D) + projection_triple_offset)
            query_part = qkv_rows[:, :, :D].reshape(split_shape)
            key_part = qkv_rows[:, :, D:2 * D].reshape(split_shape)
            value_low = low(qkv_rows[:, :, 2 * D:].reshape(split_shape))
            query_unit = low(unit_columns(query_part))
            key_unit = low(unit_columns(key_part))
            channel_affinity_logits = low_back(jnp.einsum('ithb,ithc->ihbc', query_unit, key_unit, precision=HIGH))
            channel_affinity_softmaxed = jax.nn.softmax(sharpness_factor[None, :, None, None] * channel_affinity_logits, axis=-1)
            attn_low = low(channel_affinity_softmaxed)
            mixed = low_back(low(jnp.einsum('ihbc,ithc->ithb', attn_low, value_low, precision=HIGH))).reshape(block_rows, D)
            attn_branch = inside_here * (low_back(jnp.dot(mixed, mixing_exit_matrix, precision=HIGH)).reshape(IMG_DEV, TOKS, D) + mixing_exit_offset)
            resid1 = tokens_here + mixing_branch_factor * attn_branch
            normed2 = inside_here * layer_norm(resid1, middle_standardizer_factor, middle_standardizer_offset)
            conv_pre = depthwise(normed2, early_perchannel_stencil) + early_perchannel_offset
            activated = inside_here * jax.nn.gelu(conv_pre, approximate=False)
            return (resid1, activated)
        resid1_all, activated_all = lax.map(jax.checkpoint(front), (tokens_single_precise.reshape(block_shape), inside_blocks))
        batch_mean = lax.optimization_barrier(jnp.sum(activated_all, axis=(0, 1, 2))) / total_count
        deviation = inside_blocks * (activated_all - batch_mean)
        variance = lax.optimization_barrier(jnp.sum(deviation * deviation, axis=(0, 1, 2))) / total_count
        inv_spread = lax.rsqrt(variance + 1e-05)

        def rear(triple):
            resid1_here, activated_here, inside_here = triple
            centred = (activated_here - batch_mean) * inv_spread
            batch_normed = inside_here * (centred * cohort_normalizer_factor + cohort_normalizer_offset)
            local_branch = inside_here * (depthwise(batch_normed, later_perchannel_stencil) + later_perchannel_offset)
            resid2 = resid1_here + neighbour_branch_factor * local_branch
            normed3 = low(inside_here * layer_norm(resid2, closing_standardizer_factor, closing_standardizer_offset)).reshape(block_rows, D)
            hidden_pre = low_back(jnp.dot(normed3, perceptron_entry_matrix, precision=HIGH)) + perceptron_entry_offset
            hidden_low = low(jax.nn.gelu(hidden_pre, approximate=False))
            mlp_branch = inside_here * (low_back(jnp.dot(hidden_low, perceptron_exit_matrix, precision=HIGH)).reshape(IMG_DEV, TOKS, D) + perceptron_exit_offset)
            return inside_here * (resid2 + perceptron_branch_factor * mlp_branch)
        outcome = lax.map(jax.checkpoint(rear), (resid1_all, activated_all, inside_blocks))
        return outcome.reshape(IMGS, TOKS, D)
    broadened_entries = jnp.float32
    block_outcome, reverse_sweep = jax.vjp(apply_block, token_embeddings.astype(broadened_entries), opening_standardizer_factor, opening_standardizer_offset, projection_triple_matrix.astype(broadened_entries), projection_triple_offset, sharpness_factor, mixing_exit_matrix.astype(broadened_entries), mixing_exit_offset, mixing_branch_factor, middle_standardizer_factor, middle_standardizer_offset, early_perchannel_stencil, early_perchannel_offset, cohort_normalizer_factor, cohort_normalizer_offset, later_perchannel_stencil, later_perchannel_offset, neighbour_branch_factor, closing_standardizer_factor, closing_standardizer_offset, perceptron_entry_matrix.astype(broadened_entries), perceptron_entry_offset, perceptron_exit_matrix.astype(broadened_entries), perceptron_exit_offset, perceptron_branch_factor)
    grads = reverse_sweep(upstream_sensitivity.astype(broadened_entries))
    return (block_outcome.astype(jnp.bfloat16), grads[0].astype(jnp.bfloat16), grads[1], grads[2], grads[3], grads[4], grads[5], grads[6], grads[7], grads[8], grads[9], grads[10], grads[11], grads[12], grads[13], grads[14], grads[15], grads[16], grads[17], grads[18], grads[19], grads[20], grads[21], grads[22], grads[23], grads[24])
```

```python
import math

import jax
import jax.numpy as jnp
from jax import lax
from jax.experimental import pallas as pl
from jax.experimental.pallas import tpu as pltpu
from jax.sharding import PartitionSpec as P

EPS_NORM = 1e-06
EPS_BATCH = 1e-05
EPS_UNIT = 1e-06
F32 = jnp.float32
BF16 = jnp.bfloat16
MESH = pl.DeviceIdType.MESH
G = 24
T = G * G
D = 384
FF = 1536
HEADS = 8
HD = 48
L = 128
PITCH = 32
PLANE = (G + 4) * PITCH
RC = 96
ROOT_HALF = 0.7071067811865476
ROOT_TWO_PI = 0.3989422804014327
NT = (((1,), (1,)), ((), ()))
TN = (((0,), (0,)), ((), ()))


def dot(a, b, dims=(((1,), (0,)), ((), ()))):
    return lax.dot_general(a, b, dims, preferred_element_type=F32)


def rows(start, size):
    return pl.ds(pl.multiple_of(start, 8), size)


def wide(v, times=3):
    return jnp.concatenate([v] * times, axis=1)


def fold8(v):
    return jnp.sum(v.reshape(v.shape[0] // 8, 8, v.shape[1]), axis=0)


def total(v):
    return jnp.sum(v, axis=0, keepdims=True)


def gelu_pair(u):
    phi = 0.5 + 0.5 * lax.erf(u * ROOT_HALF)
    bell = jnp.exp((u * u) * -0.5)
    return u * phi, phi + u * (bell * ROOT_TWO_PI)


def column_of(row):
    return jnp.broadcast_to(row, (L, D)).T


def write_mask(mask, edge):
    row_index = lax.broadcasted_iota(jnp.int32, (G, G, L), 0)
    col_index = lax.broadcasted_iota(jnp.int32, (G, G, L), 1)
    keep = (row_index < edge) & (col_index < edge)
    mask[...] = keep.astype(F32).reshape(T, L)


def write_sharp(sharp_mask, sharp):
    lane = lax.broadcasted_iota(jnp.int32, (HD, D), 1)
    for h in range(HEADS):
        own = (lane >= h * HD) & (lane < (h + 1) * HD)
        sharp_mask[h * HD : (h + 1) * HD, :] = jnp.where(own, sharp[h], 0.0)


def to_plane(plane, r, value):
    for g in range(RC // G):
        for c in range(3):
            plane[c, rows((r * (RC // G) + g + 2) * PITCH, G), :] = value[
                g * G : (g + 1) * G, c * L : (c + 1) * L
            ]


def row_count(n):
    return n // RC


def phase_a(i, edge, x, g1, b1, wqkv, bqkv, wm, bm, fm, g2, b2, st1, cb1,
            n1, ql, kl, vl, mixed, prob, score, sqk, m1, r1, resid1, vh2, r2, act, slope, stat,
            mask, sharp_mask, plane, plow):
    write_mask(mask, edge)

    def qkv_body(r, carry):
        sl = rows(r * RC, RC)
        xs = x[i, sl, :].astype(F32)
        mean = jnp.mean(xs, axis=1, keepdims=True)
        centre = xs - mean
        spread = lax.rsqrt(jnp.mean(centre * centre, axis=1, keepdims=True) + EPS_NORM)
        mk = wide(mask[sl, :])
        normed = ((centre * spread * g1[...] + b1[...]) * mk).astype(BF16)
        n1[i, sl, :] = normed
        m1[i, sl, :] = jnp.broadcast_to(mean, (RC, L))
        r1[i, sl, :] = jnp.broadcast_to(spread, (RC, L))
        sums = list(carry)
        for p, out in enumerate((ql, kl, vl)):
            cols = slice(p * D, (p + 1) * D)
            part = (dot(normed, wqkv[:, cols]) + bqkv[:, cols]) * mk
            if p < 2:
                sums[p] = sums[p] + fold8(part * part)
            out[i, sl, :] = part.astype(BF16)
        return tuple(sums)

    zero = jnp.zeros((8, D), F32)
    sums = lax.fori_loop(0, T // RC, qkv_body, (zero, zero))
    sq = lax.rsqrt(total(sums[0]) + EPS_UNIT)
    sk = lax.rsqrt(total(sums[1]) + EPS_UNIT)
    sqk[i, 0] = jnp.broadcast_to(sq, (8, D))
    sqk[i, 1] = jnp.broadcast_to(sk, (8, D))
    sqcol = column_of(sq)
    raw = dot(ql[i], kl[i], TN)
    for h in range(HEADS):
        band = slice(h * HD, (h + 1) * HD)
        sc = raw[band] * wide(sqcol[band]) * sk
        sh = sharp_mask[band, :]
        ex = jnp.where(sh > 0.0, jnp.exp(sc * sh), 0.0)
        pr = ex / jnp.sum(ex, axis=1, keepdims=True)
        score[i, band, :] = sc
        prob[i, band, :] = pr
        plow[band, :] = pr.astype(BF16)

    def mix_body(r, _):
        sl = rows(r * RC, RC)
        mk = wide(mask[sl, :])
        mx = dot(vl[i, sl, :], plow[...], NT).astype(BF16)
        mixed[i, sl, :] = mx
        branch = (dot(mx, wm[...]) + bm[...]) * mk
        res = x[i, sl, :].astype(F32) + fm[...] * branch
        resid1[i, sl, :] = res
        mean = jnp.mean(res, axis=1, keepdims=True)
        centre = res - mean
        spread = lax.rsqrt(jnp.mean(centre * centre, axis=1, keepdims=True) + EPS_NORM)
        vhat = centre * spread
        vh2[i, sl, :] = vhat
        r2[i, sl, :] = jnp.broadcast_to(spread, (RC, L))
        to_plane(plane, r, (vhat * g2[...] + b2[...]) * mk)
        return 0

    lax.fori_loop(0, T // RC, mix_body, 0)

    sums = []
    for c in range(3):
        cs = slice(c * L, (c + 1) * L)
        taps = [jnp.broadcast_to(st1[a, b : b + 1, cs], (G, L)) for a in range(3) for b in range(3)]

        def conv_body(r, carry):
            base = r * (4 * PITCH)
            outs = [None] * 4
            for a in range(6):
                for b in range(3):
                    v = plane[c, pl.ds(base + (a + 1) * PITCH - 1 + b, G), :]
                    for o in range(4):
                        if 0 <= a - o < 3:
                            t = v * taps[(a - o) * 3 + b]
                            outs[o] = t if outs[o] is None else outs[o] + t
            for o in range(4):
                sl = rows(r * (4 * G) + o * G, G)
                value, diff = gelu_pair(outs[o] + cb1[:, cs])
                value = value * mask[sl, :]
                act[i, sl, cs] = value
                slope[i, sl, cs] = diff.astype(slope.dtype)
                carry = carry + fold8(value)
            return carry

        sums.append(total(lax.fori_loop(0, G // 4, conv_body, jnp.zeros((8, L), F32))))
    count = (edge * edge).astype(F32)
    summed = jnp.concatenate(sums, axis=1)
    mean = summed / count

    def spread_body(r, carry):
        sl = rows(r * RC, RC)
        dev = (act[i, sl, :] - mean) * wide(mask[sl, :])
        return carry + fold8(dev * dev)

    square = total(lax.fori_loop(0, T // RC, spread_body, zero))
    stat[i, 0:1, :] = summed
    stat[i, 1:2, :] = square
    stat[i, 2:3, :] = jnp.full((1, D), count, F32)


def merge_stats(parts):
    summed = sum(p[0] for p in parts)
    count = sum(p[2] for p in parts)
    mean = summed / count
    square = sum(p[1] + p[2] * (p[0] / p[2] - mean) * (p[0] / p[2] - mean) for p in parts)
    return summed, square, count


def phase_b(i, edge, sens, resid1, act, bstat, bg, bo, st2, cb2, fl, g3, b3, w1, bb1, w2, bb2, fp,
            lout, rg, bng, dw1, dw2, sm_b, smf,
            mask, plane, plane2, res2, vh3, r3, n3, f2, hl, e1):
    write_mask(mask, edge)
    mean, inv, _ = bstat
    scale = inv * bg[...]
    shift = bo[...] - mean * scale

    def bn_body(r, _):
        sl = rows(r * RC, RC)
        to_plane(plane, r, (act[i, sl, :] * scale + shift) * wide(mask[sl, :]))
        return 0

    lax.fori_loop(0, T // RC, bn_body, 0)

    for c in range(3):
        cs = slice(c * L, (c + 1) * L)
        taps = [jnp.broadcast_to(st2[a, b : b + 1, cs], (G, L)) for a in range(3) for b in range(3)]

        def conv_body(r, _):
            base = r * (4 * PITCH)
            outs = [None] * 4
            for a in range(6):
                for b in range(3):
                    v = plane[c, pl.ds(base + (a + 1) * PITCH - 1 + b, G), :]
                    for o in range(4):
                        if 0 <= a - o < 3:
                            t = v * taps[(a - o) * 3 + b]
                            outs[o] = t if outs[o] is None else outs[o] + t
            for o in range(4):
                sl = rows(r * (4 * G) + o * G, G)
                local = (outs[o] + cb2[:, cs]) * mask[sl, :]
                res2[sl, cs] = resid1[i, sl, cs] + fl[:, cs] * local
            return 0

        lax.fori_loop(0, G // 4, conv_body, 0)

    def mlp_body(r, carry):
        gain_sum, shift_sum, bias_sum, local_sum, hidden_sum = carry
        sl = rows(r * RC, RC)
        mk = wide(mask[sl, :])
        res = res2[sl, :]
        mean = jnp.mean(res, axis=1, keepdims=True)
        centre = res - mean
        spread = lax.rsqrt(jnp.mean(centre * centre, axis=1, keepdims=True) + EPS_NORM)
        vhat = centre * spread
        vh3[sl, :] = vhat
        normed = ((vhat * g3[...] + b3[...]) * mk).astype(BF16)
        n3[sl, :] = normed
        og = sens[i, sl, :].astype(F32) * mk
        err = og * fp[...]
        bias_sum = bias_sum + fold8(err)
        low = err.astype(BF16)
        f2[sl, :] = low
        hidden_parts = []
        branch = None
        back = None
        for j in range(FF // 256):
            cols = slice(j * 256, (j + 1) * 256)
            pre = dot(normed, w1[:, cols]) + bb1[:, cols]
            value, diff = gelu_pair(pre)
            value = value.astype(BF16)
            hl[sl, cols] = value
            t = dot(value, w2[cols, :])
            branch = t if branch is None else branch + t
            he = dot(low, w2[cols, :], NT) * diff
            hidden_parts.append(fold8(he))
            he = he.astype(BF16)
            e1[sl, cols] = he
            t = dot(he, w1[:, cols], NT)
            back = t if back is None else back + t
        hidden_sum = hidden_sum + jnp.concatenate(hidden_parts, axis=1)
        lout[i, sl, :] = ((res + fp[...] * (branch + bb2[...])) * mk).astype(BF16)
        err = back * mk
        shift_sum = shift_sum + fold8(err)
        gain_sum = gain_sum + fold8(err * vhat)
        eg = err * g3[...]
        mean1 = jnp.mean(eg, axis=1, keepdims=True)
        mean2 = jnp.mean(eg * vhat, axis=1, keepdims=True)
        grad = og + spread * (eg - mean1 - vhat * mean2)
        rg[i, sl, :] = grad
        local = grad * mk * fl[...]
        local_sum = local_sum + fold8(local)
        to_plane(plane2, r, local)
        return gain_sum, shift_sum, bias_sum, local_sum, hidden_sum

    zero = jnp.zeros((8, D), F32)
    sums = lax.fori_loop(0, T // RC, mlp_body, (zero, zero, zero, zero, jnp.zeros((8, FF), F32)))
    for k in range(4):
        sm_b[k] += sums[k]
    smf[...] += sums[4]
    dw1[...] += dot(n3[...], e1[...], TN)
    dw2[...] += dot(hl[...], f2[...], TN)

    for c in range(3):
        cs = slice(c * L, (c + 1) * L)
        taps = [jnp.broadcast_to(st2[a, b : b + 1, cs], (G, L)) for a in range(3) for b in range(3)]

        def back_body(r, carry):
            kernel, gain, shift_s = list(carry[:9]), carry[9], carry[10]
            base = r * (3 * PITCH)
            outs = [None] * 3
            vs = [plane[c, rows(base + (o + 2) * PITCH, G), :] for o in range(3)]
            for a in range(5):
                for b in range(3):
                    v = plane2[c, pl.ds(base + (a + 1) * PITCH - 1 + b, G), :]
                    for o in range(3):
                        if 0 <= a - o < 3:
                            k = (2 - (a - o)) * 3 + (2 - b)
                            t = v * taps[k]
                            outs[o] = t if outs[o] is None else outs[o] + t
                            kernel[k] = kernel[k] + fold8(v * vs[o])
            for o in range(3):
                sl = rows(r * (3 * G) + o * G, G)
                grad = outs[o] * mask[sl, :]
                bng[i, sl, cs] = grad
                centred = (act[i, sl, cs] - mean[:, cs]) * inv[:, cs]
                gain = gain + fold8(grad * centred)
                shift_s = shift_s + fold8(grad)
            return tuple(kernel) + (gain, shift_s)

        init = tuple(jnp.zeros((8, L), F32) for _ in range(11))
        found = lax.fori_loop(0, G // 3, back_body, init)
        for k in range(11):
            sm_b[4 + k, :, cs] += found[k]


def phase_c(i, edge, x, n1, ql, kl, vl, mixed, prob, score, sqk, m1, r1, rg, vh2, r2, act, slope, bng,
            bstat, bsum, bg, st1, fm, g2, b2, wm, g1, wqkv,
            gin, dwm, dwqkv, sm_c, smq, srow,
            mask, sharp_mask, back, plane2, plow, mgrad, alow, qkvl, rg1):
    write_mask(mask, edge)
    mean, inv, count = bstat
    gain_all, shift_all = bsum
    zero = jnp.zeros((8, D), F32)
    coef = inv * bg[...]
    by_centred = gain_all / count * inv
    const = shift_all / count - mean * by_centred

    def bn_body(r, carry):
        sl = rows(r * RC, RC)
        mk = wide(mask[sl, :])
        grad = (bng[i, sl, :] - const - act[i, sl, :] * by_centred) * coef
        err = grad * mk * slope[i, sl, :].astype(F32)
        to_plane(plane2, r, err)
        return carry + fold8(err)

    sm_c[14] += lax.fori_loop(0, T // RC, bn_body, zero)

    for c in range(3):
        cs = slice(c * L, (c + 1) * L)
        taps = [jnp.broadcast_to(st1[a, b : b + 1, cs], (G, L)) for a in range(3) for b in range(3)]

        def back_body(r, carry):
            kernel = list(carry)
            base = r * (3 * PITCH)
            outs = [None] * 3
            vs = []
            for o in range(3):
                sl = rows(r * (3 * G) + o * G, G)
                vs.append((vh2[i, sl, cs] * g2[:, cs] + b2[:, cs]) * mask[sl, :])
            for a in range(5):
                for b in range(3):
                    v = plane2[c, pl.ds(base + (a + 1) * PITCH - 1 + b, G), :]
                    for o in range(3):
                        if 0 <= a - o < 3:
                            k = (2 - (a - o)) * 3 + (2 - b)
                            t = v * taps[k]
                            outs[o] = t if outs[o] is None else outs[o] + t
                            kernel[k] = kernel[k] + fold8(v * vs[o])
            for o in range(3):
                sl = rows(r * (3 * G) + o * G, G)
                back[sl, cs] = outs[o] * mask[sl, :]
            return tuple(kernel)

        init = tuple(jnp.zeros((8, L), F32) for _ in range(9))
        found = lax.fori_loop(0, G // 3, back_body, init)
        for k in range(9):
            sm_c[5 + k, :, cs] += found[k]

    def norm_body(r, carry):
        gain_sum, shift_sum, bias_sum = carry
        sl = rows(r * RC, RC)
        mk = wide(mask[sl, :])
        err = back[sl, :]
        vhat = vh2[i, sl, :]
        shift_sum = shift_sum + fold8(err)
        gain_sum = gain_sum + fold8(err * vhat)
        eg = err * g2[...]
        mean1 = jnp.mean(eg, axis=1, keepdims=True)
        mean2 = jnp.mean(eg * vhat, axis=1, keepdims=True)
        grad = rg[i, sl, :] + wide(r2[i, sl, :]) * (eg - mean1 - vhat * mean2)
        rg1[sl, :] = grad
        err = grad * mk * fm[...]
        bias_sum = bias_sum + fold8(err)
        low = err.astype(BF16)
        plow[sl, :] = low
        mgrad[sl, :] = dot(low, wm[...], NT).astype(BF16)
        return gain_sum, shift_sum, bias_sum

    sums = lax.fori_loop(0, T // RC, norm_body, (zero, zero, zero))
    for k in range(3):
        sm_c[2 + k] += sums[k]
    dwm[...] += dot(mixed[i], plow[...], TN)

    raw = dot(mgrad[...], vl[i], TN)
    sq, sk = sqk[i, 0, 0:1, :], sqk[i, 1, 0:1, :]
    sqcol = column_of(sq)
    colsum = zero
    rowsums = []
    for h in range(HEADS):
        band = slice(h * HD, (h + 1) * HD)
        pr = prob[i, band, :]
        weighted = raw[band] * pr
        logit = weighted - pr * jnp.sum(weighted, axis=1, keepdims=True)
        sc = score[i, band, :]
        sh = sharp_mask[band, :]
        lg = logit * sh
        cross = lg * sc
        rowsums.append(jnp.sum(cross, axis=1, keepdims=True))
        colsum = colsum + fold8(cross)
        alow[band, :] = (lg * wide(sqcol[band]) * sk).astype(BF16)
        plow[band, :] = pr.astype(BF16)
    rowcol = jnp.concatenate(rowsums, axis=0)
    rowrow = jnp.broadcast_to(rowcol, (D, L)).T[0:1, :]
    srow[...] += rowrow
    cq = sq * sq * rowrow
    ck = sk * sk * total(colsum)

    def qkv_body(r, carry):
        sums = list(carry)
        sl = rows(r * RC, RC)
        qv, kv = ql[i, sl, :], kl[i, sl, :]
        grads = (
            dot(kv, alow[...], NT) - qv.astype(F32) * cq,
            dot(qv, alow[...]) - kv.astype(F32) * ck,
            dot(mgrad[sl, :], plow[0:D, :]),
        )
        for p in range(3):
            sums[p] = sums[p] + fold8(grads[p])
            qkvl[sl, p * D : (p + 1) * D] = grads[p].astype(BF16)
        return tuple(sums)

    sums = lax.fori_loop(0, T // RC, qkv_body, (zero, zero, zero))
    for p in range(3):
        smq[:, p * D : (p + 1) * D] += sums[p]
    dwqkv[...] += dot(n1[i], qkvl[...], TN)

    def in_body(r, carry):
        gain_sum, shift_sum = carry
        sl = rows(r * RC, RC)
        err = dot(qkvl[sl, :], wqkv[...], NT) * wide(mask[sl, :])
        spread = wide(r1[i, sl, :])
        vhat = (x[i, sl, :].astype(F32) - wide(m1[i, sl, :])) * spread
        shift_sum = shift_sum + fold8(err)
        gain_sum = gain_sum + fold8(err * vhat)
        eg = err * g1[...]
        mean1 = jnp.mean(eg, axis=1, keepdims=True)
        mean2 = jnp.mean(eg * vhat, axis=1, keepdims=True)
        gin[i, sl, :] = (rg1[sl, :] + spread * (eg - mean1 - vhat * mean2)).astype(BF16)
        return gain_sum, shift_sum

    sums = lax.fori_loop(0, T // RC, in_body, (zero, zero))
    for k in range(2):
        sm_c[k] += sums[k]


def exchange_kernel(n, payload, gathered, buf, send_sem, recv_sem):
    me = lax.axis_index("img")
    barrier = pltpu.get_barrier_semaphore()

    def other(k):
        return (lax.rem(me + k, n),)

    def signal(k, _):
        pl.semaphore_signal(barrier, inc=1, device_id=other(k), device_id_type=MESH)
        return 0

    lax.fori_loop(1, n, signal, 0)
    pl.semaphore_wait(barrier, n - 1)

    def copy(k):
        return pltpu.make_async_remote_copy(
            src_ref=payload,
            dst_ref=buf.at[me],
            send_sem=send_sem,
            recv_sem=recv_sem,
            device_id=other(k),
            device_id_type=MESH,
        )

    def start(k, _):
        copy(k).start()
        return 0

    lax.fori_loop(1, n, start, 0)
    buf[me] = payload[...]
    most = buf.at[pl.ds(0, n - 1)]
    pltpu.make_async_copy(most, most, send_sem).wait()
    pltpu.make_async_copy(most, most, recv_sem).wait()
    gathered[...] = buf[...]


def exchange(n, payload, ident):
    return pl.pallas_call(
        lambda *refs: exchange_kernel(n, *refs),
        out_shape=jax.ShapeDtypeStruct((n,) + payload.shape, F32),
        in_specs=[pl.BlockSpec(memory_space=pltpu.VMEM)],
        out_specs=pl.BlockSpec(memory_space=pltpu.VMEM),
        scratch_shapes=[
            pltpu.VMEM((n,) + payload.shape, F32),
            pltpu.SemaphoreType.DMA,
            pltpu.SemaphoreType.DMA,
        ],
        compiler_params=pltpu.CompilerParams(collective_id=ident, has_side_effects=True),
    )(payload)


def stack_rows(row):
    return [row[:, c * L : (c + 1) * L] for c in range(3)]


def unstack_rows(ref, k, first):
    return jnp.concatenate([ref[k, first + c : first + c + 1, :] for c in range(3)], axis=1)


def on_device(n, x, sens, edges, g1, b1, wqkv, bqkv, sharp, wm, bm, fm, g2, b2, st1, cb1, bg, bo, st2, cb2, fl, g3, b3,
              w1, bb1, w2, bb2, fp):
    images = x.shape[0]
    sharp_in = sharp
    g1, b1, bqkv, bm, fm, g2, b2, cb1, bg, bo, cb2, fl, g3, b3, bb1, bb2, fp = (
        v.reshape(1, v.shape[0]) for v in (g1, b1, bqkv, bm, fm, g2, b2, cb1, bg, bo, cb2, fl, g3, b3, bb1, bb2, fp)
    )
    S = jax.ShapeDtypeStruct
    vm = pl.BlockSpec(memory_space=pltpu.VMEM)
    sm = pl.BlockSpec(memory_space=pltpu.SMEM)
    cp = pltpu.CompilerParams(vmem_limit_bytes=60 * 1024 * 1024)
    full = lambda t: S((images, T, D), t)
    lanes = S((images, T, L), F32)
    square = S((images, D, D), F32)

    def kernel_a(edges, sharp, x, g1, b1, wqkv, bqkv, wm, bm, fm, g2, b2, st1, cb1,
                 n1, ql, kl, vl, mixed, prob, score, sqk, m1, r1, resid1, vh2, r2, act, slope, payload,
                 mask, sharp_mask, plane, plow, stat):
        write_sharp(sharp_mask, sharp)
        plane[...] = jnp.zeros_like(plane)

        def body(i, _):
            phase_a(i, edges[i], x, g1, b1, wqkv, bqkv, wm, bm, fm, g2, b2, st1, cb1,
                    n1, ql, kl, vl, mixed, prob, score, sqk, m1, r1, resid1, vh2, r2, act, slope, stat,
                    mask, sharp_mask, plane, plow)
            return 0

        lax.fori_loop(0, images, body, 0)
        merged = merge_stats([tuple(stat[i, k : k + 1, :] for k in range(3)) for i in range(images)])
        out = stack_rows(merged[0]) + stack_rows(merged[1]) + [merged[2][:, 0:L], jnp.zeros((1, L), F32)]
        payload[...] = jnp.concatenate(out, axis=0)

    (n1, ql, kl, vl, mixed, prob, score, sqk, m1, r1, resid1, vh2, r2, act, slope, payload) = pl.pallas_call(
        kernel_a,
        in_specs=[sm, sm] + [vm] * 12,
        out_specs=[vm] * 16,
        out_shape=[full(BF16)] * 5 + [square, square, S((images, 2, 8, D), F32), lanes, lanes, full(F32), full(F32), lanes,
                   full(F32), full(BF16), S((8, L), F32)],
        scratch_shapes=[pltpu.VMEM((T, L), F32), pltpu.VMEM((D, D), F32), pltpu.VMEM((3, PLANE, L), F32),
                        pltpu.VMEM((D, D), BF16), pltpu.VMEM((images, 8, D), F32)],
        compiler_params=cp,
    )(edges, sharp, x, g1, b1, wqkv, bqkv, wm, bm, fm, g2, b2, st1, cb1)

    gathered = exchange(n, payload, 0)

    def kernel_b(edges, gathered, sens, resid1, act, bg, bo, st2, cb2, fl, g3, b3, w1, bb1, w2, bb2, fp,
                 lout, rg, bng, dw1, dw2, small, hidden_bias, stats, payload,
                 mask, plane, plane2, res2, vh3, r3, n3, f2, hl, e1, sm_b, smf):
        merged = merge_stats([
            (unstack_rows(gathered, k, 0), unstack_rows(gathered, k, 3), wide(gathered[k, 6:7, :])) for k in range(n)
        ])
        count = merged[2]
        mean = merged[0] / count
        inv = lax.rsqrt(merged[1] / count + EPS_BATCH)
        stats[...] = jnp.concatenate([mean, inv, count, jnp.zeros((5, D), F32)], axis=0)
        plane[...] = jnp.zeros_like(plane)
        plane2[...] = jnp.zeros_like(plane2)
        sm_b[...] = jnp.zeros_like(sm_b)
        smf[...] = jnp.zeros_like(smf)
        dw1[...] = jnp.zeros_like(dw1)
        dw2[...] = jnp.zeros_like(dw2)

        def body(i, _):
            bstat = (stats[0:1, :], stats[1:2, :], stats[2:3, :])
            phase_b(i, edges[i], sens, resid1, act, bstat, bg, bo, st2, cb2, fl, g3, b3, w1, bb1, w2, bb2, fp,
                    lout, rg, bng, dw1, dw2, sm_b, smf,
                    mask, plane, plane2, res2, vh3, r3, n3, f2, hl, e1)
            return 0

        lax.fori_loop(0, images, body, 0)
        sums = [total(sm_b[k]) for k in range(15)]
        small[...] = jnp.concatenate(sums + [jnp.zeros((1, D), F32)], axis=0)
        hidden_bias[...] = total(smf[...])
        payload[...] = jnp.concatenate(stack_rows(sums[13]) + stack_rows(sums[14]) + [jnp.zeros((2, L), F32)], axis=0)

    lout, rg, bng, dw1, dw2, small_b, hidden_bias, stats, payload2 = pl.pallas_call(
        kernel_b,
        in_specs=[sm] + [vm] * 16,
        out_specs=[vm] * 9,
        out_shape=[full(BF16), full(F32), full(F32), S((D, FF), F32), S((FF, D), F32), S((16, D), F32), S((1, FF), F32),
                   S((8, D), F32), S((8, L), F32)],
        scratch_shapes=[pltpu.VMEM((T, L), F32), pltpu.VMEM((3, PLANE, L), F32), pltpu.VMEM((3, PLANE, L), F32),
                        pltpu.VMEM((T, D), F32), pltpu.VMEM((T, D), F32), pltpu.VMEM((T, L), F32),
                        pltpu.VMEM((T, D), BF16), pltpu.VMEM((T, D), BF16), pltpu.VMEM((T, FF), BF16),
                        pltpu.VMEM((T, FF), BF16), pltpu.VMEM((15, 8, D), F32), pltpu.VMEM((8, FF), F32)],
        compiler_params=cp,
    )(edges, gathered, sens, resid1, act, bg, bo, st2, cb2, fl, g3, b3, w1, bb1, w2, bb2, fp)

    gathered2 = exchange(n, payload2, 1)

    def kernel_c(edges, sharp, gathered, stats, x, n1, ql, kl, vl, mixed, prob, score, sqk, m1, r1, rg, vh2, r2, act, slope,
                 bng, bg, st1, fm, g2, b2, wm, g1, wqkv,
                 gin, dwm, dwqkv, small, qkv_bias, srow,
                 mask, sharp_mask, back, plane2, plow, mgrad, alow, qkvl, rg1, sm_c, smq, bsums):
        summed = gathered[0]
        for k in range(1, n):
            summed = summed + gathered[k]
        bsums[0:1, :] = jnp.concatenate([summed[c : c + 1] for c in range(3)], axis=1)
        bsums[1:2, :] = jnp.concatenate([summed[c : c + 1] for c in range(3, 6)], axis=1)
        write_sharp(sharp_mask, sharp)
        plane2[...] = jnp.zeros_like(plane2)
        sm_c[...] = jnp.zeros_like(sm_c)
        smq[...] = jnp.zeros_like(smq)
        srow[...] = jnp.zeros_like(srow)
        dwm[...] = jnp.zeros_like(dwm)
        dwqkv[...] = jnp.zeros_like(dwqkv)

        def body(i, _):
            bstat = (stats[0:1, :], stats[1:2, :], stats[2:3, :])
            bsum = (bsums[0:1, :], bsums[1:2, :])
            phase_c(i, edges[i], x, n1, ql, kl, vl, mixed, prob, score, sqk, m1, r1, rg, vh2, r2, act, slope, bng,
                    bstat, bsum, bg, st1, fm, g2, b2, wm, g1, wqkv,
                    gin, dwm, dwqkv, sm_c, smq, srow,
                    mask, sharp_mask, back, plane2, plow, mgrad, alow, qkvl, rg1)
            return 0

        lax.fori_loop(0, images, body, 0)
        small[...] = jnp.concatenate([total(sm_c[k]) for k in range(15)] + [jnp.zeros((1, D), F32)], axis=0)
        qkv_bias[...] = total(smq[...])

    gin, dwm, dwqkv, small_c, qkv_bias, srow = pl.pallas_call(
        kernel_c,
        in_specs=[sm, sm] + [vm] * 27,
        out_specs=[vm] * 6,
        out_shape=[full(BF16), S((D, D), F32), S((D, 3 * D), F32), S((16, D), F32), S((1, 3 * D), F32), S((1, D), F32)],
        scratch_shapes=[pltpu.VMEM((T, L), F32), pltpu.VMEM((D, D), F32), pltpu.VMEM((T, D), F32),
                        pltpu.VMEM((3, PLANE, L), F32), pltpu.VMEM((T, D), BF16), pltpu.VMEM((T, D), BF16),
                        pltpu.VMEM((D, D), BF16), pltpu.VMEM((T, 3 * D), BF16), pltpu.VMEM((T, D), F32),
                        pltpu.VMEM((15, 8, D), F32), pltpu.VMEM((8, 3 * D), F32), pltpu.VMEM((8, D), F32)],
        compiler_params=cp,
    )(edges, sharp, gathered2, stats, x, n1, ql, kl, vl, mixed, prob, score, sqk, m1, r1, rg, vh2, r2, act, slope, bng,
      bg, st1, fm, g2, b2, wm, g1, wqkv)

    small_b, small_c, hidden_bias, qkv_bias, srow, dwm, dwqkv, dw1, dw2 = lax.psum(
        (small_b, small_c, hidden_bias, qkv_bias, srow, dwm, dwqkv, dw1, dw2), "img"
    )
    proj_bias = small_c[4]
    scale_attn = (jnp.sum(dwm * wm.astype(F32), axis=0) + bm[0] * proj_bias) / fm[0]
    conv2_kernel = small_b[4:13].reshape(3, 3, D)
    conv2_bias = small_b[3]
    scale_local = (jnp.sum(conv2_kernel * st2, axis=(0, 1)) + cb2[0] * conv2_bias) / fl[0]
    fc2_bias = small_b[2]
    scale_mlp = (jnp.sum(dw2 * w2.astype(F32), axis=0) + bb2[0] * fc2_bias) / fp[0]
    sharp_grad = jnp.sum(srow.reshape(HEADS, HD), axis=1) / sharp_in
    return (lout, gin, small_c[0], small_c[1], dwqkv, qkv_bias[0], sharp_grad, dwm, proj_bias, scale_attn,
            small_c[2], small_c[3], small_c[5:14].reshape(3, 3, D), small_c[14], small_b[13], small_b[14],
            conv2_kernel, conv2_bias, scale_local, small_b[0], small_b[1], dw1, hidden_bias[0], dw2, fc2_bias, scale_mlp)


def solution(mesh):
    n = mesh.shape["img"]
    split = P("img", None, None)
    return jax.shard_map(
        lambda *args: on_device(n, *args),
        mesh=mesh,
        in_specs=(split, split, P("img")) + (P(),) * 24,
        out_specs=(split, split) + (P(),) * 24,
        check_vma=False,
    )
```

```python
import math

import jax
import jax.numpy as jnp
from jax import lax
from jax.experimental import pallas as pl
from jax.experimental.pallas import tpu as pltpu
from jax.sharding import PartitionSpec as P

EPS_NORM = 1e-06
EPS_BATCH = 1e-05
EPS_UNIT = 1e-06
F32 = jnp.float32
BF16 = jnp.bfloat16
MESH = pl.DeviceIdType.MESH
G = 24
T = G * G
D = 384
FF = 1536
HEADS = 8
HD = 48
L = 128
PITCH = 32
PLANE = (G + 4) * PITCH
RC = T
RM = T
RF = T // 2
ROOT_HALF = 0.7071067811865476
ROOT_TWO_PI = 0.3989422804014327
NT = (((1,), (1,)), ((), ()))
TN = (((0,), (0,)), ((), ()))


def dot(a, b, dims=(((1,), (0,)), ((), ()))):
    return lax.dot_general(a, b, dims, preferred_element_type=F32)


def rows(start, size):
    return pl.ds(pl.multiple_of(start, 8), size)


def wide(v, times=3):
    return jnp.concatenate([v] * times, axis=1)


def fold8(v):
    return jnp.sum(v.reshape(v.shape[0] // 8, 8, v.shape[1]), axis=0)


def total(v):
    return jnp.sum(v, axis=0, keepdims=True)


def zeros(*shape):
    return jnp.zeros(shape, F32)


def lane_mean(v):
    return jnp.mean(v, axis=1, keepdims=True)


def gelu_pair(u):
    phi = 0.5 + 0.5 * lax.erf(u * ROOT_HALF)
    bell = jnp.exp((u * u) * -0.5)
    return u * phi, phi + u * (bell * ROOT_TWO_PI)


def column_of(row):
    return jnp.broadcast_to(row, (L, D)).T


def write_mask(edge, mask):
    row_index = lax.broadcasted_iota(jnp.int32, (G, G, L), 0)
    col_index = lax.broadcasted_iota(jnp.int32, (G, G, L), 1)
    keep = (row_index < edge) & (col_index < edge)
    mask[...] = keep.astype(F32).reshape(T, L)


def write_sharp(sharp_mask, sharp):
    lane = lax.broadcasted_iota(jnp.int32, (HD, D), 1)
    for h in range(HEADS):
        own = (lane >= h * HD) & (lane < (h + 1) * HD)
        sharp_mask[h * HD : (h + 1) * HD, :] = jnp.where(own, sharp[h], 0.0)


def to_plane(plane, r, value):
    count = value.shape[0] // G
    for g in range(count):
        for c in range(3):
            plane[c, rows((r * count + g + 2) * PITCH, G), :] = value[g * G : (g + 1) * G, c * L : (c + 1) * L]


def taps_of(st, cs):
    return [jnp.broadcast_to(st[a, b : b + 1, cs], (G, L)) for a in range(3) for b in range(3)]


def stencil(plane, c, r, taps, count):
    base = r * (count * PITCH)
    outs = [None] * count
    for a in range(count + 2):
        for b in range(3):
            v = plane[c, pl.ds(base + (a + 1) * PITCH - 1 + b, G), :]
            for o in range(count):
                if 0 <= a - o < 3:
                    t = v * taps[(a - o) * 3 + b]
                    outs[o] = t if outs[o] is None else outs[o] + t
    return outs


def stencil_back(plane, c, r, taps, vs, kernel):
    count = len(vs)
    base = r * (count * PITCH)
    outs = [None] * count
    for a in range(count + 2):
        for b in range(3):
            v = plane[c, pl.ds(base + (a + 1) * PITCH - 1 + b, G), :]
            for o in range(count):
                if 0 <= a - o < 3:
                    k = (2 - (a - o)) * 3 + (2 - b)
                    t = v * taps[k]
                    outs[o] = t if outs[o] is None else outs[o] + t
                    kernel[k] = kernel[k] + fold8(v * vs[o])
    return outs


def chunks(body, init, size):
    if size == T:
        return body(0, pl.ds(0, T), init)
    return lax.fori_loop(0, T // size, lambda r, c: body(r, rows(r * size, size), c), init)


def stage_a1(i, x, g1, b1, n1, mask):
    def body(r, sl, carry):
        xs = x[i, sl, :].astype(F32)
        mean = lane_mean(xs)
        centre = xs - mean
        spread = lax.rsqrt(lane_mean(centre * centre) + EPS_NORM)
        n1[i, sl, :] = ((centre * spread * g1[...] + b1[...]) * wide(mask[sl, :])).astype(BF16)
        return carry

    chunks(body, 0, RC)


def stage_a2(i, wqkv, bqkv, n1, qkv, sqk, mask):
    def body(r, sl, carry):
        sums = list(carry)
        mk = wide(mask[sl, :])
        normed = n1[i, sl, :]
        for p in range(3):
            cols = slice(p * D, (p + 1) * D)
            part = (dot(normed, wqkv[:, cols]) + bqkv[:, cols]) * mk
            if p < 2:
                sums[p] = sums[p] + fold8(part * part)
            qkv[i, sl, cols] = part.astype(BF16)
        return tuple(sums)

    sums = chunks(body, (zeros(8, D), zeros(8, D)), RM)
    for p in range(2):
        sqk[i, p] = jnp.broadcast_to(lax.rsqrt(total(sums[p]) + EPS_UNIT), (8, D))


def softmax_band(sc, sh):
    ex = jnp.where(sh > 0.0, jnp.exp(sc * sh), 0.0)
    return ex / jnp.sum(ex, axis=1, keepdims=True)


def stage_a3(i, qkv, sqk, score, sharp_mask, pmat):
    sq, sk = sqk[i, 0, 0:1, :], sqk[i, 1, 0:1, :]
    sqcol = column_of(sq)
    raw = dot(qkv[i, :, :D], qkv[i, :, D : 2 * D], TN)
    for h in range(HEADS):
        band = slice(h * HD, (h + 1) * HD)
        sc = raw[band] * wide(sqcol[band]) * sk
        score[i, band, :] = sc
        pmat[band, :] = softmax_band(sc, sharp_mask[band, :]).astype(BF16)


def stage_a4(i, x, wm, bm, fm, g2, b2, qkv, mixed, resid, vh2, r2, mask, plane, pmat):
    def body(r, sl, carry):
        mk = wide(mask[sl, :])
        mx = dot(qkv[i, sl, 2 * D :], pmat[...], NT).astype(BF16)
        mixed[i, sl, :] = mx
        branch = (dot(mx, wm[...]) + bm[...]) * mk
        res = x[i, sl, :].astype(F32) + fm[...] * branch
        resid[i, sl, :] = res
        mean = lane_mean(res)
        centre = res - mean
        spread = lax.rsqrt(lane_mean(centre * centre) + EPS_NORM)
        vhat = centre * spread
        vh2[i, sl, :] = vhat
        r2[i, sl, :] = jnp.broadcast_to(spread, (RM, L))
        to_plane(plane, r, (vhat * g2[...] + b2[...]) * mk)
        return carry

    chunks(body, 0, RM)


def stage_a5(i, st1, cb1, act, slope, stat, mask, plane):
    for c in range(3):
        cs = slice(c * L, (c + 1) * L)
        taps = taps_of(st1, cs)

        def conv_body(r, carry):
            outs = stencil(plane, c, r, taps, 4)
            diffs = []
            for o in range(4):
                sl = rows((r * 4 + o) * G, G)
                value, diff = gelu_pair(outs[o] + cb1[:, cs])
                value = value * mask[sl, :]
                act[i, sl, cs] = value
                diffs.append(diff)
                carry = carry + fold8(value)
            slope[i, pl.ds(pl.multiple_of(r * (4 * G), 32), 4 * G), cs] = jnp.concatenate(diffs, axis=0).astype(BF16)
            return carry

        stat[i, 0:1, cs] = total(lax.fori_loop(0, G // 4, conv_body, zeros(8, L)))


def stage_a6(i, edge, act, stat, mask):
    count = (edge * edge).astype(F32)
    mean = stat[i, 0:1, :] / count

    def body(r, sl, carry):
        dev = (act[i, sl, :] - mean) * wide(mask[sl, :])
        return carry + fold8(dev * dev)

    stat[i, 1:2, :] = total(chunks(body, zeros(8, D), RC))
    stat[i, 2:3, :] = jnp.full((1, D), count, F32)


def merge_stats(parts):
    summed = sum(p[0] for p in parts)
    count = sum(p[2] for p in parts)
    mean = summed / count
    square = sum(p[1] + p[2] * (p[0] / p[2] - mean) * (p[0] / p[2] - mean) for p in parts)
    return summed, square, count


def stage_b1(i, act, stats, bg, bo, mask, plane):
    mean, inv = stats[0:1, :], stats[1:2, :]
    scale = inv * bg[...]
    shift = bo[...] - mean * scale

    def body(r, sl, carry):
        to_plane(plane, r, (act[i, sl, :] * scale + shift) * wide(mask[sl, :]))
        return carry

    chunks(body, 0, RC)


def stage_b2(i, st2, cb2, fl, resid, mask, plane):
    for c in range(3):
        cs = slice(c * L, (c + 1) * L)
        taps = taps_of(st2, cs)

        def conv_body(r, carry):
            outs = stencil(plane, c, r, taps, 4)
            for o in range(4):
                sl = rows((r * 4 + o) * G, G)
                resid[i, sl, cs] = resid[i, sl, cs] + fl[:, cs] * ((outs[o] + cb2[:, cs]) * mask[sl, :])
            return carry

        lax.fori_loop(0, G // 4, conv_body, 0)


def stage_b3(i, sens, g3, b3, fp, sm_b, mask, resid, vh3, r3, n3, f2):
    def body(r, sl, carry):
        mk = wide(mask[sl, :])
        res = resid[i, sl, :]
        centre = res - lane_mean(res)
        spread = lax.rsqrt(lane_mean(centre * centre) + EPS_NORM)
        vhat = centre * spread
        vh3[i, sl, :] = vhat
        r3[sl, :] = jnp.broadcast_to(spread, (RC, L))
        n3[sl, :] = ((vhat * g3[...] + b3[...]) * mk).astype(BF16)
        err = sens[i, sl, :].astype(F32) * mk * fp[...]
        f2[sl, :] = err.astype(BF16)
        return carry + fold8(err)

    sm_b[2] += chunks(body, zeros(8, D), RC)


def stage_b4(w1, bb1, w2, smf, n3, f2, hl, e1, branch, back):
    def body(r, sl, hidden_sum):
        normed = n3[sl, :]
        low = f2[sl, :]
        parts = []
        for j in range(FF // 256):
            cols = slice(j * 256, (j + 1) * 256)
            value, diff = gelu_pair(dot(normed, w1[:, cols]) + bb1[:, cols])
            hl[sl, cols] = value.astype(BF16)
            err = dot(low, w2[cols, :], NT) * diff
            parts.append(fold8(err))
            e1[sl, cols] = err.astype(BF16)
        branch[sl, :] = dot(hl[sl, :], w2[...])
        back[sl, :] = dot(e1[sl, :], w1[...], NT)
        return hidden_sum + jnp.concatenate(parts, axis=1)

    smf[...] += chunks(body, zeros(8, FF), RF)


def stage_b5(i, sens, bb2, fp, g3, fl, resid, sm_b, mask, vh3, r3, branch, back):
    def body(r, sl, carry):
        gain_sum, shift_sum, local_sum = carry
        mk = wide(mask[sl, :])
        upstream = sens[i, sl, :].astype(F32) * mk
        sens[i, sl, :] = ((resid[i, sl, :] + fp[...] * (branch[sl, :] + bb2[...])) * mk).astype(BF16)
        err = back[sl, :] * mk
        vhat = vh3[i, sl, :]
        shift_sum = shift_sum + fold8(err)
        gain_sum = gain_sum + fold8(err * vhat)
        eg = err * g3[...]
        mean1 = lane_mean(eg)
        mean2 = lane_mean(eg * vhat)
        grad = upstream + wide(r3[sl, :]) * (eg - mean1 - vhat * mean2)
        resid[i, sl, :] = grad
        local_sum = local_sum + fold8(grad * mk)
        return gain_sum, shift_sum, local_sum

    sums = chunks(body, (zeros(8, D),) * 3, RC)
    sm_b[0] += sums[0]
    sm_b[1] += sums[1]
    sm_b[3] += sums[2] * fl[...]


def stage_b6(dw1, n3, e1):
    left = n3[...].T
    for j in range(FF // 512):
        part = dot(left, e1[:, j * 512 : (j + 1) * 512])
        for k in range(4):
            block, col = divmod(j * 512 + k * L, D)
            dw1[block * D : (block + 1) * D, col : col + L] += part[:, k * L : (k + 1) * L]


def stage_b7(dw2, hl, f2):
    dw2[...] += dot(hl[...], f2[...], TN)


def stage_b8(i, act, stats, bg, bo, fl, st2, resid, bng, sm_b, mask, plane, plane2):
    stage_b1(i, act, stats, bg, bo, mask, plane)

    def local_body(r, sl, carry):
        to_plane(plane2, r, resid[i, sl, :] * wide(mask[sl, :]) * fl[...])
        return carry

    chunks(local_body, 0, RC)
    mean, inv = stats[0:1, :], stats[1:2, :]
    for c in range(3):
        cs = slice(c * L, (c + 1) * L)
        taps = taps_of(st2, cs)

        def back_body(r, carry):
            kernel = list(carry)
            vs = [plane[c, rows((r * 4 + o + 2) * PITCH, G), :] for o in range(4)]
            outs = stencil_back(plane2, c, r, taps, vs, kernel)
            for o in range(4):
                sl = rows((r * 4 + o) * G, G)
                bng[i, sl, cs] = outs[o] * mask[sl, :]
            return tuple(kernel)

        found = lax.fori_loop(0, G // 4, back_body, (zeros(8, L),) * 9)
        for k in range(9):
            sm_b[4 + k, :, cs] += found[k]

    def sum_body(r, sl, carry):
        grad = bng[i, sl, :]
        centred = (act[i, sl, :] - mean) * inv
        return carry[0] + fold8(grad * centred), carry[1] + fold8(grad)

    sums = chunks(sum_body, (zeros(8, D),) * 2, RC)
    sm_b[13] += sums[0]
    sm_b[14] += sums[1]


def stage_c1(i, act, slope, bng, stats, bsums, bg, sm_c, mask, plane2):
    mean, inv, count = (stats[k : k + 1, :] for k in range(3))
    coef = inv * bg[...]
    by_centred = bsums[0:1, :] / count * inv
    const = bsums[1:2, :] / count - mean * by_centred

    def body(r, sl, carry):
        grad = (bng[i, sl, :] - const - act[i, sl, :] * by_centred) * coef
        err = grad * wide(mask[sl, :]) * slope[i, sl, :].astype(F32)
        to_plane(plane2, r, err)
        return carry + fold8(err)

    sm_c[14] += chunks(body, zeros(8, D), RC)


def stage_c2(i, vh2, g2, b2, st1, sm_c, mask, plane2, back):
    for c in range(3):
        cs = slice(c * L, (c + 1) * L)
        taps = taps_of(st1, cs)

        def back_body(r, carry):
            kernel = list(carry)
            sls = [rows((r * 4 + o) * G, G) for o in range(4)]
            vs = [(vh2[i, sl, cs] * g2[:, cs] + b2[:, cs]) * mask[sl, :] for sl in sls]
            outs = stencil_back(plane2, c, r, taps, vs, kernel)
            for o in range(4):
                back[sls[o], cs] = outs[o] * mask[sls[o], :]
            return tuple(kernel)

        found = lax.fori_loop(0, G // 4, back_body, (zeros(8, L),) * 9)
        for k in range(9):
            sm_c[5 + k, :, cs] += found[k]


def stage_c3(i, resid, vh2, r2, fm, g2, sm_c, mask, back, plow):
    def body(r, sl, carry):
        gain_sum, shift_sum, bias_sum = carry
        mk = wide(mask[sl, :])
        err = back[sl, :]
        vhat = vh2[i, sl, :]
        shift_sum = shift_sum + fold8(err)
        gain_sum = gain_sum + fold8(err * vhat)
        eg = err * g2[...]
        mean1 = lane_mean(eg)
        mean2 = lane_mean(eg * vhat)
        grad = resid[i, sl, :] + wide(r2[i, sl, :]) * (eg - mean1 - vhat * mean2)
        resid[i, sl, :] = grad
        err = grad * mk * fm[...]
        bias_sum = bias_sum + fold8(err)
        plow[i, sl, :] = err.astype(BF16)
        return gain_sum, shift_sum, bias_sum

    sums = chunks(body, (zeros(8, D),) * 3, RC)
    for k in range(3):
        sm_c[2 + k] += sums[k]


def stage_c4(mixed, dwm, plow):
    images = mixed.shape[0]
    dwm[...] = dot(mixed[...].reshape(images * T, D), plow[...].reshape(images * T, D), TN)


def stage_c4b(i, wm, plow):
    plow[i] = dot(plow[i], wm[...], NT).astype(BF16)


def stage_c5(i, qkv, score, sqk, srow, sharp_mask, plow, pmat, alow, cqk):
    raw = dot(plow[i], qkv[i, :, 2 * D :], TN)
    sq, sk = sqk[i, 0, 0:1, :], sqk[i, 1, 0:1, :]
    sqcol = column_of(sq)
    colsum = zeros(8, D)
    rowsums = []
    for h in range(HEADS):
        band = slice(h * HD, (h + 1) * HD)
        sc = score[i, band, :]
        sh = sharp_mask[band, :]
        pr = softmax_band(sc, sh)
        pmat[band, :] = pr.astype(BF16)
        weighted = raw[band] * pr
        logit = weighted - pr * jnp.sum(weighted, axis=1, keepdims=True)
        lg = logit * sh
        cross = lg * sc
        rowsums.append(jnp.sum(cross, axis=1, keepdims=True))
        colsum = colsum + fold8(cross)
        alow[band, :] = (lg * wide(sqcol[band]) * sk).astype(BF16)
    rowcol = jnp.concatenate(rowsums, axis=0)
    rowrow = jnp.broadcast_to(rowcol, (D, L)).T[0:1, :]
    srow[...] += rowrow
    cqk[0:1, :] = sq * sq * rowrow
    cqk[1:2, :] = sk * sk * total(colsum)


def stage_c6(i, qkv, smq, plow, pmat, alow, cqk):
    cq, ck = cqk[0:1, :], cqk[1:2, :]
    qv, kv = qkv[i, :, :D], qkv[i, :, D : 2 * D]
    grads = (
        dot(kv, alow[...], NT) - qv.astype(F32) * cq,
        dot(qv, alow[...]) - kv.astype(F32) * ck,
        dot(plow[i], pmat[...]),
    )
    for p in range(3):
        cols = slice(p * D, (p + 1) * D)
        smq[:, cols] += fold8(grads[p])
        qkv[i, :, cols] = grads[p].astype(BF16)


def stage_c7(n1, qkv, dwq, dwk, dwv):
    images = n1.shape[0]
    left = n1[...].reshape(images * T, D).T
    for p, out in enumerate((dwq, dwk, dwv)):
        out[...] = dot(left, qkv[:, :, p * D : (p + 1) * D].reshape(images * T, D))


def stage_c8(i, x, g1, wqkv, resid, sm_c, mask, qkv):
    err = dot(qkv[i], wqkv[...], NT) * wide(mask[...])
    xs = x[i].astype(F32)
    centre = xs - lane_mean(xs)
    spread = lax.rsqrt(lane_mean(centre * centre) + EPS_NORM)
    vhat = centre * spread
    sm_c[1] += fold8(err)
    sm_c[0] += fold8(err * vhat)
    eg = err * g1[...]
    mean1 = lane_mean(eg)
    mean2 = lane_mean(eg * vhat)
    x[i] = (resid[i] + spread * (eg - mean1 - vhat * mean2)).astype(BF16)


def geometry(n):
    chips = n // 2
    side = 2 if chips < 64 else 4
    return side, side, chips // (side * side)


class Place:
    def __init__(self, n):
        self.n = n
        self.me = lax.axis_index("img")
        x, y, z = geometry(n)
        self.axes = {}
        stride = 1
        for name, size in (("core", 2), ("x", x), ("y", y), ("z", z)):
            self.axes[name] = (size, stride, lax.rem(self.me // stride, size))
            stride *= size

    def other(self, k):
        return lax.rem(self.me + k, self.n)


def stream_steps(n, first):
    if n == 32:
        order = ("x", "y") if first else ("y", "x")
        return [("core", True), (order[0], True), (order[1], True), ("z", True)]
    order = ("x", "z") if first else ("z", "x")
    return [("core", True), (order[0], True), (order[1], True), ("y", False)]


STREAMS = (FF // 2,) * 6


def stream_shape(n, steps, size):
    axes = dict(zip(("core", "x", "y", "z"), (2,) + geometry(n)))
    received, copies, length = 0, 0, size
    for axis, split in steps:
        s = axes[axis]
        piece = length // s if split else length
        received += (s - 1) * piece
        copies += s - 1
        length = piece
    return received, copies


class Stream:
    def __init__(self, place, steps, buf, start, size, recv, sems, credits):
        self.place, self.buf, self.recv, self.sems, self.credits = place, buf, recv, sems, credits
        off, length, slot, sem = start, size, 0, 0
        self.down = []
        for axis, split in steps:
            s, stride, k = place.axes[axis]
            piece = length // s if split else length
            self.down.append((axis, split, off, piece, slot, sem))
            slot += (s - 1) * piece
            sem += s - 1
            if split:
                off = off + k * piece
            length = piece
        self.flying = []
        self.done = 0
        self.last = 2 * len(steps)

    def peers(self, axis):
        s, stride, k = self.place.axes[axis]
        for j in range(1, s):
            p = lax.rem(k + j, s)
            yield j, p, self.place.me + (p - k) * stride

    def send(self, src, dst, side, sem, device):
        copy = pltpu.make_async_remote_copy(
            src_ref=src,
            dst_ref=dst,
            send_sem=self.sems.at[side, sem],
            recv_sem=self.sems.at[side + 1, sem],
            device_id=(device,),
            device_id_type=MESH,
        )
        copy.start()
        self.flying.append(copy)

    def land(self):
        for copy in self.flying:
            copy.wait()
        self.flying = []

    def start_sum(self, step):
        axis, split, off, piece, slot, sem = self.down[step]
        for j, p, device in self.peers(axis):
            src = self.buf.at[rows(off + p * piece if split else off, piece), :]
            dst = self.recv.at[pl.ds(slot + (j - 1) * piece, piece), :]
            self.send(src, dst, 0, sem + j - 1, device)

    def finish_sum(self, step):
        axis, split, off, piece, slot, sem = self.down[step]
        s, stride, k = self.place.axes[axis]
        self.land()
        if split:
            for j, p, device in self.peers(axis):
                pl.semaphore_signal(self.credits.at[step], inc=1, device_id=(device,), device_id_type=MESH)
            own = off + k * piece
            size = math.gcd(piece, 96)

            def add(r, _):
                sl = rows(own + r * size, size)
                summed = self.buf[sl, :]
                for j in range(1, s):
                    summed = summed + self.recv[rows(slot + (j - 1) * piece + r * size, size), :]
                self.buf[sl, :] = summed
                return 0

            lax.fori_loop(0, piece // size, add, 0)
        else:
            sl = rows(off, piece)
            own = self.buf[sl, :]
            summed = None
            for q in range(s):
                j = lax.rem(k - q + s, s)
                at = slot + jnp.maximum(j - 1, 0) * piece
                term = jnp.where(k == q, own, self.recv[rows(at, piece), :])
                summed = term if summed is None else summed + term
            self.buf[sl, :] = summed

    def start_gather(self, step):
        axis, split, off, piece, slot, sem = self.down[step]
        if split:
            s, stride, k = self.place.axes[axis]
            pl.semaphore_wait(self.credits.at[step], s - 1)
            part = self.buf.at[rows(off + k * piece, piece), :]
            for j, p, device in self.peers(axis):
                self.send(part, part, 2, sem + j - 1, device)

    def advance(self):
        count, k = self.last // 2, self.done
        if 0 < k <= self.last:
            if k <= count:
                self.finish_sum(k - 1)
            else:
                self.land()
        if k < self.last:
            if k < count:
                self.start_sum(k)
            else:
                self.start_gather(self.last - 1 - k)
        self.done += 1


def stream_rows(n, sizes):
    return [stream_shape(n, stream_steps(n, k % 2 == 0), size)[0] for k, size in enumerate(sizes)]


def push_all(place, source, target, sems):
    def start(k, _):
        device = place.other(k)
        pltpu.make_async_remote_copy(
            src_ref=source(device),
            dst_ref=target,
            send_sem=sems.at[0],
            recv_sem=sems.at[1],
            device_id=(device,),
            device_id_type=MESH,
        ).start()
        return 0

    lax.fori_loop(1, place.n, start, 0)


def land_all(most, sems):
    for k in range(2):
        pltpu.make_async_copy(most, most, sems.at[k]).wait()


def put_small(small, k, row):
    for c in range(3):
        small[3 * k + c : 3 * k + c + 1, :] = row[:, c * L : (c + 1) * L]


def get_small(small, k):
    return jnp.concatenate([small[3 * k + c : 3 * k + c + 1, :] for c in range(3)], axis=1)


def mega_kernel(n, images, refs):
    (edges, sharp, x_in, sens_in, wqkv, wm, w1_in, w2_in, st1, st2,
     g1_in, b1_in, bqkv_in, bm_in, fm_in, g2_in, b2_in, cb1_in, bg_in, bo_in, cb2_in, fl_in, g3_in, b3_in, bb1_in, bb2_in, fp_in,
     lout, gin, dwqkv_out, dwm_out, dw1_out, dw2_out, small_out,
     vecs, x, sens, w1, w2, n1, qkv, mixed, score, sqk, r2, resid, vh2, act, vh3, slope, stat, stats, bsums, cqk,
     mask, sharp_mask, pmat, alow, plane, plane2, r3, n3, f2, hl, e1,
     sm_b, smf, sm_c, smq, srow, grads, recv, small, payload, gathered,
     in_sems, out_sems, group_sems, credits, push_sems) = refs
    place = Place(n)
    me = place.me
    barrier = pltpu.get_barrier_semaphore()

    def greet(k, _):
        pl.semaphore_signal(barrier, inc=1, device_id=(place.other(k),), device_id_type=MESH)
        return 0

    lax.fori_loop(1, n, greet, 0)

    x_copies = [pltpu.make_async_copy(x_in.at[k], x.at[k], in_sems.at[k]) for k in range(images)]
    later = [(w1_in, w1), (w2_in, w2), (sens_in, sens)]
    later_copies = [pltpu.make_async_copy(a, b, in_sems.at[images + k]) for k, (a, b) in enumerate(later)]
    for copy in x_copies + later_copies:
        copy.start()

    names = {}
    at = 0
    vectors = (("g1", g1_in), ("b1", b1_in), ("bm", bm_in), ("fm", fm_in), ("g2", g2_in), ("b2", b2_in), ("cb1", cb1_in),
               ("bg", bg_in), ("bo", bo_in), ("cb2", cb2_in), ("fl", fl_in), ("g3", g3_in), ("b3", b3_in), ("bb2", bb2_in),
               ("fp", fp_in))
    for name, ref in vectors:
        vecs[at : at + 1, 0:D] = ref[...].reshape(1, D)
        names[name] = vecs.at[at : at + 1, 0:D]
        at += 1
    vecs[at : at + 1, 0 : 3 * D] = bqkv_in[...].reshape(1, 3 * D)
    bqkv = vecs.at[at : at + 1, 0 : 3 * D]
    vecs[at + 1 : at + 2, :] = bb1_in[...].reshape(1, FF)
    bb1 = vecs.at[at + 1 : at + 2, :]
    g1, b1, bm, fm, g2, b2, cb1, bg, bo, cb2, fl, g3, b3, bb2, fp = (names[name] for name, ref in vectors)

    write_sharp(sharp_mask, sharp)
    for ref in (plane, plane2, sm_b, smf, sm_c, smq, srow, small):
        ref[...] = jnp.zeros_like(ref)
    dwq, dwk, dwv, dwm = (grads.at[k * D : (k + 1) * D, :] for k in range(4))
    branch, back = grads.at[0:T, :], grads.at[T : 2 * T, :]
    dw2 = grads.at[4 * D + FF : 4 * D + 2 * FF, :]
    dw1 = grads.at[4 * D : 4 * D + FF, :]
    grads[4 * D :, :] = zeros(2 * FF, D)

    for copy in x_copies:
        copy.wait()

    def front(i, _):
        edge = edges[i]
        write_mask(edge, mask)
        stage_a1(i, x, g1, b1, n1, mask)
        stage_a2(i, wqkv, bqkv, n1, qkv, sqk, mask)
        stage_a3(i, qkv, sqk, score, sharp_mask, pmat)
        stage_a4(i, x, wm, bm, fm, g2, b2, qkv, mixed, resid, vh2, r2, mask, plane, pmat)
        stage_a5(i, st1, cb1, act, slope, stat, mask, plane)
        stage_a6(i, edge, act, stat, mask)
        return 0

    lax.fori_loop(0, images, front, 0)

    merged = merge_stats([tuple(stat[i, k : k + 1, :] for k in range(3)) for i in range(images)])
    for k in range(2):
        put_small(payload.at[0], k, merged[k])
    payload[0, 6:7, :] = merged[2][:, 0:L]
    pl.semaphore_wait(barrier, n - 1)
    push_all(place, lambda device: payload.at[0], gathered.at[0, me], push_sems.at[0])
    gathered[0, me] = payload[0]
    for copy in later_copies:
        copy.wait()
    land_all(gathered.at[0, pl.ds(0, n - 1)], push_sems.at[0])

    def sum_both(k, carry):
        return carry + gathered[0, k]

    summed = lax.fori_loop(0, n, sum_both, zeros(8, L))
    count = summed[6:7, :]
    mean = summed[0:3, :] / count

    def sum_squares(k, carry):
        part = gathered[0, k]
        own = part[6:7, :]
        gap = part[0:3, :] / own - mean
        return carry + part[3:6, :] + own * gap * gap

    square = lax.fori_loop(0, n, sum_squares, zeros(3, L))
    inv = lax.rsqrt(square / count + EPS_BATCH)
    for c in range(3):
        stats[0:1, c * L : (c + 1) * L] = mean[c : c + 1, :]
        stats[1:2, c * L : (c + 1) * L] = inv[c : c + 1, :]
        stats[2:3, c * L : (c + 1) * L] = count

    def middle(i, _):
        write_mask(edges[i], mask)
        stage_b1(i, act, stats, bg, bo, mask, plane)
        stage_b2(i, st2, cb2, fl, resid, mask, plane)
        stage_b3(i, sens, g3, b3, fp, sm_b, mask, resid, vh3, r3, n3, f2)
        stage_b4(w1, bb1, w2, smf, n3, f2, hl, e1, branch, back)
        stage_b5(i, sens, bb2, fp, g3, fl, resid, sm_b, mask, vh3, r3, branch, back)
        stage_b6(dw1, n3, e1)
        stage_b7(dw2, hl, f2)
        return 0

    lax.fori_loop(0, images, middle, 0)
    out_copies = [pltpu.make_async_copy(sens, lout, out_sems.at[0])]
    out_copies[0].start()

    def conv_back(i, _):
        write_mask(edges[i], mask)
        stage_b8(i, act, stats, bg, bo, fl, st2, resid, vh3, sm_b, mask, plane, plane2)
        return 0

    lax.fori_loop(0, images, conv_back, 0)
    for k in range(15):
        put_small(small, k, total(sm_b[k]))
    for j in range(4):
        put_small(small, 15 + j, total(smf[:, j * D : (j + 1) * D]))
    for k in range(2):
        put_small(payload.at[1], k, total(sm_b[13 + k]))
    payload[1, 6:8, :] = zeros(2, L)
    push_all(place, lambda device: payload.at[1], gathered.at[1, me], push_sems.at[1])
    gathered[1, me] = payload[1]
    land_all(gathered.at[1, pl.ds(0, n - 1)], push_sems.at[1])
    summed = lax.fori_loop(0, n, lambda k, carry: carry + gathered[1, k], zeros(8, L))
    for k in range(2):
        bsums[k : k + 1, :] = jnp.concatenate([summed[3 * k + c : 3 * k + c + 1] for c in range(3)], axis=1)

    def rear1(i, _):
        write_mask(edges[i], mask)
        stage_c1(i, act, slope, vh3, stats, bsums, bg, sm_c, mask, plane2)
        stage_c2(i, vh2, g2, b2, st1, sm_c, mask, plane2, back)
        stage_c3(i, resid, vh2, r2, fm, g2, sm_c, mask, back, slope)
        return 0

    lax.fori_loop(0, images, rear1, 0)
    stage_c4(mixed, dwm, slope)

    def rear2(i, _):
        stage_c4b(i, wm, slope)
        stage_c5(i, qkv, score, sqk, srow, sharp_mask, slope, pmat, alow, cqk)
        stage_c6(i, qkv, smq, slope, pmat, alow, cqk)
        return 0

    lax.fori_loop(0, images, rear2, 0)
    stage_c7(n1, qkv, dwq, dwk, dwv)

    def rear3(i, _):
        write_mask(edges[i], mask)
        stage_c8(i, x, g1, wqkv, resid, sm_c, mask, qkv)
        return 0

    lax.fori_loop(0, images, rear3, 0)
    out_copies.append(pltpu.make_async_copy(x, gin, out_sems.at[1]))
    out_copies[1].start()
    for k in range(15):
        put_small(small, 19 + k, total(sm_c[k]))
    for p in range(3):
        put_small(small, 34 + p, total(smq[:, p * D : (p + 1) * D]))
    put_small(small, 37, srow[...])

    push_all(place, lambda device: small.at[rows(device * 8, 8), :], gathered.at[0, me], push_sems.at[2])
    gathered[0, me] = small[rows(me * 8, 8), :]
    streams = []
    at, start = 0, 0
    for k, (size, received) in enumerate(zip(STREAMS, stream_rows(n, STREAMS))):
        piece = recv.at[pl.ds(at, received), :]
        steps = stream_steps(n, k % 2 == 0)
        streams.append(Stream(place, steps, grads, start, size, piece, group_sems.at[k], credits.at[k]))
        at, start = at + received, start + size
    for stream in streams:
        stream.advance()
    land_all(gathered.at[0, pl.ds(0, n - 1)], push_sems.at[2])
    gathered[1, me] = lax.fori_loop(0, n, lambda k, carry: carry + gathered[0, k], zeros(8, L))
    push_all(place, lambda device: gathered.at[1, me], gathered.at[1, me], push_sems.at[3])
    for k in range(streams[0].last):
        for stream in streams:
            stream.advance()
    land_all(gathered.at[1, pl.ds(0, n - 1)], push_sems.at[3])
    for k in range(16):
        small[8 * k : 8 * k + 8, :] = gathered[1, k]

    weights = [(grads.at[p * D : (p + 1) * D, :], dwqkv_out.at[:, p * D : (p + 1) * D]) for p in range(3)]
    weights.append((dwm, dwm_out))
    weights += [(grads.at[(4 + j) * D : (5 + j) * D, :], dw1_out.at[:, j * D : (j + 1) * D]) for j in range(4)]
    weights.append((dw2, dw2_out))
    for k, (a, b) in enumerate(weights):
        out_copies.append(pltpu.make_async_copy(a, b, out_sems.at[2 + k]))
        out_copies[-1].start()

    def branch_factor(weight, grad, bias, bias_grad, factor):
        return (total(weight.astype(F32) * grad) + bias * bias_grad) / factor

    picked = [get_small(small, k) for k in range(38)]
    picked.append(branch_factor(wm[...], dwm[...], bm[...], picked[19 + 4], fm[...]))
    local = sum(st2[a, b : b + 1, :] * picked[4 + 3 * a + b] for a in range(3) for b in range(3))
    picked.append((local + cb2[...] * picked[3]) / fl[...])
    picked.append(branch_factor(w2[...], dw2[...], bb2[...], picked[2], fp[...]))
    for k, row in enumerate(picked):
        small_out[k : k + 1, :] = row
    for copy in out_copies:
        copy.wait()


def on_device(n, x, sens, edges, g1, b1, wqkv, bqkv, sharp, wm, bm, fm, g2, b2, st1, cb1, bg, bo, st2, cb2, fl, g3, b3,
              w1, bb1, w2, bb2, fp):
    images = x.shape[0]
    S = jax.ShapeDtypeStruct
    V = pltpu.VMEM
    vm = pl.BlockSpec(memory_space=pltpu.VMEM)
    sm = pl.BlockSpec(memory_space=pltpu.SMEM)
    hbm = pl.BlockSpec(memory_space=pl.ANY)
    full = (images, T, D)
    small_rows = max(16 * 8, 8 * n)
    dma = pltpu.SemaphoreType.DMA
    copies = stream_shape(n, stream_steps(n, True), FF)[1]
    lout, gin, dwqkv, dwm, dw1, dw2, small = pl.pallas_call(
        lambda *refs: mega_kernel(n, images, refs),
        in_specs=[sm, sm, hbm, hbm, vm, vm, hbm, hbm, vm, vm] + [vm] * 17,
        out_specs=[hbm] * 6 + [vm],
        out_shape=[S(full, BF16), S(full, BF16), S((D, 3 * D), F32), S((D, D), F32), S((D, FF), F32), S((FF, D), F32),
                   S((48, D), F32)],
        scratch_shapes=[
            V((24, FF), F32), V(full, BF16), V(full, BF16), V((D, FF), BF16), V((FF, D), BF16),
            V(full, BF16), V((images, T, 3 * D), BF16), V(full, BF16),
            V((images, D, D), F32), V((images, 2, 8, D), F32),
            V((images, T, L), F32), V(full, F32), V(full, F32), V(full, F32), V(full, F32),
            V(full, BF16), V((images, 8, D), F32), V((8, D), F32), V((8, D), F32), V((8, D), F32),
            V((T, L), F32), V((D, D), F32), V((D, D), BF16), V((D, D), BF16), V((3, PLANE, L), F32), V((3, PLANE, L), F32),
            V((T, L), F32), V((T, D), BF16), V((T, D), BF16), V((T, FF), BF16), V((T, FF), BF16),
            V((15, 8, D), F32), V((8, FF), F32), V((15, 8, D), F32), V((8, 3 * D), F32), V((1, D), F32),
            V((4 * D + 2 * FF, D), F32), V((sum(stream_rows(n, STREAMS)), D), F32),
            V((small_rows, L), F32), V((2, 8, L), F32), V((2, n, 8, L), F32),
            dma((images + 3,)), dma((11,)), dma((len(STREAMS), 4, copies)),
            pltpu.SemaphoreType.REGULAR((len(STREAMS), 4)), dma((4, 2)),
        ],
        compiler_params=pltpu.CompilerParams(
            collective_id=0, has_side_effects=True, vmem_limit_bytes=64 * 1024 * 1024
        ),
    )(edges, sharp, x, sens, wqkv, wm, w1, w2, st1, st2, g1, b1, bqkv, bm, fm, g2, b2, cb1, bg, bo, cb2, fl, g3, b3, bb1, bb2, fp)

    sharp_grad = jnp.sum(small[37].reshape(HEADS, HD), axis=1) / sharp
    c = 19
    return (lout, gin, small[c], small[c + 1], dwqkv, small[34:37].reshape(3 * D), sharp_grad, dwm, small[c + 4], small[38],
            small[c + 2], small[c + 3], small[c + 5 : c + 14].reshape(3, 3, D), small[c + 14], small[13], small[14],
            small[4:13].reshape(3, 3, D), small[3], small[39], small[0], small[1], dw1, small[15:19].reshape(FF), dw2,
            small[2], small[40])


def solution(mesh):
    n = mesh.shape["img"]
    split = P("img", None, None)
    return jax.shard_map(
        lambda *args: on_device(n, *args),
        mesh=mesh,
        in_specs=(split, split, P("img")) + (P(),) * 24,
        out_specs=(split, split) + (P(),) * 24,
        check_vma=False,
    )
```

```python
import math

import jax
import jax.numpy as jnp
from jax import lax
from jax.experimental import pallas as pl
from jax.experimental.pallas import tpu as pltpu
from jax.sharding import PartitionSpec as P

EPS_NORM = 1e-06
EPS_BATCH = 1e-05
EPS_UNIT = 1e-06
F32 = jnp.float32
BF16 = jnp.bfloat16
MESH = pl.DeviceIdType.MESH
G = 24
T = G * G
D = 384
FF = 1536
HEADS = 8
HD = 48
L = 128
PITCH = 32
PLANE = (G + 4) * PITCH
RC = T
RM = T
RF = T // 2
ROOT_HALF = 0.7071067811865476
ROOT_TWO_PI = 0.3989422804014327
NT = (((1,), (1,)), ((), ()))
TN = (((0,), (0,)), ((), ()))


def dot(a, b, dims=(((1,), (0,)), ((), ()))):
    return lax.dot_general(a, b, dims, preferred_element_type=F32)


def rows(start, size):
    return pl.ds(pl.multiple_of(start, 8), size)


def wide(v, times=3):
    return jnp.concatenate([v] * times, axis=1)


def fold8(v):
    return jnp.sum(v.reshape(v.shape[0] // 8, 8, v.shape[1]), axis=0)


def total(v):
    return jnp.sum(v, axis=0, keepdims=True)


def zeros(*shape):
    return jnp.zeros(shape, F32)


def lane_mean(v):
    return jnp.mean(v, axis=1, keepdims=True)


def gelu_pair(u):
    phi = 0.5 + 0.5 * lax.erf(u * ROOT_HALF)
    bell = jnp.exp((u * u) * -0.5)
    return u * phi, phi + u * (bell * ROOT_TWO_PI)


def column_of(row):
    return jnp.broadcast_to(row, (L, D)).T


def write_mask(edge, mask):
    row_index = lax.broadcasted_iota(jnp.int32, (G, G, L), 0)
    col_index = lax.broadcasted_iota(jnp.int32, (G, G, L), 1)
    keep = (row_index < edge) & (col_index < edge)
    mask[...] = keep.astype(F32).reshape(T, L)


def write_sharp(sharp_mask, sharp):
    lane = lax.broadcasted_iota(jnp.int32, (HD, D), 1)
    for h in range(HEADS):
        own = (lane >= h * HD) & (lane < (h + 1) * HD)
        sharp_mask[h * HD : (h + 1) * HD, :] = jnp.where(own, sharp[h], 0.0)


def to_plane(plane, r, value):
    count = value.shape[0] // G
    for g in range(count):
        for c in range(3):
            plane[c, rows((r * count + g + 2) * PITCH, G), :] = value[g * G : (g + 1) * G, c * L : (c + 1) * L]


def taps_of(st, cs):
    return [jnp.broadcast_to(st[a, b : b + 1, cs], (G, L)) for a in range(3) for b in range(3)]


def stencil(plane, c, r, taps, count):
    base = r * (count * PITCH)
    outs = [None] * count
    for a in range(count + 2):
        for b in range(3):
            v = plane[c, pl.ds(base + (a + 1) * PITCH - 1 + b, G), :]
            for o in range(count):
                if 0 <= a - o < 3:
                    t = v * taps[(a - o) * 3 + b]
                    outs[o] = t if outs[o] is None else outs[o] + t
    return outs


def stencil_back(plane, c, r, taps, vs, kernel):
    count = len(vs)
    base = r * (count * PITCH)
    outs = [None] * count
    for a in range(count + 2):
        for b in range(3):
            v = plane[c, pl.ds(base + (a + 1) * PITCH - 1 + b, G), :]
            for o in range(count):
                if 0 <= a - o < 3:
                    k = (2 - (a - o)) * 3 + (2 - b)
                    t = v * taps[k]
                    outs[o] = t if outs[o] is None else outs[o] + t
                    kernel[k] = kernel[k] + fold8(v * vs[o])
    return outs


def chunks(body, init, size):
    if size == T:
        return body(0, pl.ds(0, T), init)
    return lax.fori_loop(0, T // size, lambda r, c: body(r, rows(r * size, size), c), init)


def stage_a1(i, x, g1, b1, n1, mask):
    def body(r, sl, carry):
        xs = x[i, sl, :].astype(F32)
        mean = lane_mean(xs)
        centre = xs - mean
        spread = lax.rsqrt(lane_mean(centre * centre) + EPS_NORM)
        n1[i, sl, :] = ((centre * spread * g1[...] + b1[...]) * wide(mask[sl, :])).astype(BF16)
        return carry

    chunks(body, 0, RC)


def stage_a2(i, wqkv, bqkv, n1, qkv, sqk, mask):
    def body(r, sl, carry):
        sums = list(carry)
        mk = wide(mask[sl, :])
        normed = n1[i, sl, :]
        for p in range(3):
            cols = slice(p * D, (p + 1) * D)
            part = (dot(normed, wqkv[:, cols]) + bqkv[:, cols]) * mk
            if p < 2:
                sums[p] = sums[p] + fold8(part * part)
            qkv[i, sl, cols] = part.astype(BF16)
        return tuple(sums)

    sums = chunks(body, (zeros(8, D), zeros(8, D)), RM)
    for p in range(2):
        sqk[i, p] = jnp.broadcast_to(lax.rsqrt(total(sums[p]) + EPS_UNIT), (8, D))


def softmax_band(sc, sh):
    ex = jnp.where(sh > 0.0, jnp.exp(sc * sh), 0.0)
    return ex / jnp.sum(ex, axis=1, keepdims=True)


def stage_a3(i, qkv, sqk, score, sharp_mask, pmat):
    sq, sk = sqk[i, 0, 0:1, :], sqk[i, 1, 0:1, :]
    sqcol = column_of(sq)
    raw = dot(qkv[i, :, :D], qkv[i, :, D : 2 * D], TN)
    for h in range(HEADS):
        band = slice(h * HD, (h + 1) * HD)
        sc = raw[band] * wide(sqcol[band]) * sk
        score[i, band, :] = sc
        pmat[band, :] = softmax_band(sc, sharp_mask[band, :]).astype(BF16)


def stage_a4(i, x, wm, bm, fm, g2, b2, qkv, mixed, resid, vh2, r2, mask, plane, pmat):
    def body(r, sl, carry):
        mk = wide(mask[sl, :])
        mx = dot(qkv[i, sl, 2 * D :], pmat[...], NT).astype(BF16)
        mixed[i, sl, :] = mx
        branch = (dot(mx, wm[...]) + bm[...]) * mk
        res = x[i, sl, :].astype(F32) + fm[...] * branch
        resid[i, sl, :] = res
        mean = lane_mean(res)
        centre = res - mean
        spread = lax.rsqrt(lane_mean(centre * centre) + EPS_NORM)
        vhat = centre * spread
        vh2[i, sl, :] = vhat
        r2[i, sl, :] = jnp.broadcast_to(spread, (RM, L))
        to_plane(plane, r, (vhat * g2[...] + b2[...]) * mk)
        return carry

    chunks(body, 0, RM)


def stage_a5(i, st1, cb1, act, slope, stat, mask, plane):
    for c in range(3):
        cs = slice(c * L, (c + 1) * L)
        taps = taps_of(st1, cs)

        def conv_body(r, carry):
            outs = stencil(plane, c, r, taps, 4)
            diffs = []
            for o in range(4):
                sl = rows((r * 4 + o) * G, G)
                value, diff = gelu_pair(outs[o] + cb1[:, cs])
                value = value * mask[sl, :]
                act[i, sl, cs] = value
                diffs.append(diff)
                carry = carry + fold8(value)
            slope[i, pl.ds(pl.multiple_of(r * (4 * G), 32), 4 * G), cs] = jnp.concatenate(diffs, axis=0).astype(BF16)
            return carry

        stat[i, 0:1, cs] = total(lax.fori_loop(0, G // 4, conv_body, zeros(8, L)))


def stage_a6(i, edge, act, stat, mask):
    count = (edge * edge).astype(F32)
    mean = stat[i, 0:1, :] / count

    def body(r, sl, carry):
        dev = (act[i, sl, :] - mean) * wide(mask[sl, :])
        return carry + fold8(dev * dev)

    stat[i, 1:2, :] = total(chunks(body, zeros(8, D), RC))
    stat[i, 2:3, :] = jnp.full((1, D), count, F32)


def merge_stats(parts):
    summed = sum(p[0] for p in parts)
    count = sum(p[2] for p in parts)
    mean = summed / count
    square = sum(p[1] + p[2] * (p[0] / p[2] - mean) * (p[0] / p[2] - mean) for p in parts)
    return summed, square, count


def stage_b1(i, act, stats, bg, bo, mask, plane):
    mean, inv = stats[0:1, :], stats[1:2, :]
    scale = inv * bg[...]
    shift = bo[...] - mean * scale

    def body(r, sl, carry):
        to_plane(plane, r, (act[i, sl, :] * scale + shift) * wide(mask[sl, :]))
        return carry

    chunks(body, 0, RC)


def stage_b2(i, st2, cb2, fl, resid, mask, plane):
    for c in range(3):
        cs = slice(c * L, (c + 1) * L)
        taps = taps_of(st2, cs)

        def conv_body(r, carry):
            outs = stencil(plane, c, r, taps, 4)
            for o in range(4):
                sl = rows((r * 4 + o) * G, G)
                resid[i, sl, cs] = resid[i, sl, cs] + fl[:, cs] * ((outs[o] + cb2[:, cs]) * mask[sl, :])
            return carry

        lax.fori_loop(0, G // 4, conv_body, 0)


def stage_b3(i, sens, g3, b3, fp, sm_b, mask, resid, vh3, r3, n3, f2):
    def body(r, sl, carry):
        mk = wide(mask[sl, :])
        res = resid[i, sl, :]
        centre = res - lane_mean(res)
        spread = lax.rsqrt(lane_mean(centre * centre) + EPS_NORM)
        vhat = centre * spread
        vh3[i, sl, :] = vhat
        r3[sl, :] = jnp.broadcast_to(spread, (RC, L))
        n3[sl, :] = ((vhat * g3[...] + b3[...]) * mk).astype(BF16)
        err = sens[i, sl, :].astype(F32) * mk * fp[...]
        f2[sl, :] = err.astype(BF16)
        return carry + fold8(err)

    sm_b[2] += chunks(body, zeros(8, D), RC)


def stage_b4(w1, bb1, w2, smf, n3, f2, hl, e1, branch, back):
    def body(r, sl, hidden_sum):
        normed = n3[sl, :]
        low = f2[sl, :]
        parts = []
        for j in range(FF // 256):
            cols = slice(j * 256, (j + 1) * 256)
            value, diff = gelu_pair(dot(normed, w1[:, cols]) + bb1[:, cols])
            hl[sl, cols] = value.astype(BF16)
            err = dot(low, w2[cols, :], NT) * diff
            parts.append(fold8(err))
            e1[sl, cols] = err.astype(BF16)
        branch[sl, :] = dot(hl[sl, :], w2[...])
        back[sl, :] = dot(e1[sl, :], w1[...], NT)
        return hidden_sum + jnp.concatenate(parts, axis=1)

    smf[...] += chunks(body, zeros(8, FF), RF)


def stage_b5(i, sens, bb2, fp, g3, fl, resid, sm_b, mask, vh3, r3, branch, back):
    def body(r, sl, carry):
        gain_sum, shift_sum, local_sum = carry
        mk = wide(mask[sl, :])
        upstream = sens[i, sl, :].astype(F32) * mk
        sens[i, sl, :] = ((resid[i, sl, :] + fp[...] * (branch[sl, :] + bb2[...])) * mk).astype(BF16)
        err = back[sl, :] * mk
        vhat = vh3[i, sl, :]
        shift_sum = shift_sum + fold8(err)
        gain_sum = gain_sum + fold8(err * vhat)
        eg = err * g3[...]
        mean1 = lane_mean(eg)
        mean2 = lane_mean(eg * vhat)
        grad = upstream + wide(r3[sl, :]) * (eg - mean1 - vhat * mean2)
        resid[i, sl, :] = grad
        local_sum = local_sum + fold8(grad * mk)
        return gain_sum, shift_sum, local_sum

    sums = chunks(body, (zeros(8, D),) * 3, RC)
    sm_b[0] += sums[0]
    sm_b[1] += sums[1]
    sm_b[3] += sums[2] * fl[...]


def stage_b6(dw1, n3, e1):
    left = n3[...].T
    for j in range(FF // 512):
        part = dot(left, e1[:, j * 512 : (j + 1) * 512])
        for k in range(4):
            block, col = divmod(j * 512 + k * L, D)
            dw1[block * D : (block + 1) * D, col : col + L] += part[:, k * L : (k + 1) * L]


def stage_b7(dw2, hl, f2):
    dw2[...] += dot(hl[...], f2[...], TN)


def stage_b8(i, act, stats, bg, bo, fl, st2, resid, bng, sm_b, mask, plane, plane2):
    stage_b1(i, act, stats, bg, bo, mask, plane)

    def local_body(r, sl, carry):
        to_plane(plane2, r, resid[i, sl, :] * wide(mask[sl, :]) * fl[...])
        return carry

    chunks(local_body, 0, RC)
    mean, inv = stats[0:1, :], stats[1:2, :]
    for c in range(3):
        cs = slice(c * L, (c + 1) * L)
        taps = taps_of(st2, cs)

        def back_body(r, carry):
            kernel = list(carry)
            vs = [plane[c, rows((r * 4 + o + 2) * PITCH, G), :] for o in range(4)]
            outs = stencil_back(plane2, c, r, taps, vs, kernel)
            for o in range(4):
                sl = rows((r * 4 + o) * G, G)
                bng[i, sl, cs] = outs[o] * mask[sl, :]
            return tuple(kernel)

        found = lax.fori_loop(0, G // 4, back_body, (zeros(8, L),) * 9)
        for k in range(9):
            sm_b[4 + k, :, cs] += found[k]

    def sum_body(r, sl, carry):
        grad = bng[i, sl, :]
        centred = (act[i, sl, :] - mean) * inv
        return carry[0] + fold8(grad * centred), carry[1] + fold8(grad)

    sums = chunks(sum_body, (zeros(8, D),) * 2, RC)
    sm_b[13] += sums[0]
    sm_b[14] += sums[1]


def stage_c1(i, act, slope, bng, stats, bsums, bg, sm_c, mask, plane2):
    mean, inv, count = (stats[k : k + 1, :] for k in range(3))
    coef = inv * bg[...]
    by_centred = bsums[0:1, :] / count * inv
    const = bsums[1:2, :] / count - mean * by_centred

    def body(r, sl, carry):
        grad = (bng[i, sl, :] - const - act[i, sl, :] * by_centred) * coef
        err = grad * wide(mask[sl, :]) * slope[i, sl, :].astype(F32)
        to_plane(plane2, r, err)
        return carry + fold8(err)

    sm_c[14] += chunks(body, zeros(8, D), RC)


def stage_c2(i, vh2, g2, b2, st1, sm_c, mask, plane2, back):
    for c in range(3):
        cs = slice(c * L, (c + 1) * L)
        taps = taps_of(st1, cs)

        def back_body(r, carry):
            kernel = list(carry)
            sls = [rows((r * 4 + o) * G, G) for o in range(4)]
            vs = [(vh2[i, sl, cs] * g2[:, cs] + b2[:, cs]) * mask[sl, :] for sl in sls]
            outs = stencil_back(plane2, c, r, taps, vs, kernel)
            for o in range(4):
                back[sls[o], cs] = outs[o] * mask[sls[o], :]
            return tuple(kernel)

        found = lax.fori_loop(0, G // 4, back_body, (zeros(8, L),) * 9)
        for k in range(9):
            sm_c[5 + k, :, cs] += found[k]


def stage_c3(i, resid, vh2, r2, fm, g2, sm_c, mask, back, plow):
    def body(r, sl, carry):
        gain_sum, shift_sum, bias_sum = carry
        mk = wide(mask[sl, :])
        err = back[sl, :]
        vhat = vh2[i, sl, :]
        shift_sum = shift_sum + fold8(err)
        gain_sum = gain_sum + fold8(err * vhat)
        eg = err * g2[...]
        mean1 = lane_mean(eg)
        mean2 = lane_mean(eg * vhat)
        grad = resid[i, sl, :] + wide(r2[i, sl, :]) * (eg - mean1 - vhat * mean2)
        resid[i, sl, :] = grad
        err = grad * mk * fm[...]
        bias_sum = bias_sum + fold8(err)
        plow[i, sl, :] = err.astype(BF16)
        return gain_sum, shift_sum, bias_sum

    sums = chunks(body, (zeros(8, D),) * 3, RC)
    for k in range(3):
        sm_c[2 + k] += sums[k]


def stage_c4(mixed, dwm, plow):
    images = mixed.shape[0]
    dwm[...] = dot(mixed[...].reshape(images * T, D), plow[...].reshape(images * T, D), TN)


def stage_c4b(i, wm, plow):
    plow[i] = dot(plow[i], wm[...], NT).astype(BF16)


def stage_c5(i, qkv, score, sqk, srow, sharp_mask, plow, pmat, alow, cqk):
    raw = dot(plow[i], qkv[i, :, 2 * D :], TN)
    sq, sk = sqk[i, 0, 0:1, :], sqk[i, 1, 0:1, :]
    sqcol = column_of(sq)
    colsum = zeros(8, D)
    rowsums = []
    for h in range(HEADS):
        band = slice(h * HD, (h + 1) * HD)
        sc = score[i, band, :]
        sh = sharp_mask[band, :]
        pr = softmax_band(sc, sh)
        pmat[band, :] = pr.astype(BF16)
        weighted = raw[band] * pr
        logit = weighted - pr * jnp.sum(weighted, axis=1, keepdims=True)
        lg = logit * sh
        cross = lg * sc
        rowsums.append(jnp.sum(cross, axis=1, keepdims=True))
        colsum = colsum + fold8(cross)
        alow[band, :] = (lg * wide(sqcol[band]) * sk).astype(BF16)
    rowcol = jnp.concatenate(rowsums, axis=0)
    rowrow = jnp.broadcast_to(rowcol, (D, L)).T[0:1, :]
    srow[...] += rowrow
    cqk[0:1, :] = sq * sq * rowrow
    cqk[1:2, :] = sk * sk * total(colsum)


def stage_c6(i, qkv, smq, plow, pmat, alow, cqk):
    cq, ck = cqk[0:1, :], cqk[1:2, :]
    qv, kv = qkv[i, :, :D], qkv[i, :, D : 2 * D]
    grads = (
        dot(kv, alow[...], NT) - qv.astype(F32) * cq,
        dot(qv, alow[...]) - kv.astype(F32) * ck,
        dot(plow[i], pmat[...]),
    )
    for p in range(3):
        cols = slice(p * D, (p + 1) * D)
        smq[:, cols] += fold8(grads[p])
        qkv[i, :, cols] = grads[p].astype(BF16)


def stage_c7(n1, qkv, dwq, dwk, dwv):
    images = n1.shape[0]
    left = n1[...].reshape(images * T, D).T
    for p, out in enumerate((dwq, dwk, dwv)):
        out[...] = dot(left, qkv[:, :, p * D : (p + 1) * D].reshape(images * T, D))


def stage_c8(i, x, g1, wqkv, resid, sm_c, mask, qkv):
    err = dot(qkv[i], wqkv[...], NT) * wide(mask[...])
    xs = x[i].astype(F32)
    centre = xs - lane_mean(xs)
    spread = lax.rsqrt(lane_mean(centre * centre) + EPS_NORM)
    vhat = centre * spread
    sm_c[1] += fold8(err)
    sm_c[0] += fold8(err * vhat)
    eg = err * g1[...]
    mean1 = lane_mean(eg)
    mean2 = lane_mean(eg * vhat)
    x[i] = (resid[i] + spread * (eg - mean1 - vhat * mean2)).astype(BF16)


def geometry(n):
    chips = n // 2
    side = 2 if chips < 64 else 4
    return side, side, chips // (side * side)


class Place:
    def __init__(self, n):
        self.n = n
        self.me = lax.axis_index("img")
        x, y, z = geometry(n)
        self.axes = {}
        stride = 1
        for name, size in (("core", 2), ("x", x), ("y", y), ("z", z)):
            self.axes[name] = (size, stride, lax.rem(self.me // stride, size))
            stride *= size

    def other(self, k):
        return lax.rem(self.me + k, self.n)


def stream_steps(n, first):
    if n == 32:
        order = ("x", "y") if first else ("y", "x")
        return [("core", True), (order[0], True), (order[1], True), ("z", True)]
    order = ("x", "z") if first else ("z", "x")
    return [("core", True), (order[0], True), (order[1], True), ("y", False)]


STREAMS = (FF // 2,) * 6


def stream_shape(n, steps, size):
    axes = dict(zip(("core", "x", "y", "z"), (2,) + geometry(n)))
    received, copies, length = 0, 0, size
    for axis, split in steps:
        s = axes[axis]
        piece = length // s if split else length
        received += (s - 1) * piece
        copies += s - 1
        length = piece
    return received, copies


class Stream:
    def __init__(self, place, steps, buf, start, size, recv, sems, credits):
        self.place, self.buf, self.recv, self.sems, self.credits = place, buf, recv, sems, credits
        off, length, slot, sem = start, size, 0, 0
        self.down = []
        for axis, split in steps:
            s, stride, k = place.axes[axis]
            piece = length // s if split else length
            self.down.append((axis, split, off, piece, slot, sem))
            slot += (s - 1) * piece
            sem += s - 1
            if split:
                off = off + k * piece
            length = piece
        self.flying = []
        self.done = 0
        self.last = 2 * len(steps)

    def peers(self, axis):
        s, stride, k = self.place.axes[axis]
        for j in range(1, s):
            p = lax.rem(k + j, s)
            yield j, p, self.place.me + (p - k) * stride

    def send(self, src, dst, side, sem, device):
        copy = pltpu.make_async_remote_copy(
            src_ref=src,
            dst_ref=dst,
            send_sem=self.sems.at[side, sem],
            recv_sem=self.sems.at[side + 1, sem],
            device_id=(device,),
            device_id_type=MESH,
        )
        copy.start()
        self.flying.append(copy)

    def land(self):
        for copy in self.flying:
            copy.wait()
        self.flying = []

    def start_sum(self, step):
        axis, split, off, piece, slot, sem = self.down[step]
        for j, p, device in self.peers(axis):
            src = self.buf.at[rows(off + p * piece if split else off, piece), :]
            dst = self.recv.at[pl.ds(slot + (j - 1) * piece, piece), :]
            self.send(src, dst, 0, sem + j - 1, device)

    def finish_sum(self, step):
        axis, split, off, piece, slot, sem = self.down[step]
        s, stride, k = self.place.axes[axis]
        self.land()
        if split:
            for j, p, device in self.peers(axis):
                pl.semaphore_signal(self.credits.at[step], inc=1, device_id=(device,), device_id_type=MESH)
            own = off + k * piece
            size = math.gcd(piece, 96)

            def add(r, _):
                sl = rows(own + r * size, size)
                summed = self.buf[sl, :]
                for j in range(1, s):
                    summed = summed + self.recv[rows(slot + (j - 1) * piece + r * size, size), :]
                self.buf[sl, :] = summed
                return 0

            lax.fori_loop(0, piece // size, add, 0)
        else:
            sl = rows(off, piece)
            own = self.buf[sl, :]
            summed = None
            for q in range(s):
                j = lax.rem(k - q + s, s)
                at = slot + jnp.maximum(j - 1, 0) * piece
                term = jnp.where(k == q, own, self.recv[rows(at, piece), :])
                summed = term if summed is None else summed + term
            self.buf[sl, :] = summed

    def start_gather(self, step):
        axis, split, off, piece, slot, sem = self.down[step]
        if split:
            s, stride, k = self.place.axes[axis]
            pl.semaphore_wait(self.credits.at[step], s - 1)
            part = self.buf.at[rows(off + k * piece, piece), :]
            for j, p, device in self.peers(axis):
                self.send(part, part, 2, sem + j - 1, device)

    def advance(self):
        count, k = self.last // 2, self.done
        if 0 < k <= self.last:
            if k <= count:
                self.finish_sum(k - 1)
            else:
                self.land()
        if k < self.last:
            if k < count:
                self.start_sum(k)
            else:
                self.start_gather(self.last - 1 - k)
        self.done += 1


def stream_rows(n, sizes):
    return [stream_shape(n, stream_steps(n, k % 2 == 0), size)[0] for k, size in enumerate(sizes)]


def push_all(place, source, target, sems):
    def start(k, _):
        device = place.other(k)
        pltpu.make_async_remote_copy(
            src_ref=source(device),
            dst_ref=target,
            send_sem=sems.at[0],
            recv_sem=sems.at[1],
            device_id=(device,),
            device_id_type=MESH,
        ).start()
        return 0

    lax.fori_loop(1, place.n, start, 0)


def land_all(most, sems):
    for k in range(2):
        pltpu.make_async_copy(most, most, sems.at[k]).wait()


def put_small(small, k, row):
    for c in range(3):
        small[3 * k + c : 3 * k + c + 1, :] = row[:, c * L : (c + 1) * L]


def get_small(small, k):
    return jnp.concatenate([small[3 * k + c : 3 * k + c + 1, :] for c in range(3)], axis=1)


def mega_kernel(n, images, refs):
    (edges, sharp, x_in, sens_in, wqkv, wm, w1_in, w2_in, st1, st2,
     g1_in, b1_in, bqkv_in, bm_in, fm_in, g2_in, b2_in, cb1_in, bg_in, bo_in, cb2_in, fl_in, g3_in, b3_in, bb1_in, bb2_in, fp_in,
     lout, gin, dwqkv_out, dwm_out, dw1_out, dw2_out, small_out,
     vecs, x, sens, w1, w2, n1, qkv, mixed, score, sqk, r2, resid, vh2, act, vh3, slope, stat, stats, bsums, cqk,
     mask, sharp_mask, pmat, alow, plane, plane2, r3, n3, f2, hl, e1,
     sm_b, smf, sm_c, smq, srow, grads, recv, small, payload, gathered,
     in_sems, out_sems, group_sems, credits, push_sems) = refs
    place = Place(n)
    me = place.me
    barrier = pltpu.get_barrier_semaphore()

    def greet(k, _):
        pl.semaphore_signal(barrier, inc=1, device_id=(place.other(k),), device_id_type=MESH)
        return 0

    lax.fori_loop(1, n, greet, 0)

    x_copies = [pltpu.make_async_copy(x_in.at[k], x.at[k], in_sems.at[k]) for k in range(images)]
    later = [(w1_in, w1), (w2_in, w2), (sens_in, sens)]
    later_copies = [pltpu.make_async_copy(a, b, in_sems.at[images + k]) for k, (a, b) in enumerate(later)]
    for copy in x_copies + later_copies:
        copy.start()

    names = {}
    at = 0
    vectors = (("g1", g1_in), ("b1", b1_in), ("bm", bm_in), ("fm", fm_in), ("g2", g2_in), ("b2", b2_in), ("cb1", cb1_in),
               ("bg", bg_in), ("bo", bo_in), ("cb2", cb2_in), ("fl", fl_in), ("g3", g3_in), ("b3", b3_in), ("bb2", bb2_in),
               ("fp", fp_in))
    for name, ref in vectors:
        vecs[at : at + 1, 0:D] = ref[...].reshape(1, D)
        names[name] = vecs.at[at : at + 1, 0:D]
        at += 1
    vecs[at : at + 1, 0 : 3 * D] = bqkv_in[...].reshape(1, 3 * D)
    bqkv = vecs.at[at : at + 1, 0 : 3 * D]
    vecs[at + 1 : at + 2, :] = bb1_in[...].reshape(1, FF)
    bb1 = vecs.at[at + 1 : at + 2, :]
    g1, b1, bm, fm, g2, b2, cb1, bg, bo, cb2, fl, g3, b3, bb2, fp = (names[name] for name, ref in vectors)

    write_sharp(sharp_mask, sharp)
    for ref in (plane, plane2, sm_b, smf, sm_c, smq, srow, small):
        ref[...] = jnp.zeros_like(ref)
    dwq, dwk, dwv, dwm = (grads.at[k * D : (k + 1) * D, :] for k in range(4))
    branch, back = grads.at[0:T, :], grads.at[T : 2 * T, :]
    dw2 = grads.at[4 * D + FF : 4 * D + 2 * FF, :]
    dw1 = grads.at[4 * D : 4 * D + FF, :]
    grads[4 * D :, :] = zeros(2 * FF, D)

    for copy in x_copies:
        copy.wait()

    def front(i, _):
        edge = edges[i]
        write_mask(edge, mask)
        stage_a1(i, x, g1, b1, n1, mask)
        stage_a2(i, wqkv, bqkv, n1, qkv, sqk, mask)
        stage_a3(i, qkv, sqk, score, sharp_mask, pmat)
        stage_a4(i, x, wm, bm, fm, g2, b2, qkv, mixed, resid, vh2, r2, mask, plane, pmat)
        stage_a5(i, st1, cb1, act, slope, stat, mask, plane)
        stage_a6(i, edge, act, stat, mask)
        return 0

    lax.fori_loop(0, images, front, 0)

    merged = merge_stats([tuple(stat[i, k : k + 1, :] for k in range(3)) for i in range(images)])
    for k in range(2):
        put_small(payload.at[0], k, merged[k])
    payload[0, 6:7, :] = merged[2][:, 0:L]
    pl.semaphore_wait(barrier, n - 1)
    push_all(place, lambda device: payload.at[0], gathered.at[0, me], push_sems.at[0])
    gathered[0, me] = payload[0]
    for copy in later_copies:
        copy.wait()
    land_all(gathered.at[0, pl.ds(0, n - 1)], push_sems.at[0])

    def sum_both(k, carry):
        return carry + gathered[0, k]

    summed = lax.fori_loop(0, n, sum_both, zeros(8, L))
    count = summed[6:7, :]
    mean = summed[0:3, :] / count

    def sum_squares(k, carry):
        part = gathered[0, k]
        own = part[6:7, :]
        gap = part[0:3, :] / own - mean
        return carry + part[3:6, :] + own * gap * gap

    square = lax.fori_loop(0, n, sum_squares, zeros(3, L))
    inv = lax.rsqrt(square / count + EPS_BATCH)
    for c in range(3):
        stats[0:1, c * L : (c + 1) * L] = mean[c : c + 1, :]
        stats[1:2, c * L : (c + 1) * L] = inv[c : c + 1, :]
        stats[2:3, c * L : (c + 1) * L] = count

    def middle(i, _):
        write_mask(edges[i], mask)
        stage_b1(i, act, stats, bg, bo, mask, plane)
        stage_b2(i, st2, cb2, fl, resid, mask, plane)
        stage_b3(i, sens, g3, b3, fp, sm_b, mask, resid, vh3, r3, n3, f2)
        stage_b4(w1, bb1, w2, smf, n3, f2, hl, e1, branch, back)
        stage_b5(i, sens, bb2, fp, g3, fl, resid, sm_b, mask, vh3, r3, branch, back)
        stage_b6(dw1, n3, e1)
        stage_b7(dw2, hl, f2)
        return 0

    lax.fori_loop(0, images, middle, 0)

    streams = []
    at, start = 0, 0
    for k, (size, received) in enumerate(zip(STREAMS, stream_rows(n, STREAMS))):
        piece = recv.at[pl.ds(at, received), :]
        steps = stream_steps(n, k % 2 == 0)
        streams.append(Stream(place, steps, grads, start, size, piece, group_sems.at[k], credits.at[k]))
        at, start = at + received, start + size

    def tick(*which):
        for k in which:
            if streams[k].done <= streams[k].last:
                streams[k].advance()

    tick(4, 5, 2, 3)
    out_copies = [pltpu.make_async_copy(sens, lout, out_sems.at[0])]
    out_copies[0].start()

    def conv_back(i, _):
        write_mask(edges[i], mask)
        stage_b8(i, act, stats, bg, bo, fl, st2, resid, vh3, sm_b, mask, plane, plane2)
        return 0

    lax.fori_loop(0, images // 2, conv_back, 0)
    tick(4, 5)
    lax.fori_loop(images // 2, images, conv_back, 0)
    for k in range(15):
        put_small(small, k, total(sm_b[k]))
    for j in range(4):
        put_small(small, 15 + j, total(smf[:, j * D : (j + 1) * D]))
    for k in range(2):
        put_small(payload.at[1], k, total(sm_b[13 + k]))
    payload[1, 6:8, :] = zeros(2, L)
    push_all(place, lambda device: payload.at[1], gathered.at[1, me], push_sems.at[1])
    gathered[1, me] = payload[1]
    land_all(gathered.at[1, pl.ds(0, n - 1)], push_sems.at[1])
    summed = lax.fori_loop(0, n, lambda k, carry: carry + gathered[1, k], zeros(8, L))
    for k in range(2):
        bsums[k : k + 1, :] = jnp.concatenate([summed[3 * k + c : 3 * k + c + 1] for c in range(3)], axis=1)

    def rear1(i, _):
        write_mask(edges[i], mask)
        stage_c1(i, act, slope, vh3, stats, bsums, bg, sm_c, mask, plane2)
        stage_c2(i, vh2, g2, b2, st1, sm_c, mask, plane2, back)
        stage_c3(i, resid, vh2, r2, fm, g2, sm_c, mask, back, slope)
        return 0

    tick(4, 5)
    lax.fori_loop(0, images // 2, rear1, 0)
    tick(4, 5, 2, 3)
    lax.fori_loop(images // 2, images, rear1, 0)
    stage_c4(mixed, dwm, slope)

    def rear2(i, _):
        stage_c4b(i, wm, slope)
        stage_c5(i, qkv, score, sqk, srow, sharp_mask, slope, pmat, alow, cqk)
        stage_c6(i, qkv, smq, slope, pmat, alow, cqk)
        return 0

    lax.fori_loop(0, images // 4, rear2, 0)
    tick(4, 5, 2, 3)
    lax.fori_loop(images // 4, images // 2, rear2, 0)
    tick(2, 3)
    lax.fori_loop(images // 2, images, rear2, 0)
    tick(4, 5)
    stage_c7(n1, qkv, dwq, dwk, dwv)
    tick(4, 5, 2, 3, 0, 1)

    def rear3(i, _):
        write_mask(edges[i], mask)
        stage_c8(i, x, g1, wqkv, resid, sm_c, mask, qkv)
        return 0

    lax.fori_loop(0, images, rear3, 0)
    out_copies.append(pltpu.make_async_copy(x, gin, out_sems.at[1]))
    out_copies[1].start()
    for k in range(15):
        put_small(small, 19 + k, total(sm_c[k]))
    for p in range(3):
        put_small(small, 34 + p, total(smq[:, p * D : (p + 1) * D]))
    put_small(small, 37, srow[...])

    push_all(place, lambda device: small.at[rows(device * 8, 8), :], gathered.at[0, me], push_sems.at[2])
    gathered[0, me] = small[rows(me * 8, 8), :]
    tick(0, 1, 4, 5, 2, 3)
    land_all(gathered.at[0, pl.ds(0, n - 1)], push_sems.at[2])
    gathered[1, me] = lax.fori_loop(0, n, lambda k, carry: carry + gathered[0, k], zeros(8, L))
    push_all(place, lambda device: gathered.at[1, me], gathered.at[1, me], push_sems.at[3])
    for k in range(streams[0].last):
        tick(0, 1, 4, 5, 2, 3)
    land_all(gathered.at[1, pl.ds(0, n - 1)], push_sems.at[3])
    for k in range(16):
        small[8 * k : 8 * k + 8, :] = gathered[1, k]

    weights = [(grads.at[p * D : (p + 1) * D, :], dwqkv_out.at[:, p * D : (p + 1) * D]) for p in range(3)]
    weights.append((dwm, dwm_out))
    weights += [(grads.at[(4 + j) * D : (5 + j) * D, :], dw1_out.at[:, j * D : (j + 1) * D]) for j in range(4)]
    weights.append((dw2, dw2_out))
    for k, (a, b) in enumerate(weights):
        out_copies.append(pltpu.make_async_copy(a, b, out_sems.at[2 + k]))
        out_copies[-1].start()

    def branch_factor(weight, grad, bias, bias_grad, factor):
        return (total(weight.astype(F32) * grad) + bias * bias_grad) / factor

    picked = [get_small(small, k) for k in range(38)]
    picked.append(branch_factor(wm[...], dwm[...], bm[...], picked[19 + 4], fm[...]))
    local = sum(st2[a, b : b + 1, :] * picked[4 + 3 * a + b] for a in range(3) for b in range(3))
    picked.append((local + cb2[...] * picked[3]) / fl[...])
    picked.append(branch_factor(w2[...], dw2[...], bb2[...], picked[2], fp[...]))
    lane = lax.broadcasted_iota(jnp.int32, (1, D), 1)
    by_head = zeros(1, D)
    for h in range(HEADS):
        own = jnp.where((lane >= h * HD) & (lane < (h + 1) * HD), picked[37], 0.0)
        by_head = jnp.where(lane == h, jnp.sum(own, axis=1, keepdims=True) / sharp[h], by_head)
    picked.append(by_head)
    for k, row in enumerate(picked):
        small_out[k : k + 1, :] = row
    for copy in out_copies:
        copy.wait()


SINGLES = (0, 1, 2, 3, 13, 14, 19, 20, 21, 22, 23, 33, 38, 39, 40)


def deliver_kernel(*refs):
    small, outs, stage, sems = refs[6], refs[7:-7], refs[-7:-1], refs[-1]
    loads = [pltpu.make_async_copy(refs[k], stage[k], sems.at[0, k]) for k in range(6)]
    copies = [pltpu.make_async_copy(stage[k], outs[k], sems.at[1, k]) for k in range(6)]
    for load in loads:
        load.start()
    qkv_bias, hidden_bias, sharp_grad, conv1, conv2 = outs[6:11]
    for p in range(3):
        qkv_bias[p * D : (p + 1) * D] = small[34 + p : 35 + p, :].reshape(D)
    for j in range(4):
        hidden_bias[j * D : (j + 1) * D] = small[15 + j : 16 + j, :].reshape(D)
    sharp_grad[...] = small[41:42, :].reshape(D)[0:HEADS]
    for a in range(3):
        for b in range(3):
            conv2[a, b : b + 1, :] = small[4 + 3 * a + b : 5 + 3 * a + b, :]
            conv1[a, b : b + 1, :] = small[24 + 3 * a + b : 25 + 3 * a + b, :]
    for k, out in zip(SINGLES, outs[11:]):
        out[...] = small[k : k + 1, :].reshape(D)
    for load, copy in zip(loads, copies):
        load.wait()
        copy.start()
    for copy in copies:
        copy.wait()


def on_device(n, x, sens, edges, g1, b1, wqkv, bqkv, sharp, wm, bm, fm, g2, b2, st1, cb1, bg, bo, st2, cb2, fl, g3, b3,
              w1, bb1, w2, bb2, fp):
    images = x.shape[0]
    S = jax.ShapeDtypeStruct
    V = pltpu.VMEM
    vm = pl.BlockSpec(memory_space=pltpu.VMEM)
    sm = pl.BlockSpec(memory_space=pltpu.SMEM)
    hbm = pl.BlockSpec(memory_space=pl.ANY)
    full = (images, T, D)
    small_rows = max(16 * 8, 8 * n)
    dma = pltpu.SemaphoreType.DMA
    copies = stream_shape(n, stream_steps(n, True), FF)[1]
    lout, gin, dwqkv, dwm, dw1, dw2, small = pl.pallas_call(
        lambda *refs: mega_kernel(n, images, refs),
        in_specs=[sm, sm, hbm, hbm, vm, vm, hbm, hbm, vm, vm] + [vm] * 17,
        out_specs=[hbm] * 6 + [vm],
        out_shape=[S(full, BF16), S(full, BF16), S((D, 3 * D), F32), S((D, D), F32), S((D, FF), F32), S((FF, D), F32),
                   S((48, D), F32)],
        scratch_shapes=[
            V((24, FF), F32), V(full, BF16), V(full, BF16), V((D, FF), BF16), V((FF, D), BF16),
            V(full, BF16), V((images, T, 3 * D), BF16), V(full, BF16),
            V((images, D, D), F32), V((images, 2, 8, D), F32),
            V((images, T, L), F32), V(full, F32), V(full, F32), V(full, F32), V(full, F32),
            V(full, BF16), V((images, 8, D), F32), V((8, D), F32), V((8, D), F32), V((8, D), F32),
            V((T, L), F32), V((D, D), F32), V((D, D), BF16), V((D, D), BF16), V((3, PLANE, L), F32), V((3, PLANE, L), F32),
            V((T, L), F32), V((T, D), BF16), V((T, D), BF16), V((T, FF), BF16), V((T, FF), BF16),
            V((15, 8, D), F32), V((8, FF), F32), V((15, 8, D), F32), V((8, 3 * D), F32), V((1, D), F32),
            V((4 * D + 2 * FF, D), F32), V((sum(stream_rows(n, STREAMS)), D), F32),
            V((small_rows, L), F32), V((2, 8, L), F32), V((2, n, 8, L), F32),
            dma((images + 3,)), dma((11,)), dma((len(STREAMS), 4, copies)),
            pltpu.SemaphoreType.REGULAR((len(STREAMS), 4)), dma((4, 2)),
        ],
        compiler_params=pltpu.CompilerParams(
            collective_id=0, has_side_effects=True, vmem_limit_bytes=64 * 1024 * 1024
        ),
    )(edges, sharp, x, sens, wqkv, wm, w1, w2, st1, st2, g1, b1, bqkv, bm, fm, g2, b2, cb1, bg, bo, cb2, fl, g3, b3, bb1, bb2, fp)

    vector = S((D,), F32)
    stencil_shape = S((3, 3, D), F32)
    (lout, gin, dwqkv, dwm, dw1, dw2, qkv_bias, hidden_bias, sharp_grad, conv1, conv2, *singles) = pl.pallas_call(
        deliver_kernel,
        in_specs=[hbm] * 6 + [vm],
        out_specs=[hbm] * 6 + [vm] * (5 + len(SINGLES)),
        out_shape=[S(v.shape, v.dtype) for v in (lout, gin, dwqkv, dwm, dw1, dw2)]
        + [S((3 * D,), F32), S((FF,), F32), S((HEADS,), F32), stencil_shape, stencil_shape]
        + [vector] * len(SINGLES),
        scratch_shapes=[V(v.shape, v.dtype) for v in (lout, gin, dwqkv, dwm, dw1, dw2)] + [dma((2, 6))],
        compiler_params=pltpu.CompilerParams(vmem_limit_bytes=62 * 1024 * 1024),
    )(lout, gin, dwqkv, dwm, dw1, dw2, small)
    one = dict(zip(SINGLES, singles))
    return (lout, gin, one[19], one[20], dwqkv, qkv_bias, sharp_grad, dwm, one[23], one[38], one[21], one[22], conv1, one[33],
            one[13], one[14], conv2, one[3], one[39], one[0], one[1], dw1, hidden_bias, dw2, one[2], one[40])


def solution(mesh):
    n = mesh.shape["img"]
    split = P("img", None, None)
    return jax.shard_map(
        lambda *args: on_device(n, *args),
        mesh=mesh,
        in_specs=(split, split, P("img")) + (P(),) * 24,
        out_specs=(split, split) + (P(),) * 24,
        check_vma=False,
    )
```

```python
import math

import jax
import jax.numpy as jnp
from jax import lax
from jax.experimental import pallas as pl
from jax.experimental.pallas import tpu as pltpu
from jax.sharding import PartitionSpec as P

EPS_NORM = 1e-06
EPS_BATCH = 1e-05
EPS_UNIT = 1e-06
F32 = jnp.float32
BF16 = jnp.bfloat16
MESH = pl.DeviceIdType.MESH
G = 24
T = G * G
D = 384
FF = 1536
HEADS = 8
HD = 48
L = 128
PITCH = 32
PLANE = (G + 4) * PITCH
RC = T
RM = T
RF = T
FP = 512
ROOT_HALF = 0.7071067811865476
ROOT_TWO_PI = 0.3989422804014327
NT = (((1,), (1,)), ((), ()))
TN = (((0,), (0,)), ((), ()))


def dot(a, b, dims=(((1,), (0,)), ((), ()))):
    return lax.dot_general(a, b, dims, preferred_element_type=F32)


def rows(start, size):
    return pl.ds(pl.multiple_of(start, 8), size)


def wide(v, times=3):
    return jnp.concatenate([v] * times, axis=1)


def fold8(v):
    return jnp.sum(v.reshape(v.shape[0] // 8, 8, v.shape[1]), axis=0)


def total(v):
    return jnp.sum(v, axis=0, keepdims=True)


def zeros(*shape):
    return jnp.zeros(shape, F32)


def lane_mean(v):
    return jnp.mean(v, axis=1, keepdims=True)


def gelu_pair(u):
    phi = 0.5 + 0.5 * lax.erf(u * ROOT_HALF)
    bell = jnp.exp((u * u) * -0.5)
    return u * phi, phi + u * (bell * ROOT_TWO_PI)


def column_of(row):
    return jnp.broadcast_to(row, (L, D)).T


def write_mask(edge, mask):
    row_index = lax.broadcasted_iota(jnp.int32, (G, G, L), 0)
    col_index = lax.broadcasted_iota(jnp.int32, (G, G, L), 1)
    keep = (row_index < edge) & (col_index < edge)
    mask[...] = keep.astype(F32).reshape(T, L)


def write_sharp(sharp_mask, sharp):
    lane = lax.broadcasted_iota(jnp.int32, (HD, D), 1)
    for h in range(HEADS):
        own = (lane >= h * HD) & (lane < (h + 1) * HD)
        sharp_mask[h * HD : (h + 1) * HD, :] = jnp.where(own, sharp[h], 0.0)


def to_plane(plane, r, value):
    count = value.shape[0] // G
    for g in range(count):
        for c in range(3):
            plane[c, rows((r * count + g + 2) * PITCH, G), :] = value[g * G : (g + 1) * G, c * L : (c + 1) * L]


def taps_of(st, cs):
    return [jnp.broadcast_to(st[a, b : b + 1, cs], (G, L)) for a in range(3) for b in range(3)]


def stencil(plane, c, r, taps, count):
    base = r * (count * PITCH)
    outs = [None] * count
    for a in range(count + 2):
        for b in range(3):
            v = plane[c, pl.ds(base + (a + 1) * PITCH - 1 + b, G), :]
            for o in range(count):
                if 0 <= a - o < 3:
                    t = v * taps[(a - o) * 3 + b]
                    outs[o] = t if outs[o] is None else outs[o] + t
    return outs


def stencil_back(plane, c, r, taps, vs, kernel):
    count = len(vs)
    base = r * (count * PITCH)
    outs = [None] * count
    for a in range(count + 2):
        for b in range(3):
            v = plane[c, pl.ds(base + (a + 1) * PITCH - 1 + b, G), :]
            for o in range(count):
                if 0 <= a - o < 3:
                    k = (2 - (a - o)) * 3 + (2 - b)
                    t = v * taps[k]
                    outs[o] = t if outs[o] is None else outs[o] + t
                    kernel[k] = kernel[k] + fold8(v * vs[o])
    return outs


def chunks(body, init, size):
    if size == T:
        return body(0, pl.ds(0, T), init)
    return lax.fori_loop(0, T // size, lambda r, c: body(r, rows(r * size, size), c), init)


def stage_a1(i, x, g1, b1, n1, mask):
    def body(r, sl, carry):
        xs = x[i, sl, :].astype(F32)
        mean = lane_mean(xs)
        centre = xs - mean
        spread = lax.rsqrt(lane_mean(centre * centre) + EPS_NORM)
        n1[i, sl, :] = ((centre * spread * g1[...] + b1[...]) * wide(mask[sl, :])).astype(BF16)
        return carry

    chunks(body, 0, RC)


def stage_a2(i, wqkv, bqkv, n1, qkv, sqk, mask):
    def body(r, sl, carry):
        sums = list(carry)
        mk = wide(mask[sl, :])
        normed = n1[i, sl, :]
        for p in range(3):
            cols = slice(p * D, (p + 1) * D)
            part = (dot(normed, wqkv[:, cols]) + bqkv[:, cols]) * mk
            if p < 2:
                sums[p] = sums[p] + fold8(part * part)
            qkv[i, sl, cols] = part.astype(BF16)
        return tuple(sums)

    sums = chunks(body, (zeros(8, D), zeros(8, D)), RM)
    for p in range(2):
        sqk[i, p] = jnp.broadcast_to(lax.rsqrt(total(sums[p]) + EPS_UNIT), (8, D))


def softmax_band(sc, sh):
    ex = jnp.where(sh > 0.0, jnp.exp(sc * sh), 0.0)
    return ex / jnp.sum(ex, axis=1, keepdims=True)


def stage_a3(i, qkv, sqk, score, sharp_mask, pmat):
    sq, sk = sqk[i, 0, 0:1, :], sqk[i, 1, 0:1, :]
    sqcol = column_of(sq)
    raw = dot(qkv[i, :, :D], qkv[i, :, D : 2 * D], TN)
    for h in range(HEADS):
        band = slice(h * HD, (h + 1) * HD)
        sc = raw[band] * wide(sqcol[band]) * sk
        score[i, band, :] = sc
        pmat[band, :] = softmax_band(sc, sharp_mask[band, :]).astype(BF16)


def stage_a4(i, x, wm, bm, fm, g2, b2, qkv, mixed, resid, vh2, r2, mask, plane, pmat):
    def body(r, sl, carry):
        mk = wide(mask[sl, :])
        mx = dot(qkv[i, sl, 2 * D :], pmat[...], NT).astype(BF16)
        mixed[i, sl, :] = mx
        branch = (dot(mx, wm[...]) + bm[...]) * mk
        res = x[i, sl, :].astype(F32) + fm[...] * branch
        resid[i, sl, :] = res
        mean = lane_mean(res)
        centre = res - mean
        spread = lax.rsqrt(lane_mean(centre * centre) + EPS_NORM)
        vhat = centre * spread
        vh2[i, sl, :] = vhat
        r2[i, sl, :] = jnp.broadcast_to(spread, (RM, L))
        to_plane(plane, r, (vhat * g2[...] + b2[...]) * mk)
        return carry

    chunks(body, 0, RM)


def stage_a5(i, st1, cb1, act, slope, stat, mask, plane):
    for c in range(3):
        cs = slice(c * L, (c + 1) * L)
        taps = taps_of(st1, cs)

        def conv_body(r, carry):
            outs = stencil(plane, c, r, taps, 4)
            diffs = []
            for o in range(4):
                sl = rows((r * 4 + o) * G, G)
                value, diff = gelu_pair(outs[o] + cb1[:, cs])
                value = value * mask[sl, :]
                act[i, sl, cs] = value
                diffs.append(diff)
                carry = carry + fold8(value)
            slope[i, pl.ds(pl.multiple_of(r * (4 * G), 32), 4 * G), cs] = jnp.concatenate(diffs, axis=0).astype(BF16)
            return carry

        stat[i, 0:1, cs] = total(lax.fori_loop(0, G // 4, conv_body, zeros(8, L)))


def stage_a6(i, edge, act, stat, mask):
    count = (edge * edge).astype(F32)
    mean = stat[i, 0:1, :] / count

    def body(r, sl, carry):
        dev = (act[i, sl, :] - mean) * wide(mask[sl, :])
        return carry + fold8(dev * dev)

    stat[i, 1:2, :] = total(chunks(body, zeros(8, D), RC))
    stat[i, 2:3, :] = jnp.full((1, D), count, F32)


def merge_stats(parts):
    summed = sum(p[0] for p in parts)
    count = sum(p[2] for p in parts)
    mean = summed / count
    square = sum(p[1] + p[2] * (p[0] / p[2] - mean) * (p[0] / p[2] - mean) for p in parts)
    return summed, square, count


def stage_b1(i, act, stats, bg, bo, mask, plane):
    mean, inv = stats[0:1, :], stats[1:2, :]
    scale = inv * bg[...]
    shift = bo[...] - mean * scale

    def body(r, sl, carry):
        to_plane(plane, r, (act[i, sl, :] * scale + shift) * wide(mask[sl, :]))
        return carry

    chunks(body, 0, RC)


def stage_b2(i, st2, cb2, fl, resid, mask, plane):
    for c in range(3):
        cs = slice(c * L, (c + 1) * L)
        taps = taps_of(st2, cs)

        def conv_body(r, carry):
            outs = stencil(plane, c, r, taps, 4)
            for o in range(4):
                sl = rows((r * 4 + o) * G, G)
                resid[i, sl, cs] = resid[i, sl, cs] + fl[:, cs] * ((outs[o] + cb2[:, cs]) * mask[sl, :])
            return carry

        lax.fori_loop(0, G // 4, conv_body, 0)


def stage_b3(i, sens, g3, b3, fp, resid, sm_b, mask, n3, f2):
    mk = wide(mask[...])
    res = resid[i]
    centre = res - lane_mean(res)
    spread = lax.rsqrt(lane_mean(centre * centre) + EPS_NORM)
    n3[i] = ((centre * spread * g3[...] + b3[...]) * mk).astype(BF16)
    err = sens[i].astype(F32) * mk * fp[...]
    f2[i] = err.astype(BF16)
    sm_b[2] += fold8(err)


def stage_b4(i, part, w1, bb1, w2, smf, n3, f2, hl, e1, branch, back):
    def body(r, sl, hidden_sum):
        normed = n3[i, sl, :]
        low = f2[i, sl, :]
        sums = []
        for j in range(FP // 256):
            cols = slice(j * 256, (j + 1) * 256)
            units = slice(part * FP + j * 256, part * FP + (j + 1) * 256)
            value, diff = gelu_pair(dot(normed, w1[:, units]) + bb1[:, units])
            hl[i, sl, cols] = value.astype(BF16)
            err = dot(low, w2[units, :], NT) * diff
            sums.append(fold8(err))
            e1[i, sl, cols] = err.astype(BF16)
        units = slice(part * FP, (part + 1) * FP)
        forward = dot(hl[i, sl, :], w2[units, :])
        backward = dot(e1[i, sl, :], w1[:, units], NT)
        if part == 0:
            branch[i, sl, :] = forward
            back[i, sl, :] = backward
        else:
            branch[i, sl, :] += forward
            back[i, sl, :] += backward
        return hidden_sum + jnp.concatenate(sums, axis=1)

    smf[:, part * FP : (part + 1) * FP] += chunks(body, zeros(8, FP), RF)


def stage_b5(i, sens, bb2, fp, g3, fl, resid, sm_b, mask, branch, back):
    mk = wide(mask[...])
    res = resid[i]
    centre = res - lane_mean(res)
    spread = lax.rsqrt(lane_mean(centre * centre) + EPS_NORM)
    vhat = centre * spread
    upstream = sens[i].astype(F32) * mk
    sens[i] = ((res + fp[...] * (branch[i] + bb2[...])) * mk).astype(BF16)
    err = back[i] * mk
    sm_b[1] += fold8(err)
    sm_b[0] += fold8(err * vhat)
    eg = err * g3[...]
    mean1 = lane_mean(eg)
    mean2 = lane_mean(eg * vhat)
    grad = upstream + spread * (eg - mean1 - vhat * mean2)
    resid[i] = grad
    sm_b[3] += fold8(grad * mk) * fl[...]


def stage_b6(out, left, right):
    images, _, width = left.shape
    out[...] = dot(right[...].reshape(images * T, D), left[...].reshape(images * T, width), TN).T


def stage_b8(i, act, stats, bg, bo, fl, st2, resid, bng, sm_b, mask, plane, plane2):
    stage_b1(i, act, stats, bg, bo, mask, plane)

    def local_body(r, sl, carry):
        to_plane(plane2, r, resid[i, sl, :] * wide(mask[sl, :]) * fl[...])
        return carry

    chunks(local_body, 0, RC)
    mean, inv = stats[0:1, :], stats[1:2, :]
    for c in range(3):
        cs = slice(c * L, (c + 1) * L)
        taps = taps_of(st2, cs)

        def back_body(r, carry):
            kernel = list(carry)
            vs = [plane[c, rows((r * 4 + o + 2) * PITCH, G), :] for o in range(4)]
            outs = stencil_back(plane2, c, r, taps, vs, kernel)
            for o in range(4):
                sl = rows((r * 4 + o) * G, G)
                bng[i, sl, cs] = outs[o] * mask[sl, :]
            return tuple(kernel)

        found = lax.fori_loop(0, G // 4, back_body, (zeros(8, L),) * 9)
        for k in range(9):
            sm_b[4 + k, :, cs] += found[k]

    def sum_body(r, sl, carry):
        grad = bng[i, sl, :]
        centred = (act[i, sl, :] - mean) * inv
        return carry[0] + fold8(grad * centred), carry[1] + fold8(grad)

    sums = chunks(sum_body, (zeros(8, D),) * 2, RC)
    sm_b[13] += sums[0]
    sm_b[14] += sums[1]


def stage_c1(i, act, slope, bng, stats, bsums, bg, sm_c, mask, plane2):
    mean, inv, count = (stats[k : k + 1, :] for k in range(3))
    coef = inv * bg[...]
    by_centred = bsums[0:1, :] / count * inv
    const = bsums[1:2, :] / count - mean * by_centred

    def body(r, sl, carry):
        grad = (bng[i, sl, :] - const - act[i, sl, :] * by_centred) * coef
        err = grad * wide(mask[sl, :]) * slope[i, sl, :].astype(F32)
        to_plane(plane2, r, err)
        return carry + fold8(err)

    sm_c[14] += chunks(body, zeros(8, D), RC)


def stage_c2(i, vh2, g2, b2, st1, sm_c, mask, plane2, back):
    for c in range(3):
        cs = slice(c * L, (c + 1) * L)
        taps = taps_of(st1, cs)

        def back_body(r, carry):
            kernel = list(carry)
            sls = [rows((r * 4 + o) * G, G) for o in range(4)]
            vs = [(vh2[i, sl, cs] * g2[:, cs] + b2[:, cs]) * mask[sl, :] for sl in sls]
            outs = stencil_back(plane2, c, r, taps, vs, kernel)
            for o in range(4):
                back[sls[o], cs] = outs[o] * mask[sls[o], :]
            return tuple(kernel)

        found = lax.fori_loop(0, G // 4, back_body, (zeros(8, L),) * 9)
        for k in range(9):
            sm_c[5 + k, :, cs] += found[k]


def stage_c3(i, resid, vh2, r2, fm, g2, sm_c, mask, back, plow):
    def body(r, sl, carry):
        gain_sum, shift_sum, bias_sum = carry
        mk = wide(mask[sl, :])
        err = back[sl, :]
        vhat = vh2[i, sl, :]
        shift_sum = shift_sum + fold8(err)
        gain_sum = gain_sum + fold8(err * vhat)
        eg = err * g2[...]
        mean1 = lane_mean(eg)
        mean2 = lane_mean(eg * vhat)
        grad = resid[i, sl, :] + wide(r2[i, sl, :]) * (eg - mean1 - vhat * mean2)
        resid[i, sl, :] = grad
        err = grad * mk * fm[...]
        bias_sum = bias_sum + fold8(err)
        plow[i, sl, :] = err.astype(BF16)
        return gain_sum, shift_sum, bias_sum

    sums = chunks(body, (zeros(8, D),) * 3, RC)
    for k in range(3):
        sm_c[2 + k] += sums[k]


def stage_c4(mixed, dwm, plow):
    images = mixed.shape[0]
    dwm[...] = dot(mixed[...].reshape(images * T, D), plow[...].reshape(images * T, D), TN)


def stage_c5a(i, wm, qkv, score, smq, sharp_mask, plow, pmat, attn_grad):
    mixed_grad = dot(plow[i], wm[...], NT).astype(BF16)
    for h in range(HEADS):
        band = slice(h * HD, (h + 1) * HD)
        pmat[band, :] = softmax_band(score[i, band, :], sharp_mask[band, :]).astype(BF16)
    raw = dot(mixed_grad, qkv[i, :, 2 * D :], TN)
    for h in range(HEADS):
        band = slice(h * HD, (h + 1) * HD)
        attn_grad[i, band, :] = jnp.where(sharp_mask[band, :] > 0.0, raw[band], 0.0)
    value_grad = dot(mixed_grad, pmat[...])
    smq[:, 2 * D :] += fold8(value_grad)
    qkv[i, :, 2 * D :] = value_grad.astype(BF16)


def stage_c5b(i, score, sqk, srow, sharp_mask, attn_grad, alow, cqk):
    sq, sk = sqk[i, 0, 0:1, :], sqk[i, 1, 0:1, :]
    sqcol = column_of(sq)
    colsum = zeros(8, D)
    rowsums = []
    for h in range(HEADS):
        band = slice(h * HD, (h + 1) * HD)
        sc = score[i, band, :]
        sh = sharp_mask[band, :]
        pr = softmax_band(sc, sh)
        weighted = attn_grad[i, band, :] * pr
        logit = weighted - pr * jnp.sum(weighted, axis=1, keepdims=True)
        lg = logit * sh
        cross = lg * sc
        rowsums.append(jnp.sum(cross, axis=1, keepdims=True))
        colsum = colsum + fold8(cross)
        alow[band, :] = (lg * wide(sqcol[band]) * sk).astype(BF16)
    rowcol = jnp.concatenate(rowsums, axis=0)
    rowrow = jnp.broadcast_to(rowcol, (D, L)).T[0:1, :]
    srow[...] += rowrow
    cqk[0:1, :] = sq * sq * rowrow
    cqk[1:2, :] = sk * sk * total(colsum)


def stage_c6(i, qkv, smq, pmat, alow, cqk):
    cq, ck = cqk[0:1, :], cqk[1:2, :]
    qv, kv = qkv[i, :, :D], qkv[i, :, D : 2 * D]
    grads = (dot(kv, alow[...], NT) - qv.astype(F32) * cq, dot(qv, alow[...]) - kv.astype(F32) * ck)
    for p in range(2):
        cols = slice(p * D, (p + 1) * D)
        smq[:, cols] += fold8(grads[p])
        qkv[i, :, cols] = grads[p].astype(BF16)


def stage_c7(part, n1, qkv, out):
    images = n1.shape[0]
    left = n1[...].reshape(images * T, D)
    out[...] = dot(left, qkv[:, :, part * D : (part + 1) * D].reshape(images * T, D), TN)


def stage_c8(i, x, g1, wqkv, resid, sm_c, mask, qkv):
    err = dot(qkv[i], wqkv[...], NT) * wide(mask[...])
    xs = x[i].astype(F32)
    centre = xs - lane_mean(xs)
    spread = lax.rsqrt(lane_mean(centre * centre) + EPS_NORM)
    vhat = centre * spread
    sm_c[1] += fold8(err)
    sm_c[0] += fold8(err * vhat)
    eg = err * g1[...]
    mean1 = lane_mean(eg)
    mean2 = lane_mean(eg * vhat)
    x[i] = (resid[i] + spread * (eg - mean1 - vhat * mean2)).astype(BF16)


def geometry(n):
    chips = n // 2
    side = 2 if chips < 64 else 4
    return side, side, chips // (side * side)


class Place:
    def __init__(self, n):
        self.n = n
        self.me = lax.axis_index("img")
        x, y, z = geometry(n)
        self.axes = {}
        stride = 1
        for name, size in (("core", 2), ("x", x), ("y", y), ("z", z)):
            self.axes[name] = (size, stride, lax.rem(self.me // stride, size))
            stride *= size
        self.axes["plane"] = (x * y, 2, lax.rem(self.me // 2, x * y))

    def other(self, k):
        return lax.rem(self.me + k, self.n)


def stream_steps(n, first):
    if n == 32:
        order = ("plane", "z") if first else ("z", "plane")
        return [("core", True), (order[0], True), (order[1], True)]
    order = ("x", "z") if first else ("z", "x")
    return [("core", True), (order[0], True), (order[1], True), ("y", False)]


STREAMS = ((512, True), (512, False), (512, True), (512, True), (512, True), (512, True), (512, False), (512, True), (512, True))
TAIL, PART0, PART1, PART2 = (0, 1, 2), (3, 4), (5, 6), (7, 8)


def stream_shape(n, steps, size):
    x, y, z = geometry(n)
    axes = {"core": 2, "x": x, "y": y, "z": z, "plane": x * y}
    received, copies, length = 0, 0, size
    for axis, split in steps:
        s = axes[axis]
        piece = length // s if split else length
        received += (s - 1) * piece
        copies += s - 1
        length = piece
    return received, copies


PLAN = {
    "part0": (PART0,),
    "mlp1": {2: (PART0,)},
    "part1": (PART1,),
    "mlp2": {2: (PART1,), 3: (PART0,)},
    "part2": (PART2,),
    "conv_back": {1: (PART2,), 2: (PART1,), 3: (PART0,)},
    "exchange": (PART0, PART1, PART2,),
    "rear1": {},
    "rear2": {0: (PART2,), 1: (PART0,), 2: (PART1,)},
    "value": (PART0, PART2,),
    "rear3": {},
    "query": (TAIL, PART1,),
    "rear4": {0: (PART2,), 2: (TAIL,), 3: (PART1,)},
    "small": (PART2,),
    "end": (PART0, PART1, PART2, TAIL),
}


class Stream:
    def __init__(self, place, steps, buf, start, size, recv, sems, credits):
        self.place, self.buf, self.recv, self.sems, self.credits = place, buf, recv, sems, credits
        off, length, slot, sem = start, size, 0, 0
        self.down = []
        for axis, split in steps:
            s, stride, k = place.axes[axis]
            piece = length // s if split else length
            self.down.append((axis, split, off, piece, slot, sem))
            slot += (s - 1) * piece
            sem += s - 1
            if split:
                off = off + k * piece
            length = piece
        self.done = 0
        self.last = 2 * len(steps)

    def peers(self, axis):
        s, stride, k = self.place.axes[axis]
        for j in range(1, s):
            p = lax.rem(k + j, s)
            yield j, p, self.place.me + (p - k) * stride

    def copies(self, step, gather):
        axis, split, off, piece, slot, sem = self.down[step]
        s, stride, k = self.place.axes[axis]
        side = 2 if gather else 0
        for j, p, device in self.peers(axis):
            if gather:
                src = dst = self.buf.at[rows(off + k * piece, piece), :]
            else:
                src = self.buf.at[rows(off + p * piece if split else off, piece), :]
                dst = self.recv.at[pl.ds(slot + (j - 1) * piece, piece), :]
            yield pltpu.make_async_remote_copy(
                src_ref=src,
                dst_ref=dst,
                send_sem=self.sems.at[side, sem + j - 1],
                recv_sem=self.sems.at[side + 1, sem + j - 1],
                device_id=(device,),
                device_id_type=MESH,
            )

    def finish_sum(self, step):
        axis, split, off, piece, slot, sem = self.down[step]
        s, stride, k = self.place.axes[axis]
        for copy in self.copies(step, False):
            copy.wait()
        if split:
            for j, p, device in self.peers(axis):
                pl.semaphore_signal(self.credits.at[step], inc=1, device_id=(device,), device_id_type=MESH)
            own = off + k * piece
            size = next(s_ for s_ in (128, 96, 64, 32, 24, 16, 8) if piece % s_ == 0)

            def add(r, _):
                sl = rows(own + r * size, size)
                summed = self.buf[sl, :]
                for j in range(1, s):
                    summed = summed + self.recv[rows(slot + (j - 1) * piece + r * size, size), :]
                self.buf[sl, :] = summed
                return 0

            if piece == size:
                add(0, 0)
            else:
                lax.fori_loop(0, piece // size, add, 0)
        else:
            sl = rows(off, piece)
            own = self.buf[sl, :]
            summed = None
            for q in range(s):
                j = lax.rem(k - q + s, s)
                at = slot + jnp.maximum(j - 1, 0) * piece
                term = jnp.where(k == q, own, self.recv[rows(at, piece), :])
                summed = term if summed is None else summed + term
            self.buf[sl, :] = summed

    def advance(self, k):
        count = self.last // 2
        if 0 < k <= count:
            self.finish_sum(k - 1)
        elif count < k <= self.last and self.down[self.last - k][1]:
            for copy in self.copies(self.last - k, True):
                copy.wait()
        if k < count:
            for copy in self.copies(k, False):
                copy.start()
        elif k < self.last and self.down[self.last - 1 - k][1]:
            step = self.last - 1 - k
            pl.semaphore_wait(self.credits.at[step], self.place.axes[self.down[step][0]][0] - 1)
            for copy in self.copies(step, True):
                copy.start()


def stream_rows(n):
    return [stream_shape(n, stream_steps(n, first), size)[0] for size, first in STREAMS]


def push_all(place, source, target, sems):
    def start(k, _):
        device = place.other(k)
        pltpu.make_async_remote_copy(
            src_ref=source(device),
            dst_ref=target,
            send_sem=sems.at[0],
            recv_sem=sems.at[1],
            device_id=(device,),
            device_id_type=MESH,
        ).start()
        return 0

    lax.fori_loop(1, place.n, start, 0)


def land_all(most, sems):
    for k in range(2):
        pltpu.make_async_copy(most, most, sems.at[k]).wait()


def put_small(small, k, row):
    for c in range(3):
        small[3 * k + c : 3 * k + c + 1, :] = row[:, c * L : (c + 1) * L]


def get_small(small, k):
    return jnp.concatenate([small[3 * k + c : 3 * k + c + 1, :] for c in range(3)], axis=1)


def mega_kernel(n, images, refs):
    (edges, sharp, x_in, sens_in, wqkv_in, wm_in, w1_in, w2_in, st1_in, st2_in,
     g1_in, b1_in, bqkv_in, bm_in, fm_in, g2_in, b2_in, cb1_in, bg_in, bo_in, cb2_in, fl_in, g3_in, b3_in, bb1_in, bb2_in, fp_in,
     lout, gin, dwqkv_out, dwm_out, dw1_out, dw2_out, small_out, n1_away, mixed_away, vh2_away,
     vecs, x, sens, wqkv, wm, w1, w2, st1, st2, n1, qkv, mixed, score, sqk, r2, resid, vh2, act, vh3, slope, stat, stats, bsums, cqk,
     mask, sharp_mask, pmat, alow, plane, plane2, hl, e1,
     sm_b, smf, sm_c, smq, srow, grads, recv, small, payload, gathered,
     in_sems, out_sems, away_sems, group_sems, credits, push_sems) = refs
    place = Place(n)
    me = place.me
    barrier = pltpu.get_barrier_semaphore()

    def greet(k, _):
        pl.semaphore_signal(barrier, inc=1, device_id=(place.other(k),), device_id_type=MESH)
        return 0

    vectors = (("g1", g1_in), ("b1", b1_in), ("bm", bm_in), ("fm", fm_in), ("g2", g2_in), ("b2", b2_in), ("cb1", cb1_in),
               ("bg", bg_in), ("bo", bo_in), ("cb2", cb2_in), ("fl", fl_in), ("g3", g3_in), ("b3", b3_in), ("bb2", bb2_in),
               ("fp", fp_in), ("bqkv", bqkv_in), ("bb1", bb1_in))
    pairs = [(ref, vecs.at[k, pl.ds(0, ref.shape[0])]) for k, (name, ref) in enumerate(vectors)]
    pairs += [(wqkv_in, wqkv), (wm_in, wm), (st1_in, st1), (st2_in, st2)]
    pairs += [(x_in.at[k], x.at[k]) for k in range(images)]
    early = len(pairs)
    pairs += [(w1_in, w1), (w2_in, w2), (sens_in, sens)]
    in_copies = [pltpu.make_async_copy(a, b, in_sems.at[k]) for k, (a, b) in enumerate(pairs)]
    for copy in in_copies:
        copy.start()
    lax.fori_loop(1, n, greet, 0)
    (g1, b1, bm, fm, g2, b2, cb1, bg, bo, cb2, fl, g3, b3, bb2, fp, bqkv, bb1) = (
        vecs.at[k : k + 1, 0 : ref.shape[0]] for k, (name, ref) in enumerate(vectors)
    )

    write_sharp(sharp_mask, sharp)
    for ref in (plane, plane2, sm_b, smf, sm_c, smq, srow, small):
        ref[...] = jnp.zeros_like(ref)
    dwq, dwk, dwv, dwm = (grads.at[k * D : (k + 1) * D, :] for k in range(4))
    back = grads.at[0:T, :]
    starts = [4 * D + part * 2 * FP for part in range(FF // FP)]
    first = [grads.at[at : at + FP, :] for at in starts]
    second = [grads.at[at + FP : at + 2 * FP, :] for at in starts]
    n3, f2, branch, rear = n1, mixed, vh2, vh3
    away = [(n1, n1_away), (mixed, mixed_away), (vh2, vh2_away)]

    for copy in in_copies[:early]:
        copy.wait()

    def front(i, _):
        edge = edges[i]
        write_mask(edge, mask)
        stage_a1(i, x, g1, b1, n1, mask)
        stage_a2(i, wqkv, bqkv, n1, qkv, sqk, mask)
        stage_a3(i, qkv, sqk, score, sharp_mask, pmat)
        stage_a4(i, x, wm, bm, fm, g2, b2, qkv, mixed, resid, vh2, r2, mask, plane, pmat)
        stage_a5(i, st1, cb1, act, slope, stat, mask, plane)
        stage_a6(i, edge, act, stat, mask)
        for k, (a, b) in enumerate(away):
            pltpu.make_async_copy(a.at[i], b.at[i], away_sems.at[k]).start()
        return 0

    lax.fori_loop(0, images, front, 0)

    merged = merge_stats([tuple(stat[i, k : k + 1, :] for k in range(3)) for i in range(images)])
    for k in range(2):
        put_small(payload.at[0], k, merged[k])
    payload[0, 6:7, :] = merged[2][:, 0:L]
    pl.semaphore_wait(barrier, n - 1)
    push_all(place, lambda device: payload.at[0], gathered.at[0, me], push_sems.at[0])
    gathered[0, me] = payload[0]
    for copy in in_copies[early:]:
        copy.wait()
    land_all(gathered.at[0, pl.ds(0, n - 1)], push_sems.at[0])

    parts = gathered[0]
    summed = jnp.sum(parts, axis=0)
    count = summed[6:7, :]
    average = summed / count
    own = jnp.broadcast_to(parts[:, 6:7, :], parts.shape)
    gap = parts / own - average
    square = summed[3:6, :] + jnp.sum(own * gap * gap, axis=0)[0:3, :]
    mean = average[0:3, :]
    inv = lax.rsqrt(square / count + EPS_BATCH)
    for c in range(3):
        stats[0:1, c * L : (c + 1) * L] = mean[c : c + 1, :]
        stats[1:2, c * L : (c + 1) * L] = inv[c : c + 1, :]
        stats[2:3, c * L : (c + 1) * L] = count

    streams = []
    at, start = 0, 0
    for k, ((size, x_first), received) in enumerate(zip(STREAMS, stream_rows(n))):
        piece = recv.at[pl.ds(at, received), :]
        steps = stream_steps(n, x_first)
        streams.append(Stream(place, steps, grads, start, size, piece, group_sems.at[k], credits.at[k]))
        at, start = at + received, start + size

    def book(sets):
        moves = []
        for which in sets:
            for k in which:
                if streams[k].done <= streams[k].last:
                    moves.append((k, streams[k].done))
                    streams[k].done += 1
        return moves

    def move(moves):
        for k, step in moves:
            streams[k].advance(step)

    def tick(*sets):
        move(book(sets))

    def image_loop(body, plan):
        booked = {k: book(sets) for k, sets in sorted(plan.items())}

        def step(i, _):
            body(i)
            for k, moves in booked.items():

                @pl.when(i == k)
                def _():
                    move(moves)

            return 0

        lax.fori_loop(0, images, step, 0)

    for k, (a, b) in enumerate(away):
        pltpu.make_async_copy(a, b, away_sems.at[k]).wait()

    def middle(i):
        write_mask(edges[i], mask)
        stage_b1(i, act, stats, bg, bo, mask, plane)
        stage_b2(i, st2, cb2, fl, resid, mask, plane)
        stage_b3(i, sens, g3, b3, fp, resid, sm_b, mask, n3, f2)

    image_loop(middle, {})
    for part in range(FF // FP):

        def feed(i):
            stage_b4(i, part, w1, bb1, w2, smf, n3, f2, hl, e1, branch, rear)

        image_loop(feed, PLAN[f"mlp{part}"] if part else {})
        stage_b6(second[part], hl, f2)
        stage_b6(first[part], e1, n3)
        tick(*(PLAN[f"part{part}"] if part else (PART0,)))
    home = [pltpu.make_async_copy(b, a, away_sems.at[k]) for k, (a, b) in enumerate(away)]
    for copy in home[:2]:
        copy.start()

    def conv_back(i):
        write_mask(edges[i], mask)
        stage_b5(i, sens, bb2, fp, g3, fl, resid, sm_b, mask, branch, rear)
        stage_b8(i, act, stats, bg, bo, fl, st2, resid, vh3, sm_b, mask, plane, plane2)

    image_loop(conv_back, PLAN["conv_back"])
    home[2].start()
    out_copies = [pltpu.make_async_copy(sens, lout, out_sems.at[0])]
    out_copies[0].start()
    for k in range(15):
        put_small(small, k, total(sm_b[k]))
    for j in range(4):
        put_small(small, 15 + j, total(smf[:, j * D : (j + 1) * D]))
    for k in range(2):
        put_small(payload.at[1], k, total(sm_b[13 + k]))
    payload[1, 6:8, :] = zeros(2, L)
    push_all(place, lambda device: payload.at[1], gathered.at[1, me], push_sems.at[1])
    gathered[1, me] = payload[1]
    land_all(gathered.at[1, pl.ds(0, n - 1)], push_sems.at[1])
    tick(*PLAN["exchange"])
    for copy in home:
        copy.wait()
    summed = jnp.sum(gathered[1], axis=0)
    for k in range(2):
        bsums[k : k + 1, :] = jnp.concatenate([summed[3 * k + c : 3 * k + c + 1] for c in range(3)], axis=1)

    def rear1(i):
        write_mask(edges[i], mask)
        stage_c1(i, act, slope, vh3, stats, bsums, bg, sm_c, mask, plane2)
        stage_c2(i, vh2, g2, b2, st1, sm_c, mask, plane2, back)
        stage_c3(i, resid, vh2, r2, fm, g2, sm_c, mask, back, slope)

    image_loop(rear1, PLAN["rear1"])

    def rear2(i):
        stage_c5a(i, wm, qkv, score, smq, sharp_mask, slope, pmat, vh3)

    image_loop(rear2, PLAN["rear2"])
    stage_c4(mixed, dwm, slope)
    stage_c7(2, n1, qkv, dwv)
    tick(*PLAN["value"])

    def rear3(i):
        stage_c5b(i, score, sqk, srow, sharp_mask, vh3, alow, cqk)
        stage_c6(i, qkv, smq, pmat, alow, cqk)

    image_loop(rear3, PLAN["rear3"])
    stage_c7(0, n1, qkv, dwq)
    stage_c7(1, n1, qkv, dwk)
    tick(*PLAN["query"])

    def rear4(i):
        write_mask(edges[i], mask)
        stage_c8(i, x, g1, wqkv, resid, sm_c, mask, qkv)

    image_loop(rear4, PLAN["rear4"])
    out_copies.append(pltpu.make_async_copy(x, gin, out_sems.at[1]))
    out_copies[1].start()
    for k in range(15):
        put_small(small, 19 + k, total(sm_c[k]))
    for p in range(3):
        put_small(small, 34 + p, total(smq[:, p * D : (p + 1) * D]))
    put_small(small, 37, srow[...])

    weights = [(grads.at[p * D : (p + 1) * D, :], dwqkv_out.at[:, p * D : (p + 1) * D]) for p in range(3)]
    weights.append((dwm, dwm_out))
    weights += [(act.at[j, 0:D, :], dw1_out.at[:, j * D : (j + 1) * D]) for j in range(4)]
    weights += [(second[part], dw2_out.at[part * FP : (part + 1) * FP, :]) for part in range(FF // FP)]
    weights = [pltpu.make_async_copy(a, b, out_sems.at[2 + k]) for k, (a, b) in enumerate(weights)]
    out_copies += weights
    later_weights = weights[:4]

    def complete(which):
        return all(streams[k].done > streams[k].last for k in which)

    push_all(place, lambda device: small.at[rows(device * 8, 8), :], gathered.at[0, me], push_sems.at[2])
    gathered[0, me] = small[rows(me * 8, 8), :]
    tick(*PLAN["small"])
    fed = False
    rounds = 0
    while not complete(range(len(streams))):
        if not fed and complete(PART0 + PART1 + PART2):
            fed = True
            for u in range(FF // L):
                block, col = divmod(u * L, D)
                part, row = divmod(u * L, FP)
                act[block, 0:D, col : col + L] = first[part][row : row + L, :].T
            for copy in weights[4:]:
                copy.start()
        tick(*PLAN["end"])
        rounds += 1
        if rounds == 3:
            land_all(gathered.at[0, pl.ds(0, n - 1)], push_sems.at[2])
            gathered[1, me] = jnp.sum(gathered[0], axis=0)
            push_all(place, lambda device: gathered.at[1, me], gathered.at[1, me], push_sems.at[3])
    for copy in later_weights:
        copy.start()
    land_all(gathered.at[1, pl.ds(0, n - 1)], push_sems.at[3])
    for k in range(16):
        small[8 * k : 8 * k + 8, :] = gathered[1, k]

    def branch_factor(weight, grad, bias, bias_grad, factor):
        return (total(weight.astype(F32) * grad) + bias * bias_grad) / factor

    picked = [get_small(small, k) for k in range(38)]
    picked.append(branch_factor(wm[...], dwm[...], bm[...], picked[19 + 4], fm[...]))
    local = sum(st2[a, b : b + 1, :] * picked[4 + 3 * a + b] for a in range(3) for b in range(3))
    picked.append((local + cb2[...] * picked[3]) / fl[...])
    mlp = sum(total(w2[part * FP : (part + 1) * FP, :].astype(F32) * second[part][...]) for part in range(FF // FP))
    picked.append((mlp + bb2[...] * picked[2]) / fp[...])
    lane = lax.broadcasted_iota(jnp.int32, (1, D), 1)
    by_head = zeros(1, D)
    for h in range(HEADS):
        own = jnp.where((lane >= h * HD) & (lane < (h + 1) * HD), picked[37], 0.0)
        by_head = jnp.where(lane == h, jnp.sum(own, axis=1, keepdims=True) / sharp[h], by_head)
    picked.append(by_head)
    for k, row in enumerate(picked):
        small_out[k : k + 1, :] = row
    for copy in out_copies:
        copy.wait()


SINGLES = (0, 1, 2, 3, 13, 14, 19, 20, 21, 22, 23, 33, 38, 39, 40)


def deliver_kernel(*refs):
    small, outs, stage, sems = refs[6], refs[7:-7], refs[-7:-1], refs[-1]
    parts = []
    for k in range(6):
        parts.append((k, pl.ds(0, refs[k].shape[0])))
    loads = [pltpu.make_async_copy(refs[k].at[at], stage[k].at[at], sems.at[0, q]) for q, (k, at) in enumerate(parts)]
    for load in loads:
        load.start()
    sharp_grad, conv1, conv2, qkv_bias, hidden_bias = outs[6:11]
    sharp_grad[...] = small[41:42, :].reshape(D)[0:HEADS]
    for a in range(3):
        for b in range(3):
            conv2[a, b : b + 1, :] = small[4 + 3 * a + b : 5 + 3 * a + b, :]
            conv1[a, b : b + 1, :] = small[24 + 3 * a + b : 25 + 3 * a + b, :]
    pairs = [(small.at[34 + p], qkv_bias.at[pl.ds(p * D, D)]) for p in range(3)]
    pairs += [(small.at[15 + j], hidden_bias.at[pl.ds(j * D, D)]) for j in range(FF // D)]
    pairs += [(small.at[k], out) for k, out in zip(SINGLES, outs[11:])]
    copies = [pltpu.make_async_copy(a, b, sems.at[1, len(parts) + k]) for k, (a, b) in enumerate(pairs)]
    for copy in copies:
        copy.start()
    for q, (k, at) in enumerate(parts):
        loads[q].wait()
        copies.append(pltpu.make_async_copy(stage[k].at[at], outs[k].at[at], sems.at[1, q]))
        copies[-1].start()
    for copy in copies:
        copy.wait()


def on_device(n, x, sens, edges, g1, b1, wqkv, bqkv, sharp, wm, bm, fm, g2, b2, st1, cb1, bg, bo, st2, cb2, fl, g3, b3,
              w1, bb1, w2, bb2, fp):
    images = x.shape[0]
    S = jax.ShapeDtypeStruct
    V = pltpu.VMEM
    vm = pl.BlockSpec(memory_space=pltpu.VMEM)
    sm = pl.BlockSpec(memory_space=pltpu.SMEM)
    hbm = pl.BlockSpec(memory_space=pl.ANY)
    full = (images, T, D)
    dma = pltpu.SemaphoreType.DMA
    copies = stream_shape(n, stream_steps(n, True), FF)[1]
    lout, gin, dwqkv, dwm, dw1, dw2, small, *_ = pl.pallas_call(
        lambda *refs: mega_kernel(n, images, refs),
        in_specs=[sm, sm] + [hbm] * 25,
        out_specs=[hbm] * 6 + [vm] + [hbm] * 3,
        out_shape=[S(full, BF16), S(full, BF16), S((D, 3 * D), F32), S((D, D), F32), S((D, FF), F32), S((FF, D), F32),
                   S((48, D), F32), S(full, BF16), S(full, BF16), S(full, F32)],
        scratch_shapes=[
            V((24, FF), F32), V(full, BF16), V(full, BF16), V((D, 3 * D), BF16), V((D, D), BF16),
            V((D, FF), BF16), V((FF, D), BF16), V((3, 3, D), F32), V((3, 3, D), F32),
            V(full, BF16), V((images, T, 3 * D), BF16), V(full, BF16),
            V((images, D, D), F32), V((images, 2, 8, D), F32),
            V((images, T, L), F32), V(full, F32), V(full, F32), V(full, F32), V(full, F32),
            V(full, BF16), V((images, 8, D), F32), V((8, D), F32), V((8, D), F32), V((8, D), F32),
            V((T, L), F32), V((D, D), F32), V((D, D), BF16), V((D, D), BF16), V((3, PLANE, L), F32), V((3, PLANE, L), F32),
            V((images, T, FP), BF16), V((images, T, FP), BF16),
            V((15, 8, D), F32), V((8, FF), F32), V((15, 8, D), F32), V((8, 3 * D), F32), V((1, D), F32),
            V((4 * D + 2 * FF, D), F32), V((sum(stream_rows(n)), D), F32),
            V((8 * n, L), F32), V((2, 8, L), F32), V((2, n, 8, L), F32),
            dma((images + 24,)), dma((13,)), dma((3,)), dma((len(STREAMS), 4, copies)),
            pltpu.SemaphoreType.REGULAR((len(STREAMS), 4)), dma((4, 2)),
        ],
        compiler_params=pltpu.CompilerParams(
            collective_id=0, has_side_effects=True, vmem_limit_bytes=64 * 1024 * 1024
        ),
    )(edges, sharp, x, sens, wqkv, wm, w1, w2, st1, st2, g1, b1, bqkv, bm, fm, g2, b2, cb1, bg, bo, cb2, fl, g3, b3, bb1, bb2, fp)

    vector = S((D,), F32)
    stencil_shape = S((3, 3, D), F32)
    (lout, gin, dwqkv, dwm, dw1, dw2, sharp_grad, conv1, conv2, qkv_bias, hidden_bias, *singles) = pl.pallas_call(
        deliver_kernel,
        in_specs=[hbm] * 6 + [vm],
        out_specs=[hbm] * 6 + [vm] * 3 + [hbm] * (2 + len(SINGLES)),
        out_shape=[S(v.shape, v.dtype) for v in (lout, gin, dwqkv, dwm, dw1, dw2)]
        + [S((HEADS,), F32), stencil_shape, stencil_shape, S((3 * D,), F32), S((FF,), F32)]
        + [vector] * len(SINGLES),
        scratch_shapes=[V(v.shape, v.dtype) for v in (lout, gin, dwqkv, dwm, dw1, dw2)] + [dma((2, 13 + len(SINGLES)))],
        compiler_params=pltpu.CompilerParams(vmem_limit_bytes=62 * 1024 * 1024),
    )(lout, gin, dwqkv, dwm, dw1, dw2, small)
    one = dict(zip(SINGLES, singles))
    return (lout, gin, one[19], one[20], dwqkv, qkv_bias, sharp_grad, dwm, one[23], one[38], one[21], one[22], conv1, one[33],
            one[13], one[14], conv2, one[3], one[39], one[0], one[1], dw1, hidden_bias, dw2, one[2], one[40])


def solution(mesh):
    n = mesh.shape["img"]
    split = P("img", None, None)
    return jax.shard_map(
        lambda *args: on_device(n, *args),
        mesh=mesh,
        in_specs=(split, split, P("img")) + (P(),) * 24,
        out_specs=(split, split) + (P(),) * 24,
        check_vma=False,
    )
```

```python
import math

import jax
import jax.numpy as jnp
from jax import lax
from jax.experimental import pallas as pl
from jax.experimental.pallas import tpu as pltpu
from jax.sharding import PartitionSpec as P

EPS_NORM = 1e-06
EPS_BATCH = 1e-05
EPS_UNIT = 1e-06
F32 = jnp.float32
BF16 = jnp.bfloat16
MESH = pl.DeviceIdType.MESH
G = 24
T = G * G
D = 384
FF = 1536
HEADS = 8
HD = 48
L = 128
PITCH = 32
PLANE = (G + 4) * PITCH
RC = T
RM = T
RF = T
FP = 512
ROOT_HALF = 0.7071067811865476
ROOT_TWO_PI = 0.3989422804014327
NT = (((1,), (1,)), ((), ()))
TN = (((0,), (0,)), ((), ()))


def dot(a, b, dims=(((1,), (0,)), ((), ()))):
    return lax.dot_general(a, b, dims, preferred_element_type=F32)


def rows(start, size):
    return pl.ds(pl.multiple_of(start, 8), size)


def wide(v, times=3):
    return jnp.concatenate([v] * times, axis=1)


def fold8(v):
    return jnp.sum(v.reshape(v.shape[0] // 8, 8, v.shape[1]), axis=0)


def total(v):
    return jnp.sum(v, axis=0, keepdims=True)


def zeros(*shape):
    return jnp.zeros(shape, F32)


def lane_mean(v):
    return jnp.mean(v, axis=1, keepdims=True)


def gelu_pair(u):
    phi = 0.5 + 0.5 * lax.erf(u * ROOT_HALF)
    bell = jnp.exp((u * u) * -0.5)
    return u * phi, phi + u * (bell * ROOT_TWO_PI)


def column_of(row):
    return jnp.broadcast_to(row, (L, D)).T


def write_mask(edge, mask):
    row_index = lax.broadcasted_iota(jnp.int32, (G, G, L), 0)
    col_index = lax.broadcasted_iota(jnp.int32, (G, G, L), 1)
    keep = (row_index < edge) & (col_index < edge)
    mask[...] = keep.astype(F32).reshape(T, L)


def write_sharp(sharp_mask, sharp):
    lane = lax.broadcasted_iota(jnp.int32, (HD, D), 1)
    for h in range(HEADS):
        own = (lane >= h * HD) & (lane < (h + 1) * HD)
        sharp_mask[h * HD : (h + 1) * HD, :] = jnp.where(own, sharp[h], 0.0)


def to_plane(plane, r, value):
    count = value.shape[0] // G
    for g in range(count):
        for c in range(3):
            plane[c, rows((r * count + g + 2) * PITCH, G), :] = value[g * G : (g + 1) * G, c * L : (c + 1) * L]


def taps_of(st, cs):
    return [jnp.broadcast_to(st[a, b : b + 1, cs], (G, L)) for a in range(3) for b in range(3)]


def stencil(plane, c, r, taps, count):
    base = r * (count * PITCH)
    outs = [None] * count
    for a in range(count + 2):
        for b in range(3):
            v = plane[c, pl.ds(base + (a + 1) * PITCH - 1 + b, G), :]
            for o in range(count):
                if 0 <= a - o < 3:
                    t = v * taps[(a - o) * 3 + b]
                    outs[o] = t if outs[o] is None else outs[o] + t
    return outs


def stencil_back(plane, c, r, taps, vs, kernel):
    count = len(vs)
    base = r * (count * PITCH)
    outs = [None] * count
    for a in range(count + 2):
        for b in range(3):
            v = plane[c, pl.ds(base + (a + 1) * PITCH - 1 + b, G), :]
            for o in range(count):
                if 0 <= a - o < 3:
                    k = (2 - (a - o)) * 3 + (2 - b)
                    t = v * taps[k]
                    outs[o] = t if outs[o] is None else outs[o] + t
                    kernel[k] = kernel[k] + fold8(v * vs[o])
    return outs


def chunks(body, init, size):
    if size == T:
        return body(0, pl.ds(0, T), init)
    return lax.fori_loop(0, T // size, lambda r, c: body(r, rows(r * size, size), c), init)


def stage_a1(i, x, g1, b1, n1, mask):
    def body(r, sl, carry):
        xs = x[i, sl, :].astype(F32)
        mean = lane_mean(xs)
        centre = xs - mean
        spread = lax.rsqrt(lane_mean(centre * centre) + EPS_NORM)
        n1[i, sl, :] = ((centre * spread * g1[...] + b1[...]) * wide(mask[sl, :])).astype(BF16)
        return carry

    chunks(body, 0, RC)


def stage_a2(i, wqkv, bqkv, n1, qkv, sqk, mask):
    def body(r, sl, carry):
        sums = list(carry)
        mk = wide(mask[sl, :])
        normed = n1[i, sl, :]
        for p in range(3):
            cols = slice(p * D, (p + 1) * D)
            part = (dot(normed, wqkv[:, cols]) + bqkv[:, cols]) * mk
            if p < 2:
                sums[p] = sums[p] + fold8(part * part)
            qkv[i, sl, cols] = part.astype(BF16)
        return tuple(sums)

    sums = chunks(body, (zeros(8, D), zeros(8, D)), RM)
    for p in range(2):
        sqk[i, p] = jnp.broadcast_to(lax.rsqrt(total(sums[p]) + EPS_UNIT), (8, D))


def softmax_band(sc, sh):
    ex = jnp.where(sh > 0.0, jnp.exp(sc * sh), 0.0)
    return ex / jnp.sum(ex, axis=1, keepdims=True)


def stage_a3(i, qkv, sqk, score, sharp_mask, pmat):
    sq, sk = sqk[i, 0, 0:1, :], sqk[i, 1, 0:1, :]
    sqcol = column_of(sq)
    raw = dot(qkv[i, :, :D], qkv[i, :, D : 2 * D], TN)
    for h in range(HEADS):
        band = slice(h * HD, (h + 1) * HD)
        sc = raw[band] * wide(sqcol[band]) * sk
        score[i, band, :] = sc
        pmat[band, :] = softmax_band(sc, sharp_mask[band, :]).astype(BF16)


def stage_a4(i, x, wm, bm, fm, g2, b2, qkv, mixed, resid, vh2, r2, mask, plane, pmat):
    def body(r, sl, carry):
        mk = wide(mask[sl, :])
        mx = dot(qkv[i, sl, 2 * D :], pmat[...], NT).astype(BF16)
        mixed[i, sl, :] = mx
        branch = (dot(mx, wm[...]) + bm[...]) * mk
        res = x[i, sl, :].astype(F32) + fm[...] * branch
        resid[i, sl, :] = res
        mean = lane_mean(res)
        centre = res - mean
        spread = lax.rsqrt(lane_mean(centre * centre) + EPS_NORM)
        vhat = centre * spread
        vh2[i, sl, :] = vhat
        r2[i, sl, :] = jnp.broadcast_to(spread, (RM, L))
        to_plane(plane, r, (vhat * g2[...] + b2[...]) * mk)
        return carry

    chunks(body, 0, RM)


def stage_a5(i, st1, cb1, act, slope, stat, mask, plane):
    for c in range(3):
        cs = slice(c * L, (c + 1) * L)
        taps = taps_of(st1, cs)

        def conv_body(r, carry):
            outs = stencil(plane, c, r, taps, 4)
            diffs = []
            for o in range(4):
                sl = rows((r * 4 + o) * G, G)
                value, diff = gelu_pair(outs[o] + cb1[:, cs])
                value = value * mask[sl, :]
                act[i, sl, cs] = value
                diffs.append(diff)
                carry = carry + fold8(value)
            slope[i, pl.ds(pl.multiple_of(r * (4 * G), 32), 4 * G), cs] = jnp.concatenate(diffs, axis=0).astype(BF16)
            return carry

        stat[i, 0:1, cs] = total(lax.fori_loop(0, G // 4, conv_body, zeros(8, L)))


def stage_a6(i, edge, act, stat, mask):
    count = (edge * edge).astype(F32)
    mean = stat[i, 0:1, :] / count

    def body(r, sl, carry):
        dev = (act[i, sl, :] - mean) * wide(mask[sl, :])
        return carry + fold8(dev * dev)

    stat[i, 1:2, :] = total(chunks(body, zeros(8, D), RC))
    stat[i, 2:3, :] = jnp.full((1, D), count, F32)


def merge_stats(parts):
    summed = sum(p[0] for p in parts)
    count = sum(p[2] for p in parts)
    mean = summed / count
    square = sum(p[1] + p[2] * (p[0] / p[2] - mean) * (p[0] / p[2] - mean) for p in parts)
    return summed, square, count


def stage_b1(i, act, stats, bg, bo, mask, plane):
    mean, inv = stats[0:1, :], stats[1:2, :]
    scale = inv * bg[...]
    shift = bo[...] - mean * scale

    def body(r, sl, carry):
        to_plane(plane, r, (act[i, sl, :] * scale + shift) * wide(mask[sl, :]))
        return carry

    chunks(body, 0, RC)


def stage_b2(i, st2, cb2, fl, resid, mask, plane):
    for c in range(3):
        cs = slice(c * L, (c + 1) * L)
        taps = taps_of(st2, cs)

        def conv_body(r, carry):
            outs = stencil(plane, c, r, taps, 4)
            for o in range(4):
                sl = rows((r * 4 + o) * G, G)
                resid[i, sl, cs] = resid[i, sl, cs] + fl[:, cs] * ((outs[o] + cb2[:, cs]) * mask[sl, :])
            return carry

        lax.fori_loop(0, G // 4, conv_body, 0)


def stage_b3(i, sens, g3, b3, fp, resid, sm_b, mask, n3, f2):
    mk = wide(mask[...])
    res = resid[i]
    centre = res - lane_mean(res)
    spread = lax.rsqrt(lane_mean(centre * centre) + EPS_NORM)
    n3[i] = ((centre * spread * g3[...] + b3[...]) * mk).astype(BF16)
    err = sens[i].astype(F32) * mk * fp[...]
    f2[i] = err.astype(BF16)
    sm_b[2] += fold8(err)


def stage_b4(i, part, w1, bb1, w2, smf, n3, f2, hl, e1, branch, back):
    def body(r, sl, hidden_sum):
        normed = n3[i, sl, :]
        low = f2[i, sl, :]
        sums = []
        for j in range(FP // 256):
            cols = slice(j * 256, (j + 1) * 256)
            units = slice(part * FP + j * 256, part * FP + (j + 1) * 256)
            value, diff = gelu_pair(dot(normed, w1[:, units]) + bb1[:, units])
            hl[i, sl, cols] = value.astype(BF16)
            err = dot(low, w2[units, :], NT) * diff
            sums.append(fold8(err))
            e1[i, sl, cols] = err.astype(BF16)
        units = slice(part * FP, (part + 1) * FP)
        forward = dot(hl[i, sl, :], w2[units, :])
        backward = dot(e1[i, sl, :], w1[:, units], NT)
        if part == 0:
            branch[i, sl, :] = forward
            back[i, sl, :] = backward
        else:
            branch[i, sl, :] += forward
            back[i, sl, :] += backward
        return hidden_sum + jnp.concatenate(sums, axis=1)

    smf[:, part * FP : (part + 1) * FP] += chunks(body, zeros(8, FP), RF)


def stage_b5(i, sens, bb2, fp, g3, fl, resid, sm_b, mask, branch, back):
    mk = wide(mask[...])
    res = resid[i]
    centre = res - lane_mean(res)
    spread = lax.rsqrt(lane_mean(centre * centre) + EPS_NORM)
    vhat = centre * spread
    upstream = sens[i].astype(F32) * mk
    sens[i] = ((res + fp[...] * (branch[i] + bb2[...])) * mk).astype(BF16)
    err = back[i] * mk
    sm_b[1] += fold8(err)
    sm_b[0] += fold8(err * vhat)
    eg = err * g3[...]
    mean1 = lane_mean(eg)
    mean2 = lane_mean(eg * vhat)
    grad = upstream + spread * (eg - mean1 - vhat * mean2)
    resid[i] = grad
    sm_b[3] += fold8(grad * mk) * fl[...]


def stage_b6(out, left, right):
    images, _, width = left.shape
    out[...] = dot(right[...].reshape(images * T, D), left[...].reshape(images * T, width), TN).T


def stage_b8(i, act, stats, bg, bo, fl, st2, resid, bng, sm_b, mask, plane, plane2):
    stage_b1(i, act, stats, bg, bo, mask, plane)

    def local_body(r, sl, carry):
        to_plane(plane2, r, resid[i, sl, :] * wide(mask[sl, :]) * fl[...])
        return carry

    chunks(local_body, 0, RC)
    mean, inv = stats[0:1, :], stats[1:2, :]
    for c in range(3):
        cs = slice(c * L, (c + 1) * L)
        taps = taps_of(st2, cs)

        def back_body(r, carry):
            kernel = list(carry)
            vs = [plane[c, rows((r * 4 + o + 2) * PITCH, G), :] for o in range(4)]
            outs = stencil_back(plane2, c, r, taps, vs, kernel)
            for o in range(4):
                sl = rows((r * 4 + o) * G, G)
                bng[i, sl, cs] = outs[o] * mask[sl, :]
            return tuple(kernel)

        found = lax.fori_loop(0, G // 4, back_body, (zeros(8, L),) * 9)
        for k in range(9):
            sm_b[4 + k, :, cs] += found[k]

    def sum_body(r, sl, carry):
        grad = bng[i, sl, :]
        centred = (act[i, sl, :] - mean) * inv
        return carry[0] + fold8(grad * centred), carry[1] + fold8(grad)

    sums = chunks(sum_body, (zeros(8, D),) * 2, RC)
    sm_b[13] += sums[0]
    sm_b[14] += sums[1]


def stage_c1(i, act, slope, bng, stats, bsums, bg, sm_c, mask, plane2):
    mean, inv, count = (stats[k : k + 1, :] for k in range(3))
    coef = inv * bg[...]
    by_centred = bsums[0:1, :] / count * inv
    const = bsums[1:2, :] / count - mean * by_centred

    def body(r, sl, carry):
        grad = (bng[i, sl, :] - const - act[i, sl, :] * by_centred) * coef
        err = grad * wide(mask[sl, :]) * slope[i, sl, :].astype(F32)
        to_plane(plane2, r, err)
        return carry + fold8(err)

    sm_c[14] += chunks(body, zeros(8, D), RC)


def stage_c2(i, vh2, g2, b2, st1, sm_c, mask, plane2, back):
    for c in range(3):
        cs = slice(c * L, (c + 1) * L)
        taps = taps_of(st1, cs)

        def back_body(r, carry):
            kernel = list(carry)
            sls = [rows((r * 4 + o) * G, G) for o in range(4)]
            vs = [(vh2[i, sl, cs] * g2[:, cs] + b2[:, cs]) * mask[sl, :] for sl in sls]
            outs = stencil_back(plane2, c, r, taps, vs, kernel)
            for o in range(4):
                back[sls[o], cs] = outs[o] * mask[sls[o], :]
            return tuple(kernel)

        found = lax.fori_loop(0, G // 4, back_body, (zeros(8, L),) * 9)
        for k in range(9):
            sm_c[5 + k, :, cs] += found[k]


def stage_c3(i, resid, vh2, r2, fm, g2, sm_c, mask, back, plow):
    def body(r, sl, carry):
        gain_sum, shift_sum, bias_sum = carry
        mk = wide(mask[sl, :])
        err = back[sl, :]
        vhat = vh2[i, sl, :]
        shift_sum = shift_sum + fold8(err)
        gain_sum = gain_sum + fold8(err * vhat)
        eg = err * g2[...]
        mean1 = lane_mean(eg)
        mean2 = lane_mean(eg * vhat)
        grad = resid[i, sl, :] + wide(r2[i, sl, :]) * (eg - mean1 - vhat * mean2)
        resid[i, sl, :] = grad
        err = grad * mk * fm[...]
        bias_sum = bias_sum + fold8(err)
        plow[i, sl, :] = err.astype(BF16)
        return gain_sum, shift_sum, bias_sum

    sums = chunks(body, (zeros(8, D),) * 3, RC)
    for k in range(3):
        sm_c[2 + k] += sums[k]


def stage_c4(mixed, dwm, plow):
    images = mixed.shape[0]
    dwm[...] = dot(mixed[...].reshape(images * T, D), plow[...].reshape(images * T, D), TN)


def stage_c5a(i, wm, qkv, score, smq, sharp_mask, plow, pmat, attn_grad):
    mixed_grad = dot(plow[i], wm[...], NT).astype(BF16)
    for h in range(HEADS):
        band = slice(h * HD, (h + 1) * HD)
        pmat[band, :] = softmax_band(score[i, band, :], sharp_mask[band, :]).astype(BF16)
    raw = dot(mixed_grad, qkv[i, :, 2 * D :], TN)
    for h in range(HEADS):
        band = slice(h * HD, (h + 1) * HD)
        attn_grad[i, band, :] = jnp.where(sharp_mask[band, :] > 0.0, raw[band], 0.0)
    value_grad = dot(mixed_grad, pmat[...])
    smq[:, 2 * D :] += fold8(value_grad)
    qkv[i, :, 2 * D :] = value_grad.astype(BF16)


def stage_c5b(i, score, sqk, srow, sharp_mask, attn_grad, alow, cqk):
    sq, sk = sqk[i, 0, 0:1, :], sqk[i, 1, 0:1, :]
    sqcol = column_of(sq)
    colsum = zeros(8, D)
    rowsums = []
    for h in range(HEADS):
        band = slice(h * HD, (h + 1) * HD)
        sc = score[i, band, :]
        sh = sharp_mask[band, :]
        pr = softmax_band(sc, sh)
        weighted = attn_grad[i, band, :] * pr
        logit = weighted - pr * jnp.sum(weighted, axis=1, keepdims=True)
        lg = logit * sh
        cross = lg * sc
        rowsums.append(jnp.sum(cross, axis=1, keepdims=True))
        colsum = colsum + fold8(cross)
        alow[band, :] = (lg * wide(sqcol[band]) * sk).astype(BF16)
    rowcol = jnp.concatenate(rowsums, axis=0)
    rowrow = jnp.broadcast_to(rowcol, (D, L)).T[0:1, :]
    srow[...] += rowrow
    cqk[0:1, :] = sq * sq * rowrow
    cqk[1:2, :] = sk * sk * total(colsum)


def stage_c6(i, qkv, smq, pmat, alow, cqk):
    cq, ck = cqk[0:1, :], cqk[1:2, :]
    qv, kv = qkv[i, :, :D], qkv[i, :, D : 2 * D]
    grads = (dot(kv, alow[...], NT) - qv.astype(F32) * cq, dot(qv, alow[...]) - kv.astype(F32) * ck)
    for p in range(2):
        cols = slice(p * D, (p + 1) * D)
        smq[:, cols] += fold8(grads[p])
        qkv[i, :, cols] = grads[p].astype(BF16)


def stage_c7(part, n1, qkv, out):
    images = n1.shape[0]
    left = n1[...].reshape(images * T, D)
    out[...] = dot(left, qkv[:, :, part * D : (part + 1) * D].reshape(images * T, D), TN)


def stage_c8(i, x, g1, wqkv, resid, sm_c, mask, qkv):
    err = dot(qkv[i], wqkv[...], NT) * wide(mask[...])
    xs = x[i].astype(F32)
    centre = xs - lane_mean(xs)
    spread = lax.rsqrt(lane_mean(centre * centre) + EPS_NORM)
    vhat = centre * spread
    sm_c[1] += fold8(err)
    sm_c[0] += fold8(err * vhat)
    eg = err * g1[...]
    mean1 = lane_mean(eg)
    mean2 = lane_mean(eg * vhat)
    x[i] = (resid[i] + spread * (eg - mean1 - vhat * mean2)).astype(BF16)


def geometry(n):
    chips = n // 2
    side = 2 if chips < 64 else 4
    return side, side, chips // (side * side)


class Place:
    def __init__(self, n):
        self.n = n
        self.me = lax.axis_index("img")
        x, y, z = geometry(n)
        self.axes = {}
        stride = 1
        for name, size in (("core", 2), ("x", x), ("y", y), ("z", z)):
            self.axes[name] = (size, stride, lax.rem(self.me // stride, size))
            stride *= size
        self.axes["plane"] = (x * y, 2, lax.rem(self.me // 2, x * y))

    def other(self, k):
        return lax.rem(self.me + k, self.n)


def stream_steps(n, first):
    if n == 32:
        order = ("plane", "z") if first else ("z", "plane")
        return [("core", True), (order[0], True), (order[1], True)]
    order = ("x", "z") if first else ("z", "x")
    return [("core", True), (order[0], True), (order[1], True), ("y", False)]


STREAMS = ((512, True), (512, False), (512, True), (512, True), (512, True), (512, True), (512, False), (512, True), (512, True))
TAIL, LAST, PART0, PART1, PART2 = (0, 1), (2,), (3, 4), (5, 6), (7, 8)


def stream_shape(n, steps, size):
    x, y, z = geometry(n)
    axes = {"core": 2, "x": x, "y": y, "z": z, "plane": x * y}
    received, copies, length = 0, 0, size
    for axis, split in steps:
        s = axes[axis]
        piece = length // s if split else length
        received += (s - 1) * piece
        copies += s - 1
        length = piece
    return received, copies


PLAN = {
    "part0": (PART0,),
    "mlp1": {2: (PART0,)},
    "part1": (PART1,),
    "mlp2": {2: (PART1,), 3: (PART0,)},
    "part2": (PART2,),
    "conv_back": {1: (PART2,), 2: (PART1,), 3: (PART0,)},
    "exchange": (PART0, PART1, PART2,),
    "rear1": {},
    "rear2": {0: (PART2,), 1: (PART0,), 2: (PART1,)},
    "value": (PART0, PART2, LAST),
    "rear3": {2: (LAST,)},
    "query": (TAIL, PART1,),
    "rear4": {0: (PART2,), 1: (LAST,), 2: (TAIL,), 3: (PART1,)},
    "small": (PART2,),
    "end": (TAIL, LAST, PART0, PART1, PART2),
}


class Stream:
    def __init__(self, place, steps, buf, start, size, recv, sems, credits):
        self.place, self.buf, self.recv, self.sems, self.credits = place, buf, recv, sems, credits
        off, length, slot, sem = start, size, 0, 0
        self.down = []
        for axis, split in steps:
            s, stride, k = place.axes[axis]
            piece = length // s if split else length
            self.down.append((axis, split, off, piece, slot, sem))
            slot += (s - 1) * piece
            sem += s - 1
            if split:
                off = off + k * piece
            length = piece
        self.done = 0
        self.last = 2 * len(steps)

    def peers(self, axis):
        s, stride, k = self.place.axes[axis]
        for j in range(1, s):
            p = lax.rem(k + j, s)
            yield j, p, self.place.me + (p - k) * stride

    def copies(self, step, gather):
        axis, split, off, piece, slot, sem = self.down[step]
        s, stride, k = self.place.axes[axis]
        side = 2 if gather else 0
        for j, p, device in self.peers(axis):
            if gather:
                src = dst = self.buf.at[rows(off + k * piece, piece), :]
            else:
                src = self.buf.at[rows(off + p * piece if split else off, piece), :]
                dst = self.recv.at[pl.ds(slot + (j - 1) * piece, piece), :]
            yield pltpu.make_async_remote_copy(
                src_ref=src,
                dst_ref=dst,
                send_sem=self.sems.at[side, sem + j - 1],
                recv_sem=self.sems.at[side + 1, sem + j - 1],
                device_id=(device,),
                device_id_type=MESH,
            )

    def finish_sum(self, step):
        axis, split, off, piece, slot, sem = self.down[step]
        s, stride, k = self.place.axes[axis]
        for copy in self.copies(step, False):
            copy.wait()
        if split:
            for j, p, device in self.peers(axis):
                pl.semaphore_signal(self.credits.at[step], inc=1, device_id=(device,), device_id_type=MESH)
            own = off + k * piece
            size = next(s_ for s_ in (128, 96, 64, 32, 24, 16, 8) if piece % s_ == 0)

            def add(r, _):
                sl = rows(own + r * size, size)
                summed = self.buf[sl, :]
                for j in range(1, s):
                    summed = summed + self.recv[rows(slot + (j - 1) * piece + r * size, size), :]
                self.buf[sl, :] = summed
                return 0

            if piece == size:
                add(0, 0)
            else:
                lax.fori_loop(0, piece // size, add, 0)
        else:
            sl = rows(off, piece)
            own = self.buf[sl, :]
            summed = None
            for q in range(s):
                j = lax.rem(k - q + s, s)
                at = slot + jnp.maximum(j - 1, 0) * piece
                term = jnp.where(k == q, own, self.recv[rows(at, piece), :])
                summed = term if summed is None else summed + term
            self.buf[sl, :] = summed

    def advance(self, k):
        count = self.last // 2
        if 0 < k <= count:
            self.finish_sum(k - 1)
        elif count < k <= self.last and self.down[self.last - k][1]:
            for copy in self.copies(self.last - k, True):
                copy.wait()
        if k < count:
            for copy in self.copies(k, False):
                copy.start()
        elif k < self.last and self.down[self.last - 1 - k][1]:
            step = self.last - 1 - k
            pl.semaphore_wait(self.credits.at[step], self.place.axes[self.down[step][0]][0] - 1)
            for copy in self.copies(step, True):
                copy.start()


def stream_rows(n):
    return [stream_shape(n, stream_steps(n, first), size)[0] for size, first in STREAMS]


def push_all(place, source, target, sems):
    def start(k, _):
        device = place.other(k)
        pltpu.make_async_remote_copy(
            src_ref=source(device),
            dst_ref=target,
            send_sem=sems.at[0],
            recv_sem=sems.at[1],
            device_id=(device,),
            device_id_type=MESH,
        ).start()
        return 0

    lax.fori_loop(1, place.n, start, 0)


def land_all(most, sems):
    for k in range(2):
        pltpu.make_async_copy(most, most, sems.at[k]).wait()


def put_small(small, k, row):
    for c in range(3):
        small[3 * k + c : 3 * k + c + 1, :] = row[:, c * L : (c + 1) * L]


def get_small(small, k):
    return jnp.concatenate([small[3 * k + c : 3 * k + c + 1, :] for c in range(3)], axis=1)


def mega_kernel(n, images, refs):
    (edges, sharp, x_in, sens_in, wqkv_in, wm_in, w1_in, w2_in, st1_in, st2_in,
     g1_in, b1_in, bqkv_in, bm_in, fm_in, g2_in, b2_in, cb1_in, bg_in, bo_in, cb2_in, fl_in, g3_in, b3_in, bb1_in, bb2_in, fp_in,
     lout, gin, dwqkv_out, dwm_out, dw1_out, dw2_out, small_out, n1_away, mixed_away, vh2_away,
     vecs, x, sens, wqkv, wm, w1, w2, st1, st2, n1, qkv, mixed, score, sqk, r2, resid, vh2, act, vh3, slope, stat, stats, bsums, cqk,
     mask, sharp_mask, pmat, alow, plane, plane2, hl, e1,
     sm_b, smf, sm_c, smq, srow, grads, recv, small, payload, gathered,
     in_sems, out_sems, away_sems, group_sems, credits, push_sems) = refs
    place = Place(n)
    me = place.me
    barrier = pltpu.get_barrier_semaphore()

    def greet(k, _):
        pl.semaphore_signal(barrier, inc=1, device_id=(place.other(k),), device_id_type=MESH)
        return 0

    vectors = (("g1", g1_in), ("b1", b1_in), ("bm", bm_in), ("fm", fm_in), ("g2", g2_in), ("b2", b2_in), ("cb1", cb1_in),
               ("bg", bg_in), ("bo", bo_in), ("cb2", cb2_in), ("fl", fl_in), ("g3", g3_in), ("b3", b3_in), ("bb2", bb2_in),
               ("fp", fp_in), ("bqkv", bqkv_in), ("bb1", bb1_in))
    pairs = [(ref, vecs.at[k, pl.ds(0, ref.shape[0])]) for k, (name, ref) in enumerate(vectors)]
    pairs += [(wqkv_in, wqkv), (wm_in, wm), (st1_in, st1), (st2_in, st2)]
    pairs += [(x_in.at[k], x.at[k]) for k in range(images)]
    early = len(pairs)
    pairs += [(w1_in, w1), (w2_in, w2), (sens_in, sens)]
    in_copies = [pltpu.make_async_copy(a, b, in_sems.at[k]) for k, (a, b) in enumerate(pairs)]
    for copy in in_copies:
        copy.start()
    lax.fori_loop(1, n, greet, 0)
    (g1, b1, bm, fm, g2, b2, cb1, bg, bo, cb2, fl, g3, b3, bb2, fp, bqkv, bb1) = (
        vecs.at[k : k + 1, 0 : ref.shape[0]] for k, (name, ref) in enumerate(vectors)
    )

    write_sharp(sharp_mask, sharp)
    for ref in (plane, plane2, sm_b, smf, sm_c, smq, srow, small):
        ref[...] = jnp.zeros_like(ref)
    dwq, dwk, dwv, dwm = (grads.at[k * D : (k + 1) * D, :] for k in range(4))
    back = grads.at[0:T, :]
    starts = [4 * D + part * 2 * FP for part in range(FF // FP)]
    first = [grads.at[at : at + FP, :] for at in starts]
    second = [grads.at[at + FP : at + 2 * FP, :] for at in starts]
    n3, f2, branch, rear = n1, mixed, vh2, vh3
    away = [(n1, n1_away), (mixed, mixed_away), (vh2, vh2_away)]

    for copy in in_copies[:early]:
        copy.wait()

    def front(i, _):
        edge = edges[i]
        write_mask(edge, mask)
        stage_a1(i, x, g1, b1, n1, mask)
        stage_a2(i, wqkv, bqkv, n1, qkv, sqk, mask)
        stage_a3(i, qkv, sqk, score, sharp_mask, pmat)
        stage_a4(i, x, wm, bm, fm, g2, b2, qkv, mixed, resid, vh2, r2, mask, plane, pmat)
        stage_a5(i, st1, cb1, act, slope, stat, mask, plane)
        stage_a6(i, edge, act, stat, mask)
        for k, (a, b) in enumerate(away):
            pltpu.make_async_copy(a.at[i], b.at[i], away_sems.at[k]).start()
        return 0

    lax.fori_loop(0, images, front, 0)

    merged = merge_stats([tuple(stat[i, k : k + 1, :] for k in range(3)) for i in range(images)])
    for k in range(2):
        put_small(payload.at[0], k, merged[k])
    payload[0, 6:7, :] = merged[2][:, 0:L]
    pl.semaphore_wait(barrier, n - 1)
    push_all(place, lambda device: payload.at[0], gathered.at[0, me], push_sems.at[0])
    gathered[0, me] = payload[0]
    for copy in in_copies[early:]:
        copy.wait()
    land_all(gathered.at[0, pl.ds(0, n - 1)], push_sems.at[0])

    parts = gathered[0]
    summed = jnp.sum(parts, axis=0)
    count = summed[6:7, :]
    average = summed / count
    own = jnp.broadcast_to(parts[:, 6:7, :], parts.shape)
    gap = parts / own - average
    square = summed[3:6, :] + jnp.sum(own * gap * gap, axis=0)[0:3, :]
    mean = average[0:3, :]
    inv = lax.rsqrt(square / count + EPS_BATCH)
    for c in range(3):
        stats[0:1, c * L : (c + 1) * L] = mean[c : c + 1, :]
        stats[1:2, c * L : (c + 1) * L] = inv[c : c + 1, :]
        stats[2:3, c * L : (c + 1) * L] = count

    streams = []
    at, start = 0, 0
    for k, ((size, x_first), received) in enumerate(zip(STREAMS, stream_rows(n))):
        piece = recv.at[pl.ds(at, received), :]
        steps = stream_steps(n, x_first)
        streams.append(Stream(place, steps, grads, start, size, piece, group_sems.at[k], credits.at[k]))
        at, start = at + received, start + size

    def book(sets):
        moves = []
        for which in sets:
            for k in which:
                if streams[k].done <= streams[k].last:
                    moves.append((k, streams[k].done))
                    streams[k].done += 1
        return moves

    def move(moves):
        for k, step in moves:
            streams[k].advance(step)

    def tick(*sets):
        move(book(sets))

    def image_loop(body, plan):
        booked = {k: book(sets) for k, sets in sorted(plan.items())}

        def step(i, _):
            body(i)
            for k, moves in booked.items():

                @pl.when(i == k)
                def _():
                    move(moves)

            return 0

        lax.fori_loop(0, images, step, 0)

    for k, (a, b) in enumerate(away):
        pltpu.make_async_copy(a, b, away_sems.at[k]).wait()

    def middle(i):
        write_mask(edges[i], mask)
        stage_b1(i, act, stats, bg, bo, mask, plane)
        stage_b2(i, st2, cb2, fl, resid, mask, plane)
        stage_b3(i, sens, g3, b3, fp, resid, sm_b, mask, n3, f2)

    image_loop(middle, {})
    for part in range(FF // FP):

        def feed(i):
            stage_b4(i, part, w1, bb1, w2, smf, n3, f2, hl, e1, branch, rear)

        image_loop(feed, PLAN[f"mlp{part}"] if part else {})
        stage_b6(second[part], hl, f2)
        stage_b6(first[part], e1, n3)
        tick(*(PLAN[f"part{part}"] if part else (PART0,)))
    home = [pltpu.make_async_copy(b, a, away_sems.at[k]) for k, (a, b) in enumerate(away)]
    for copy in home[:2]:
        copy.start()

    def conv_back(i):
        write_mask(edges[i], mask)
        stage_b5(i, sens, bb2, fp, g3, fl, resid, sm_b, mask, branch, rear)
        stage_b8(i, act, stats, bg, bo, fl, st2, resid, vh3, sm_b, mask, plane, plane2)

    image_loop(conv_back, PLAN["conv_back"])
    home[2].start()
    out_copies = [pltpu.make_async_copy(sens, lout, out_sems.at[0])]
    out_copies[0].start()
    for k in range(15):
        put_small(small, k, total(sm_b[k]))
    for j in range(4):
        put_small(small, 15 + j, total(smf[:, j * D : (j + 1) * D]))
    for k in range(2):
        put_small(payload.at[1], k, total(sm_b[13 + k]))
    payload[1, 6:8, :] = zeros(2, L)
    push_all(place, lambda device: payload.at[1], gathered.at[1, me], push_sems.at[1])
    gathered[1, me] = payload[1]
    land_all(gathered.at[1, pl.ds(0, n - 1)], push_sems.at[1])
    tick(*PLAN["exchange"])
    for copy in home:
        copy.wait()
    summed = jnp.sum(gathered[1], axis=0)
    for k in range(2):
        bsums[k : k + 1, :] = jnp.concatenate([summed[3 * k + c : 3 * k + c + 1] for c in range(3)], axis=1)

    def rear1(i):
        write_mask(edges[i], mask)
        stage_c1(i, act, slope, vh3, stats, bsums, bg, sm_c, mask, plane2)
        stage_c2(i, vh2, g2, b2, st1, sm_c, mask, plane2, back)
        stage_c3(i, resid, vh2, r2, fm, g2, sm_c, mask, back, slope)

    image_loop(rear1, PLAN["rear1"])

    def rear2(i):
        stage_c5a(i, wm, qkv, score, smq, sharp_mask, slope, pmat, vh3)

    image_loop(rear2, PLAN["rear2"])
    stage_c4(mixed, dwm, slope)
    stage_c7(2, n1, qkv, dwv)
    tick(*PLAN["value"])

    def rear3(i):
        stage_c5b(i, score, sqk, srow, sharp_mask, vh3, alow, cqk)
        stage_c6(i, qkv, smq, pmat, alow, cqk)

    image_loop(rear3, PLAN["rear3"])
    stage_c7(0, n1, qkv, dwq)
    stage_c7(1, n1, qkv, dwk)
    tick(*PLAN["query"])

    def rear4(i):
        write_mask(edges[i], mask)
        stage_c8(i, x, g1, wqkv, resid, sm_c, mask, qkv)

    image_loop(rear4, PLAN["rear4"])
    out_copies.append(pltpu.make_async_copy(x, gin, out_sems.at[1]))
    out_copies[1].start()
    for k in range(15):
        put_small(small, 19 + k, total(sm_c[k]))
    for p in range(3):
        put_small(small, 34 + p, total(smq[:, p * D : (p + 1) * D]))
    put_small(small, 37, srow[...])

    weights = [(grads.at[p * D : (p + 1) * D, :], dwqkv_out.at[:, p * D : (p + 1) * D]) for p in range(3)]
    weights.append((dwm, dwm_out))
    weights += [(act.at[j, 0:D, :], dw1_out.at[:, j * D : (j + 1) * D]) for j in range(4)]
    weights += [(second[part], dw2_out.at[part * FP : (part + 1) * FP, :]) for part in range(FF // FP)]
    weights = [pltpu.make_async_copy(a, b, out_sems.at[2 + k]) for k, (a, b) in enumerate(weights)]
    out_copies += weights
    later_weights = weights[:4]

    def complete(which):
        return all(streams[k].done > streams[k].last for k in which)

    push_all(place, lambda device: small.at[rows(device * 8, 8), :], gathered.at[0, me], push_sems.at[2])
    gathered[0, me] = small[rows(me * 8, 8), :]
    tick(*PLAN["small"])
    fed = False
    rounds = 0
    while not complete(range(len(streams))):
        if not fed and complete(PART0 + PART1 + PART2):
            fed = True
            for u in range(FF // L):
                block, col = divmod(u * L, D)
                part, row = divmod(u * L, FP)
                act[block, 0:D, col : col + L] = first[part][row : row + L, :].T
            for copy in weights[4:]:
                copy.start()
        tick(*PLAN["end"])
        rounds += 1
        if rounds == 3:
            land_all(gathered.at[0, pl.ds(0, n - 1)], push_sems.at[2])
            gathered[1, me] = jnp.sum(gathered[0], axis=0)
            push_all(place, lambda device: gathered.at[1, me], gathered.at[1, me], push_sems.at[3])
    for copy in later_weights:
        copy.start()
    land_all(gathered.at[1, pl.ds(0, n - 1)], push_sems.at[3])
    for k in range(16):
        small[8 * k : 8 * k + 8, :] = gathered[1, k]

    def branch_factor(weight, grad, bias, bias_grad, factor):
        return (total(weight.astype(F32) * grad) + bias * bias_grad) / factor

    picked = [get_small(small, k) for k in range(38)]
    picked.append(branch_factor(wm[...], dwm[...], bm[...], picked[19 + 4], fm[...]))
    local = sum(st2[a, b : b + 1, :] * picked[4 + 3 * a + b] for a in range(3) for b in range(3))
    picked.append((local + cb2[...] * picked[3]) / fl[...])
    mlp = sum(total(w2[part * FP : (part + 1) * FP, :].astype(F32) * second[part][...]) for part in range(FF // FP))
    picked.append((mlp + bb2[...] * picked[2]) / fp[...])
    lane = lax.broadcasted_iota(jnp.int32, (1, D), 1)
    by_head = zeros(1, D)
    for h in range(HEADS):
        own = jnp.where((lane >= h * HD) & (lane < (h + 1) * HD), picked[37], 0.0)
        by_head = jnp.where(lane == h, jnp.sum(own, axis=1, keepdims=True) / sharp[h], by_head)
    picked.append(by_head)
    for k, row in enumerate(picked):
        small_out[k : k + 1, :] = row
    for copy in out_copies:
        copy.wait()


SINGLES = (0, 1, 2, 3, 13, 14, 19, 20, 21, 22, 23, 33, 38, 39, 40)


def deliver_kernel(*refs):
    small, outs, stage, sems = refs[6], refs[7:-7], refs[-7:-1], refs[-1]
    parts = []
    for k in range(6):
        parts.append((k, pl.ds(0, refs[k].shape[0])))
    loads = [pltpu.make_async_copy(refs[k].at[at], stage[k].at[at], sems.at[0, q]) for q, (k, at) in enumerate(parts)]
    for load in loads:
        load.start()
    sharp_grad, conv1, conv2, qkv_bias, hidden_bias = outs[6:11]
    sharp_grad[...] = small[41:42, :].reshape(D)[0:HEADS]
    for a in range(3):
        for b in range(3):
            conv2[a, b : b + 1, :] = small[4 + 3 * a + b : 5 + 3 * a + b, :]
            conv1[a, b : b + 1, :] = small[24 + 3 * a + b : 25 + 3 * a + b, :]
    pairs = [(small.at[34 + p], qkv_bias.at[pl.ds(p * D, D)]) for p in range(3)]
    pairs += [(small.at[15 + j], hidden_bias.at[pl.ds(j * D, D)]) for j in range(FF // D)]
    pairs += [(small.at[k], out) for k, out in zip(SINGLES, outs[11:])]
    copies = [pltpu.make_async_copy(a, b, sems.at[1, len(parts) + k]) for k, (a, b) in enumerate(pairs)]
    for copy in copies:
        copy.start()
    for q, (k, at) in enumerate(parts):
        loads[q].wait()
        copies.append(pltpu.make_async_copy(stage[k].at[at], outs[k].at[at], sems.at[1, q]))
        copies[-1].start()
    for copy in copies:
        copy.wait()


def on_device(n, x, sens, edges, g1, b1, wqkv, bqkv, sharp, wm, bm, fm, g2, b2, st1, cb1, bg, bo, st2, cb2, fl, g3, b3,
              w1, bb1, w2, bb2, fp):
    images = x.shape[0]
    S = jax.ShapeDtypeStruct
    V = pltpu.VMEM
    vm = pl.BlockSpec(memory_space=pltpu.VMEM)
    sm = pl.BlockSpec(memory_space=pltpu.SMEM)
    hbm = pl.BlockSpec(memory_space=pl.ANY)
    full = (images, T, D)
    dma = pltpu.SemaphoreType.DMA
    copies = stream_shape(n, stream_steps(n, True), FF)[1]
    lout, gin, dwqkv, dwm, dw1, dw2, small, *_ = pl.pallas_call(
        lambda *refs: mega_kernel(n, images, refs),
        in_specs=[sm, sm] + [hbm] * 25,
        out_specs=[hbm] * 6 + [vm] + [hbm] * 3,
        out_shape=[S(full, BF16), S(full, BF16), S((D, 3 * D), F32), S((D, D), F32), S((D, FF), F32), S((FF, D), F32),
                   S((48, D), F32), S(full, BF16), S(full, BF16), S(full, F32)],
        scratch_shapes=[
            V((24, FF), F32), V(full, BF16), V(full, BF16), V((D, 3 * D), BF16), V((D, D), BF16),
            V((D, FF), BF16), V((FF, D), BF16), V((3, 3, D), F32), V((3, 3, D), F32),
            V(full, BF16), V((images, T, 3 * D), BF16), V(full, BF16),
            V((images, D, D), F32), V((images, 2, 8, D), F32),
            V((images, T, L), F32), V(full, F32), V(full, F32), V(full, F32), V(full, F32),
            V(full, BF16), V((images, 8, D), F32), V((8, D), F32), V((8, D), F32), V((8, D), F32),
            V((T, L), F32), V((D, D), F32), V((D, D), BF16), V((D, D), BF16), V((3, PLANE, L), F32), V((3, PLANE, L), F32),
            V((images, T, FP), BF16), V((images, T, FP), BF16),
            V((15, 8, D), F32), V((8, FF), F32), V((15, 8, D), F32), V((8, 3 * D), F32), V((1, D), F32),
            V((4 * D + 2 * FF, D), F32), V((sum(stream_rows(n)), D), F32),
            V((8 * n, L), F32), V((2, 8, L), F32), V((2, n, 8, L), F32),
            dma((images + 24,)), dma((13,)), dma((3,)), dma((len(STREAMS), 4, copies)),
            pltpu.SemaphoreType.REGULAR((len(STREAMS), 4)), dma((4, 2)),
        ],
        compiler_params=pltpu.CompilerParams(
            collective_id=0, has_side_effects=True, vmem_limit_bytes=64 * 1024 * 1024
        ),
    )(edges, sharp, x, sens, wqkv, wm, w1, w2, st1, st2, g1, b1, bqkv, bm, fm, g2, b2, cb1, bg, bo, cb2, fl, g3, b3, bb1, bb2, fp)

    vector = S((D,), F32)
    stencil_shape = S((3, 3, D), F32)
    (lout, gin, dwqkv, dwm, dw1, dw2, sharp_grad, conv1, conv2, qkv_bias, hidden_bias, *singles) = pl.pallas_call(
        deliver_kernel,
        in_specs=[hbm] * 6 + [vm],
        out_specs=[hbm] * 6 + [vm] * 3 + [hbm] * (2 + len(SINGLES)),
        out_shape=[S(v.shape, v.dtype) for v in (lout, gin, dwqkv, dwm, dw1, dw2)]
        + [S((HEADS,), F32), stencil_shape, stencil_shape, S((3 * D,), F32), S((FF,), F32)]
        + [vector] * len(SINGLES),
        scratch_shapes=[V(v.shape, v.dtype) for v in (lout, gin, dwqkv, dwm, dw1, dw2)] + [dma((2, 13 + len(SINGLES)))],
        compiler_params=pltpu.CompilerParams(vmem_limit_bytes=62 * 1024 * 1024),
    )(lout, gin, dwqkv, dwm, dw1, dw2, small)
    one = dict(zip(SINGLES, singles))
    return (lout, gin, one[19], one[20], dwqkv, qkv_bias, sharp_grad, dwm, one[23], one[38], one[21], one[22], conv1, one[33],
            one[13], one[14], conv2, one[3], one[39], one[0], one[1], dw1, hidden_bias, dw2, one[2], one[40])


def solution(mesh):
    n = mesh.shape["img"]
    split = P("img", None, None)
    return jax.shard_map(
        lambda *args: on_device(n, *args),
        mesh=mesh,
        in_specs=(split, split, P("img")) + (P(),) * 24,
        out_specs=(split, split) + (P(),) * 24,
        check_vma=False,
    )
```
